32 devices in a mesh: fsdp: 4 (over y, x), frame: 8 (over z, core).
Axes of the slice: x: 2, y: 2, z: 4, core: 2. Of those that a mesh axis runs over, the one named last changes fastest.
Arguments:
- queries: bfloat16 [8, 512, 1024], P('frame', 'fsdp'), may hold values from -5 to 5
- key_rows: bfloat16 [8, 512, 1024], P('frame', 'fsdp'), may hold values from -5 to 5
- value_rows: bfloat16 [8, 512, 1024], P('frame', 'fsdp'), may hold values from -6 to 6
- out_weight: bfloat16 [1024, 2048], P(('fsdp', 'frame')), may hold values from -0.75 to 0.75
- conv_weight: bfloat16 [31, 2048], replicated, may hold values from -1 to 1
- grad_out: bfloat16 [8, 512, 2048], P('frame', 'fsdp'), may hold values from -6 to 6
Outputs:
- block_out: bfloat16 [8, 512, 2048], P('frame', 'fsdp')
- grad_queries: bfloat16 [8, 512, 1024], P('frame', 'fsdp')
- grad_keys: bfloat16 [8, 512, 1024], P('frame', 'fsdp')
- grad_values: bfloat16 [8, 512, 1024], P('frame', 'fsdp')
- weight_grad: float32 [1024, 2048], P(('fsdp', 'frame'))
- conv_grad: float32 [31, 2048], replicated
The draws below stay inside these ranges and needn't reach their ends.
All inputs are finite; a program needn't handle non-finite values.
Results may differ from the reference program's by a relative error of at most 0.014.
Values may be sent and summed in bfloat16 or wider, within the bound.
No kernel may reach another device: no remote copies, remote signals or barrier semaphores. Data moves between devices by JAX's collectives and lax.ppermute only.
A program may use at most 128 MiB of HBM per device.

```python
import math
import jax
import jax.numpy as jnp
from jax import lax

D = 2048
HEADS = 8
HDIM = 128
KERNEL = 31
INNER = 1024
SPAN = 512
SPANS = 8


def base_field(key):
    field = jnp.clip(1.5 * jax.random.normal(key, (SPANS, SPAN, INNER), jnp.float32), -5.0, 5.0)
    return field


def draw_queries(key, part):
    field = base_field(jax.random.fold_in(key, 1))
    return field.astype(jnp.bfloat16)


def draw_key_rows(key, part):
    field = base_field(jax.random.fold_in(key, 2))
    return field.astype(jnp.bfloat16)


def shard_levels(key, shape, cuts, smallest, top_value):
    def one(axis_at, parts):
        heights = jax.random.uniform(jax.random.fold_in(jax.random.fold_in(key, 6), axis_at), (parts,), jnp.float32, smallest / len(cuts), top_value / len(cuts))
        return jnp.repeat(jnp.exp(heights), shape[axis_at] // parts).reshape((-1,) + (1,) * (len(shape) - axis_at - 1))

    level = one(*cuts[0])
    for cut in cuts[1:]:
        level = level * one(*cut)
    return level


def scatter_about(stream_key, dims, deviation, bound, shards=(), kind=jnp.bfloat16):
    gain = shard_levels(stream_key, dims, shards, -0.22, 0.18) if shards else 1.0
    drawn = jax.random.normal(stream_key, dims, jnp.float32) * deviation * gain
    return jnp.minimum(jnp.maximum(drawn, -bound), bound).astype(kind)


def setup_inputs(seed: int = 0) -> dict:
    streams_of = jax.random.split(jax.random.key(seed), 7)
    return {
        "queries": draw_queries(jax.random.fold_in(streams_of[6], 71), 0),
        "key_rows": draw_key_rows(jax.random.fold_in(streams_of[6], 71), 0),
        "value_rows": scatter_about(streams_of[2], (SPANS, SPAN, INNER), 1.0, 6.0, ((0, 8), (1, 4))),
        "out_weight": scatter_about(streams_of[3], (INNER, D), (INNER // 16) ** -0.5, 0.75, ((0, 32),)),
        "conv_weight": scatter_about(streams_of[4], (KERNEL, D), KERNEL ** -0.5, 1.0),
        "grad_out": scatter_about(streams_of[5], (SPANS, SPAN, D), 1.0, 6.0, ((0, 8), (1, 4))),
    }


def reference(queries, key_rows, value_rows, out_weight, conv_weight, grad_out):
    inv_root = 1.0 / math.sqrt(HDIM)
    half_width = KERNEL // 2
    conv_taps = conv_weight.astype(jnp.float32)

    def one_span(running, inputs):
        span_q, span_k, span_v, span_g = inputs
        pieces = []
        kept_weights = []
        for head_index in range(HEADS):
            columns = slice(head_index * HDIM, (head_index + 1) * HDIM)
            scores = jnp.dot(span_q[:, columns], span_k[:, columns].T, preferred_element_type=jnp.float32) * inv_root
            row_max = lax.optimization_barrier(jnp.max(scores, axis=1))
            exponent = jnp.exp(scores - row_max[:, None])
            row_sum = lax.optimization_barrier(jnp.sum(exponent, axis=1))
            weights = exponent / row_sum[:, None]
            rounded = weights.astype(jnp.bfloat16)
            pieces.append(jnp.dot(rounded, span_v[:, columns], preferred_element_type=jnp.float32).astype(jnp.bfloat16))
            kept_weights.append(weights)
        attention = jnp.concatenate(pieces, axis=1)
        projected = jnp.dot(attention, out_weight, preferred_element_type=jnp.float32).astype(jnp.bfloat16)
        padded = jnp.pad(projected.astype(jnp.float32), ((half_width, half_width), (0, 0)))
        conv_value = jnp.zeros((SPAN, D), jnp.float32)
        for offset in range(KERNEL):
            conv_value = conv_value + conv_taps[offset] * padded[offset:offset + SPAN]
        sigmoid_conv = jax.nn.sigmoid(conv_value)
        block_out = (padded[half_width:half_width + SPAN] + conv_value * sigmoid_conv).astype(jnp.bfloat16)
        upstream = span_g.astype(jnp.float32)
        grad_conv = (upstream * sigmoid_conv * (1.0 + conv_value * (1.0 - sigmoid_conv))).astype(jnp.bfloat16)
        grad_padded = jnp.pad(grad_conv.astype(jnp.float32), ((half_width, half_width), (0, 0)))
        grad_sum = upstream
        for offset in range(KERNEL):
            start_row = 2 * half_width - offset
            grad_sum = grad_sum + conv_taps[offset] * grad_padded[start_row:start_row + SPAN]
        grad_projected = grad_sum.astype(jnp.bfloat16)
        conv_terms = jnp.stack([lax.optimization_barrier(jnp.sum(grad_conv.astype(jnp.float32) * padded[offset:offset + SPAN], axis=0)) for offset in range(KERNEL)])
        weight_terms = jnp.dot(attention.T, grad_projected, preferred_element_type=jnp.float32)
        grad_attention = jnp.dot(grad_projected, out_weight.T, preferred_element_type=jnp.float32).astype(jnp.bfloat16)
        query_list = []
        key_list = []
        value_list = []
        for head_index in range(HEADS):
            columns = slice(head_index * HDIM, (head_index + 1) * HDIM)
            weights = kept_weights[head_index]
            grad_head = grad_attention[:, columns]
            grad_probs = jnp.dot(grad_head, span_v[:, columns].T, preferred_element_type=jnp.float32)
            row_dot = lax.optimization_barrier(jnp.sum(weights * grad_probs, axis=1))
            grad_scores = (weights * (grad_probs - row_dot[:, None])).astype(jnp.bfloat16)
            query_list.append((jnp.dot(grad_scores, span_k[:, columns], preferred_element_type=jnp.float32) * inv_root).astype(jnp.bfloat16))
            key_list.append((jnp.dot(grad_scores.T, span_q[:, columns], preferred_element_type=jnp.float32) * inv_root).astype(jnp.bfloat16))
            value_list.append(jnp.dot(weights.astype(jnp.bfloat16).T, grad_head, preferred_element_type=jnp.float32).astype(jnp.bfloat16))
        outputs = (block_out, jnp.concatenate(query_list, axis=1), jnp.concatenate(key_list, axis=1), jnp.concatenate(value_list, axis=1))
        return ((running[0] + weight_terms, running[1] + conv_terms), outputs)
    start_sums = (jnp.zeros((INNER, D), jnp.float32), jnp.zeros((KERNEL, D), jnp.float32))
    sums_done, stacked = lax.scan(one_span, start_sums, (queries, key_rows, value_rows, grad_out))
    grad_scale = 1.0 / math.sqrt(SPAN * SPANS)
    return (stacked[0], stacked[1], stacked[2], stacked[3], sums_done[0] * grad_scale, sums_done[1] * grad_scale)
```

```python
import functools
import math

import jax
import jax.numpy as jnp
from jax import lax
from jax.experimental import pallas as pl
from jax.experimental.pallas import tpu as pltpu
from jax.sharding import PartitionSpec as P

HDIM = 128
KERNEL = 31
HALF = KERNEL // 2
LANES = 128
TILE = 64
TAPS = 32
F32 = jnp.float32
BF16 = jnp.bfloat16
ROOT = 1.0 / math.sqrt(HDIM)


def swap(cells, axis, mask):
    count = lax.axis_size(axis)
    return lax.ppermute(cells, axis, [(i, i ^ mask) for i in range(count)])


def call(body, outs, *operands, scratch=(), flops=0, loose=0):
    vmem = pl.BlockSpec(memory_space=pltpu.VMEM)
    in_specs = [vmem] * (len(operands) - loose) + [pl.BlockSpec(memory_space=pl.ANY)] * loose
    moved = sum(x.size * x.dtype.itemsize for x in operands[: len(operands) - loose])
    moved += sum(math.prod(s) * jnp.dtype(t).itemsize for s, t in outs)
    return pl.pallas_call(
        body,
        out_shape=[jax.ShapeDtypeStruct(s, t) for s, t in outs],
        in_specs=in_specs,
        out_specs=[vmem] * len(outs),
        scratch_shapes=list(scratch),
        cost_estimate=pl.CostEstimate(flops=flops, bytes_accessed=moved, transcendentals=0),
        compiler_params=pltpu.CompilerParams(vmem_limit_bytes=40 * 1024 * 1024),
    )(*operands)


def block(index, size, unit):
    return pl.ds(pl.multiple_of(index * size, unit), size)


def product(left, right, left_dim, right_dim):
    return lax.dot_general(
        left, right, (((left_dim,), (right_dim,)), ((), ())), preferred_element_type=F32
    )


def tree_sum(terms):
    while len(terms) > 1:
        terms = [terms[i] + terms[i + 1] for i in range(0, len(terms), 2)]
    return terms[0]


def pack_rows(groups, *refs):
    queries, keys, values = refs[:3]
    outs = refs[3:]
    me = lax.axis_index("fsdp")
    width = queries.shape[1] // groups
    for k in range(groups):
        columns = block(me ^ k, width, LANES)
        for at, source in enumerate((queries, keys, values)):
            outs[k][:, at * width : (at + 1) * width] = source[:, columns]


def pack_columns(groups, *refs):
    source = refs[0]
    outs = refs[-groups:]
    me = lax.axis_index("fsdp")
    width = source.shape[1] // groups
    for k in range(groups):
        outs[k][...] = source[:, block(me ^ k, width, LANES)]


def attend(groups, *refs):
    pieces = refs[:groups]
    rows_ref, out = refs[groups:]
    me = lax.axis_index("fsdp")
    local = pieces[0].shape[0]
    width = out.shape[1]
    for k in range(groups):
        rows_ref[block(me ^ k, local, local), :] = pieces[k][...]
    for head in range(width // HDIM):
        at = head * HDIM
        queries = rows_ref[:, at : at + HDIM]
        keys = rows_ref[:, width + at : width + at + HDIM]
        values = rows_ref[:, 2 * width + at : 2 * width + at + HDIM]
        scores = product(queries, keys, 1, 1) * ROOT
        exponent = jnp.exp(scores - jnp.max(scores, axis=1, keepdims=True))
        probs = exponent * (1.0 / jnp.sum(exponent, axis=1, keepdims=True))
        out[:, at : at + HDIM] = product(probs.astype(BF16), values, 1, 0).astype(BF16)


def join_weight(groups, count, *refs):
    pieces = refs[:count]
    out = refs[count]
    me = lax.axis_index("frame")
    rows = pieces[0].shape[0] // groups
    width = rows * count
    for n in range(count):
        for k in range(groups):
            start = pl.multiple_of(k * width + (me ^ n) * rows, rows)
            out[pl.ds(start, rows), :] = pieces[n][k * rows : (k + 1) * rows, :]


def shifted(padded, start, tile):
    for residue in range(8):
        taps = range(residue, KERNEL, 8)
        reach = 8 * (len(taps) - 1)
        rows = padded[start + 1 + residue : start + 1 + residue + tile + reach, :]
        yield taps, rows


def convolve(groups, *refs):
    attention = refs[:groups]
    weight, taps_ref = refs[groups : groups + 2]
    projected_ref, slope_ref = refs[groups + 2 : groups + 4]
    outs = refs[groups + 4 : 2 * groups + 4]
    padded, taps, result = refs[2 * groups + 4 :]
    me = lax.axis_index("fsdp")
    frames, depth = attention[0].shape
    channels = weight.shape[1]
    local = frames // groups
    padded[0:16, :] = jnp.zeros((16, LANES), F32)
    padded[frames + 16 : frames + 32, :] = jnp.zeros((16, LANES), F32)

    def lane_block(c, carry):
        columns = block(c, LANES, LANES)
        total = product(attention[0][...], weight[0:depth, columns], 1, 0)
        for k in range(1, groups):
            total += product(attention[k][...], weight[k * depth : (k + 1) * depth, columns], 1, 0)
        rounded = total.astype(BF16)
        projected_ref[:, columns] = rounded
        padded[16 : frames + 16, :] = rounded.astype(F32)
        taps[0:KERNEL, :] = taps_ref[:, block(me * (channels // LANES) + c, LANES, LANES)].astype(F32)
        for start in range(0, frames, TILE):
            conv = jnp.zeros((TILE, LANES), F32)
            for indices, rows in shifted(padded, start, TILE):
                for at, j in enumerate(indices):
                    conv += taps[j : j + 1, :] * rows[8 * at : 8 * at + TILE, :]
            gate = 1.0 / (1.0 + jnp.exp(-conv))
            own = padded[start + 16 : start + 16 + TILE, :]
            result[start : start + TILE, :] = own + conv * gate
            slope_ref[start : start + TILE, columns] = gate * (1.0 + conv * (1.0 - gate))
        for k in range(groups):
            outs[k][:, columns] = result[block(me ^ k, local, local), :].astype(BF16)
        return carry

    lax.fori_loop(0, channels // LANES, lane_block, 0)


def convolve_back(groups, *refs):
    upstream = refs[:groups]
    projected_ref, slope_ref, weight, taps_ref = refs[groups : groups + 4]
    grad_ref, tap_ref = refs[groups + 4 : groups + 6]
    outs = refs[groups + 6 : 2 * groups + 6]
    padded, taps, above, sums = refs[2 * groups + 6 :]
    me = lax.axis_index("fsdp")
    frames, channels = projected_ref.shape
    local = frames // groups
    depth = weight.shape[0] // groups
    padded[0:16, :] = jnp.zeros((16, LANES), F32)
    padded[frames + 16 : frames + 32, :] = jnp.zeros((16, LANES), F32)

    def lane_block(c, carry):
        columns = block(c, LANES, LANES)
        for k in range(groups):
            above[block(me ^ k, local, local), :] = upstream[k][:, columns].astype(F32)
        taps[0:KERNEL, :] = taps_ref[:, block(me * (channels // LANES) + c, LANES, LANES)].astype(F32)
        padded[16 : frames + 16, :] = (above[...] * slope_ref[:, columns]).astype(BF16).astype(F32)
        sums[...] = jnp.zeros(sums.shape, F32)
        for start in range(0, frames, TILE):
            total = above[start : start + TILE, :]
            own = projected_ref[start : start + TILE, columns].astype(F32)
            for indices, rows in shifted(padded, start, TILE):
                for at, j in enumerate(indices):
                    part = rows[8 * at : 8 * at + TILE, :]
                    tap = KERNEL - 1 - j
                    total += taps[tap : tap + 1, :] * part
                    terms = own * part
                    sums[8 * tap : 8 * tap + 8, :] += tree_sum(
                        [terms[8 * i : 8 * i + 8, :] for i in range(TILE // 8)]
                    )
            grad_ref[start : start + TILE, columns] = total.astype(BF16)
        tap_ref[:, columns] = jnp.sum(sums[...].reshape(TAPS, 8, LANES), axis=1)
        return carry

    lax.fori_loop(0, channels // LANES, lane_block, 0)
    grads = grad_ref[...]
    for k in range(groups):
        outs[k][...] = product(grads, weight[k * depth : (k + 1) * depth, :], 1, 1).astype(BF16)


def weight_terms(groups, count, rows, *refs):
    attention = refs[:groups]
    grads, tap_ref = refs[groups : groups + 2]
    outs = refs[groups + 2 : groups + 4]
    terms = refs[groups + 4]
    me = lax.axis_index("frame")
    gathered = groups * rows
    half = count // 2
    for k in range(groups):
        terms[...] = product(attention[k][...], grads[...], 0, 0)
        for m in range(half):
            for core in range(2):
                there = pl.ds(pl.multiple_of((me ^ (2 * m + core)) * rows, rows), rows)
                at = m * gathered + k * rows
                outs[core][at : at + rows, :] = terms[there, :].astype(BF16)
    for core in range(2):
        outs[core][half * gathered :, :] = tap_ref[...].astype(BF16)


def plain_terms(groups, *refs):
    attention = refs[:groups]
    grads, out = refs[groups:]
    depth = attention[0].shape[1]
    for k in range(groups):
        out[k * depth : (k + 1) * depth, :] = product(attention[k][...], grads[...], 0, 0).astype(BF16)


def add_core(gathered, *refs):
    mine, other = refs[:2]
    outs = refs[2:]
    taps = len(outs) * gathered
    shared = (mine[taps:, :].astype(F32) + other[taps:, :].astype(F32)).astype(BF16)
    for m, out in enumerate(outs):
        rows = slice(m * gathered, (m + 1) * gathered)
        out[0:gathered, :] = (mine[rows, :].astype(F32) + other[rows, :].astype(F32)).astype(BF16)
        out[gathered:, :] = shared


def add_spans(pieces, rows, *refs):
    outs = refs[pieces:]
    total = tree_sum([ref[...].astype(F32) for ref in refs[:pieces]])
    gathered = len(outs) * rows
    for k, out in enumerate(outs):
        out[0:TAPS, :] = total[gathered:, :].astype(BF16)
        out[TAPS:, :] = total[k * rows : (k + 1) * rows, :].astype(BF16)


def join_sums(groups, scale, *refs):
    pieces = refs[:groups]
    weight_ref, tap_ref = refs[groups:]
    me = lax.axis_index("fsdp")
    width = pieces[0].shape[1]
    for k in range(groups):
        columns = block(me ^ k, width, LANES)
        tap_ref[:, columns] = pieces[k][0:KERNEL, :].astype(F32) * scale
        weight_ref[:, columns] = pieces[k][TAPS:, :].astype(F32) * scale


def attend_back(groups, *refs):
    rows_ref = refs[0]
    upstream = refs[1 : groups + 1]
    outs = refs[groups + 1 : 2 * groups + 1]
    grads, result = refs[2 * groups + 1 :]
    me = lax.axis_index("fsdp")
    width = upstream[0].shape[1]
    local = outs[0].shape[0]
    grads[...] = tree_sum([ref[...].astype(F32) for ref in upstream]).astype(BF16)
    for head in range(width // HDIM):
        at = head * HDIM
        queries = rows_ref[:, at : at + HDIM]
        keys = rows_ref[:, width + at : width + at + HDIM]
        values = rows_ref[:, 2 * width + at : 2 * width + at + HDIM]
        above = grads[:, at : at + HDIM]
        scores = product(queries, keys, 1, 1) * ROOT
        exponent = jnp.exp(scores - jnp.max(scores, axis=1, keepdims=True))
        weights = exponent * (1.0 / jnp.sum(exponent, axis=1, keepdims=True))
        slopes = product(above, values, 1, 1)
        row_dot = jnp.sum(weights * slopes, axis=1, keepdims=True)
        grad_scores = (weights * (slopes - row_dot)).astype(BF16)
        result[:, at : at + HDIM] = (product(grad_scores, keys, 1, 0) * ROOT).astype(BF16)
        result[:, width + at : width + at + HDIM] = (
            product(grad_scores, queries, 0, 0) * ROOT
        ).astype(BF16)
        result[:, 2 * width + at : 2 * width + at + HDIM] = product(
            weights.astype(BF16), above, 0, 0
        ).astype(BF16)
    for k in range(groups):
        outs[k][...] = result[block(me ^ k, local, local), :]


def join_rows(groups, *refs):
    pieces = refs[:groups]
    outs = refs[groups:]
    me = lax.axis_index("fsdp")
    width = pieces[0].shape[1] // len(outs)
    for k in range(groups):
        columns = block(me ^ k, width, LANES)
        for at, out in enumerate(outs):
            out[0, :, columns] = pieces[k][:, at * width : (at + 1) * width]


def gather_weight(out_weight, groups, count):
    rows, model = out_weight.shape
    channels = model // groups
    direct = rows % 16 == 0
    if direct:
        sent = call(functools.partial(pack_columns, groups), [((rows, channels), BF16)] * groups, out_weight)
    else:
        me = lax.axis_index("fsdp")
        sent = [
            lax.dynamic_slice_in_dim(out_weight, (me ^ k) * channels, channels, axis=1)
            for k in range(groups)
        ]
    mine = jnp.concatenate(
        [sent[0]] + [swap(sent[k], "fsdp", k) for k in range(1, groups)], axis=0
    )
    across = [mine] + [swap(mine, "frame", 2 * m) for m in range(1, count // 2)]
    pieces = []
    for piece in across:
        pieces += [piece, swap(piece, "frame", 1)]
    if direct:
        return call(
            functools.partial(join_weight, groups, count),
            [((groups * count * rows, channels), BF16)],
            *pieces,
        )[0]
    me = lax.axis_index("frame")
    ordered = jnp.take(jnp.stack(pieces), me ^ jnp.arange(count), axis=0)
    ordered = ordered.reshape(count, groups, rows, channels).transpose(1, 0, 2, 3)
    return ordered.reshape(groups * count * rows, channels)


def reduce_sums(attention, grads, tap_terms, groups, count, rows, scale):
    channels = grads.shape[1]
    depth = attention[0].shape[1]
    half = count // 2
    gathered = groups * rows
    flops = 2 * grads.shape[0] * depth * groups * channels
    if rows % 16 == 0:
        mine, other = call(
            functools.partial(weight_terms, groups, count, rows),
            [((half * gathered + TAPS, channels), BF16)] * 2,
            *attention,
            grads,
            tap_terms,
            scratch=[pltpu.VMEM((depth, channels), F32)],
            flops=flops,
        )
    else:
        (terms,) = call(
            functools.partial(plain_terms, groups),
            [((groups * depth, channels), BF16)],
            *attention,
            grads,
            flops=flops,
        )
        me = lax.axis_index("frame")
        terms = jnp.take(
            terms.reshape(groups, count, rows, channels), me ^ jnp.arange(count), axis=1
        )
        terms = terms.reshape(groups, half, 2, rows, channels).transpose(2, 1, 0, 3, 4)
        terms = terms.reshape(2, half * gathered, channels)
        mine, other = [
            jnp.concatenate([terms[core], tap_terms.astype(BF16)], axis=0) for core in range(2)
        ]
    sent = call(
        functools.partial(add_core, gathered),
        [((gathered + TAPS, channels), BF16)] * half,
        mine,
        swap(other, "frame", 1),
    )
    pieces = [sent[0]] + [swap(sent[m], "frame", 2 * m) for m in range(1, half)]
    sent = call(
        functools.partial(add_spans, half, rows),
        [((TAPS + rows, channels), BF16)] * groups,
        *pieces,
    )
    pieces = [sent[0]] + [swap(sent[k], "fsdp", k) for k in range(1, groups)]
    return call(
        functools.partial(join_sums, groups, scale),
        [((rows, groups * channels), F32), ((KERNEL, groups * channels), F32)],
        *pieces,
    )


def shards(queries, key_rows, value_rows, out_weight, conv_weight, grad_out):
    local, inner = queries.shape[1:]
    model = grad_out.shape[2]
    groups = lax.axis_size("fsdp")
    count = lax.axis_size("frame")
    frames = local * groups
    width = inner // groups
    channels = model // groups
    scale = 1.0 / math.sqrt(frames * count)
    weight = gather_weight(out_weight, groups, count)

    sent = call(
        functools.partial(pack_rows, groups),
        [((local, 3 * width), BF16)] * groups,
        queries[0],
        key_rows[0],
        value_rows[0],
    )
    pieces = [sent[0]] + [swap(sent[k], "fsdp", k) for k in range(1, groups)]
    rows, own = call(
        functools.partial(attend, groups),
        [((frames, 3 * width), BF16), ((frames, width), BF16)],
        *pieces,
        flops=4 * frames * frames * width,
    )
    attention = [own] + [swap(own, "fsdp", k) for k in range(1, groups)]

    sent = call(
        functools.partial(pack_columns, groups),
        [((local, channels), BF16)] * groups,
        grad_out[0],
        attention[1],
        loose=1,
    )
    upstream = [sent[0]] + [swap(sent[k], "fsdp", k) for k in range(1, groups)]

    outs = call(
        functools.partial(convolve, groups),
        [((frames, channels), BF16), ((frames, channels), F32)] + [((local, channels), BF16)] * groups,
        *attention,
        weight,
        conv_weight,
        scratch=[
            pltpu.VMEM((frames + 32, LANES), F32),
            pltpu.VMEM((TAPS, LANES), F32),
            pltpu.VMEM((frames, LANES), F32),
        ],
        flops=2 * frames * inner * channels,
    )
    projected, slope = outs[:2]
    sent = outs[2:]
    pieces = [sent[0]] + [swap(sent[k], "fsdp", k) for k in range(1, groups)]
    (block_out,) = call(functools.partial(join_rows, groups), [((1, local, model), BF16)], *pieces)

    outs = call(
        functools.partial(convolve_back, groups),
        [((frames, channels), BF16), ((TAPS, channels), F32)] + [((frames, width), BF16)] * groups,
        *upstream,
        projected,
        slope,
        weight,
        conv_weight,
        scratch=[
            pltpu.VMEM((frames + 32, LANES), F32),
            pltpu.VMEM((TAPS, LANES), F32),
            pltpu.VMEM((frames, LANES), F32),
            pltpu.VMEM((8 * TAPS, LANES), F32),
        ],
        flops=2 * frames * inner * channels,
    )
    grads, tap_terms = outs[:2]
    sent = outs[2:]
    above = [sent[0]] + [swap(sent[k], "fsdp", k) for k in range(1, groups)]
    weight_grad, conv_grad = reduce_sums(
        attention, grads, tap_terms, groups, count, out_weight.shape[0], scale
    )
    sent = call(
        functools.partial(attend_back, groups),
        [((local, 3 * width), BF16)] * groups,
        rows,
        *above,
        scratch=[pltpu.VMEM((frames, width), BF16), pltpu.VMEM((frames, 3 * width), BF16)],
        flops=10 * frames * frames * width,
    )
    pieces = [sent[0]] + [swap(sent[k], "fsdp", k) for k in range(1, groups)]
    grad_queries, grad_keys, grad_values = call(
        functools.partial(join_rows, groups), [((1, local, inner), BF16)] * 3, *pieces
    )
    return (block_out, grad_queries, grad_keys, grad_values, weight_grad, conv_grad)


def solution(mesh):
    return jax.shard_map(
        shards,
        mesh=mesh,
        in_specs=(
            P("frame", "fsdp", None),
            P("frame", "fsdp", None),
            P("frame", "fsdp", None),
            P(("fsdp", "frame"), None),
            P(),
            P("frame", "fsdp", None),
        ),
        out_specs=(
            P("frame", "fsdp", None),
            P("frame", "fsdp", None),
            P("frame", "fsdp", None),
            P("frame", "fsdp", None),
            P(("fsdp", "frame"), None),
            P(),
        ),
        check_vma=False,
    )
```

```python
import functools
import math

import jax
import jax.numpy as jnp
from jax import lax
from jax.experimental import pallas as pl
from jax.experimental.pallas import tpu as pltpu
from jax.sharding import PartitionSpec as P

HDIM = 128
KERNEL = 31
LANES = 128
TILE = 64
TAPS = 32
CONV_COST = 600
ATTEND_COST = 24
BACK_COST = 48
PACK_LIMIT = 60
F32 = jnp.float32
BF16 = jnp.bfloat16
ROOT = 1.0 / math.sqrt(HDIM)


def swap(cells, axis, mask):
    count = lax.axis_size(axis)
    return lax.ppermute(cells, axis, [(i, i ^ mask) for i in range(count)])


def exchange(sent):
    return [sent[0]] + [swap(sent[k], "fsdp", k) for k in range(1, len(sent))]


def masks_of(count):
    return [1 << i for i in range(count.bit_length() - 1)]


def order_of(count):
    order = [0]
    for mask in reversed(masks_of(count)):
        order += [n ^ mask for n in order]
    return order


def call(body, outs, *operands, scratch=(), flops=0, near=True, stored=False, after=(), limit=40):
    vmem = pl.BlockSpec(memory_space=pltpu.VMEM)
    hbm = pl.BlockSpec(memory_space=pltpu.HBM)
    count = len(operands)
    moved = sum(x.size * x.dtype.itemsize for x in operands)
    moved += sum(math.prod(s) * jnp.dtype(t).itemsize for s, t in outs)
    return pl.pallas_call(
        lambda *refs: body(*refs[:count], *refs[count + len(after) :]),
        out_shape=[jax.ShapeDtypeStruct(s, t) for s, t in outs],
        in_specs=[vmem if near else hbm] * count + [pl.BlockSpec(memory_space=pl.ANY)] * len(after),
        out_specs=[hbm if stored else vmem] * len(outs),
        scratch_shapes=list(scratch),
        cost_estimate=pl.CostEstimate(flops=flops, bytes_accessed=moved, transcendentals=0),
        compiler_params=pltpu.CompilerParams(vmem_limit_bytes=limit * 1024 * 1024),
    )(*operands, *after)


def block(index, size, unit):
    return pl.ds(pl.multiple_of(index * size, unit), size)


def product(left, right, left_dim, right_dim):
    return lax.dot_general(
        left, right, (((left_dim,), (right_dim,)), ((), ())), preferred_element_type=F32
    )


def tree_sum(terms):
    while len(terms) > 1:
        terms = [terms[i] + terms[i + 1] for i in range(0, len(terms), 2)]
    return terms[0]


def places(top, end, rows):
    return (
        (0, 0, top[0], 0),
        (1, 0, top[1], 0),
        (2, 0, top[2], 0),
        (3, 0, top[2], rows),
        (0, 1, end[0], 0),
        (2, 1, end[1], 0),
        (1, 1, end[2], 0),
        (3, 1, end[2], rows),
    )


def split_up(outs, k, rows, columns, cells):
    own, beside, across, later_across, later_beside = outs
    half = rows // 2
    top, end = cells[:half, :], cells[half:, :]
    if k == 0:
        own[:, columns] = cells
    elif k == 1:
        beside[:half, columns] = top
        later_beside[:, columns] = end
    elif k == 2:
        later_across[:, columns] = top
        across[:half, columns] = end
    else:
        beside[half:, columns] = top
        across[half:, columns] = end


def pack_rows(groups, *refs):
    sources = refs[:5]
    outs = refs[5 : -groups - 6]
    weight_outs = refs[-groups - 6 : -6]
    held = refs[-6:-1]
    arrived = refs[-1]
    copies = [pltpu.make_async_copy(sources[i], held[i], arrived.at[i]) for i in range(5)]
    for copy in copies:
        copy.start()
    for copy in copies:
        copy.wait()
    me = lax.axis_index("fsdp")
    for k in range(groups):
        at = 0
        for source in held[:4]:
            width = source.shape[1] // groups
            there = slice(at, at + width)
            cells = source[:, block(me ^ k, width, LANES)]
            if groups == 4:
                split_up(outs, k, cells.shape[0], there, cells)
            else:
                outs[k][:, there] = cells
            at += width
        weight_outs[k][...] = held[4][:, block(me ^ k, held[4].shape[1] // groups, LANES)]


def stack_parts(mine, other, out):
    rows = mine.shape[0]
    out[:rows, :] = mine[...]
    out[rows:, :] = other[rows:, :]


def stack_all(*refs):
    at = 0
    for source in refs[:-1]:
        refs[-1][at : at + source.shape[0], :] = source[...]
        at += source.shape[0]


def attend(groups, *refs):
    folded = groups == 4
    pieces = refs[: 5 if folded else groups]
    rows_ref = refs[len(pieces)]
    upstream_ref = refs[len(pieces) + 1]
    outs = refs[len(pieces) + 2 :]
    edge = rows_ref.shape[1]
    me = lax.axis_index("fsdp")
    local = pieces[0].shape[0]
    half, width = outs[0].shape
    if folded:
        share = local // 2
        own, beside, later_across, across, later_beside = pieces
        ends = ((own, beside, later_across), (own, across, later_beside))
        for k, i, source, at in places(*ends, share):
            if k == 0:
                at = i * share
            start = pl.multiple_of((me ^ k) * local + i * share, share)
            rows_ref[pl.ds(start, share), :] = source[at : at + share, :edge]
            upstream_ref[pl.ds(start, share), :] = source[at : at + share, edge:]
    else:
        for k in range(groups):
            rows_ref[block(me ^ k, local, local), :] = pieces[k][:, :edge]
            upstream_ref[block(me ^ k, local, local), :] = pieces[k][:, edge:]
    for head in range(width // HDIM):
        at = head * HDIM
        queries = rows_ref[:, at : at + HDIM]
        keys = rows_ref[:, width + at : width + at + HDIM]
        values = rows_ref[:, 2 * width + at : 2 * width + at + HDIM]
        scores = product(queries, keys, 1, 1) * ROOT
        exponent = jnp.exp(scores - jnp.max(scores, axis=1, keepdims=True))
        probs = exponent * (1.0 / jnp.sum(exponent, axis=1, keepdims=True))
        mixed = product(probs.astype(BF16), values, 1, 0).astype(BF16)
        for i, out in enumerate(outs):
            out[:, at : at + HDIM] = mixed[i * half : (i + 1) * half, :]


def join_weight(groups, count, mine, other, out):
    me = lax.axis_index("frame")
    rows = mine.shape[0] // (count // 2 * groups)
    width = rows * count
    for i, n in enumerate(order_of(count)[: count // 2]):
        for k in range(groups):
            at = (i * groups + k) * rows
            for core, source in enumerate((mine, other)):
                start = pl.multiple_of(k * width + (me ^ n ^ core) * rows, rows)
                out[pl.ds(start, rows), :] = source[at : at + rows, :]


def shifted(padded, start, tile):
    for residue in range(8):
        taps = range(residue, KERNEL, 8)
        reach = 8 * (len(taps) - 1)
        rows = padded[start + 1 + residue : start + 1 + residue + tile + reach, :]
        yield taps, rows


def convolve(groups, *refs):
    pieces = refs[: -groups - 8]
    weight, taps_ref, attention, projected_ref, slope_ref = refs[-groups - 8 : -groups - 3]
    ahead = refs[-groups - 3 : -3]
    padded, taps, result = refs[-3:]
    me = lax.axis_index("fsdp")
    frames = attention.shape[0]
    channels = weight.shape[1]
    local = frames // groups
    padded[0:16, :] = jnp.zeros((16, LANES), F32)
    padded[frames + 16 : frames + 32, :] = jnp.zeros((16, LANES), F32)
    if groups == 4:
        half, depth = pieces[0].shape
        for k, i, source, at in places(pieces[:3], pieces[3:], half):
            start = i * half
            attention[start : start + half, k * depth : (k + 1) * depth] = source[at : at + half, :]
    else:
        depth = pieces[0].shape[1]
        for k in range(groups):
            attention[:, k * depth : (k + 1) * depth] = pieces[k][...]
    projected_ref[...] = product(attention[...], weight[...], 1, 0).astype(BF16)

    def lane_block(c, carry):
        columns = block(c, LANES, LANES)
        padded[16 : frames + 16, :] = projected_ref[:, columns].astype(F32)
        taps[0:KERNEL, :] = taps_ref[:, block(me * (channels // LANES) + c, LANES, LANES)].astype(F32)
        for start in range(0, frames, TILE):
            conv = jnp.zeros((TILE, LANES), F32)
            for indices, rows in shifted(padded, start, TILE):
                for at, j in enumerate(indices):
                    conv += taps[j : j + 1, :] * rows[8 * at : 8 * at + TILE, :]
            gate = 1.0 / (1.0 + jnp.exp(-conv))
            own = padded[start + 16 : start + 16 + TILE, :]
            result[start : start + TILE, :] = own + conv * gate
            slope_ref[start : start + TILE, columns] = gate * (1.0 + conv * (1.0 - gate))
        for k in range(groups):
            ahead[k][:, columns] = result[block(me ^ k, local, local), :].astype(BF16)
        return carry

    lax.fori_loop(0, channels // LANES, lane_block, 0)


def convolve_back(groups, *refs):
    upstream, projected_ref, slope_ref, weight, taps_ref, grad_ref, tap_ref = refs[:7]
    outs = refs[-groups - 4 : -4]
    padded, taps, above, sums = refs[-4:]
    me = lax.axis_index("fsdp")
    frames, channels = projected_ref.shape
    local = frames // groups
    depth = weight.shape[0] // groups
    padded[0:16, :] = jnp.zeros((16, LANES), F32)
    padded[frames + 16 : frames + 32, :] = jnp.zeros((16, LANES), F32)

    def lane_block(c, carry):
        columns = block(c, LANES, LANES)
        above[...] = upstream[:, columns].astype(F32)
        taps[0:KERNEL, :] = taps_ref[:, block(me * (channels // LANES) + c, LANES, LANES)].astype(F32)
        padded[16 : frames + 16, :] = (above[...] * slope_ref[:, columns]).astype(BF16).astype(F32)
        sums[...] = jnp.zeros(sums.shape, F32)
        for start in range(0, frames, TILE):
            total = above[start : start + TILE, :]
            own = projected_ref[start : start + TILE, columns].astype(F32)
            for indices, rows in shifted(padded, start, TILE):
                for at, j in enumerate(indices):
                    part = rows[8 * at : 8 * at + TILE, :]
                    tap = KERNEL - 1 - j
                    total += taps[tap : tap + 1, :] * part
                    terms = own * part
                    sums[8 * tap : 8 * tap + 8, :] += tree_sum(
                        [terms[8 * i : 8 * i + 8, :] for i in range(TILE // 8)]
                    )
            grad_ref[start : start + TILE, columns] = total.astype(BF16)
        tap_ref[:, columns] = jnp.sum(sums[...].reshape(TAPS, 8, LANES), axis=1)
        return carry

    lax.fori_loop(0, channels // LANES, lane_block, 0)
    grads = grad_ref[...]
    for k in range(groups):
        terms = product(grads, weight[k * depth : (k + 1) * depth, :], 1, 1).astype(BF16)
        if groups == 4:
            half = frames // 2
            top, end = outs[k % 2], outs[2 + k // 2]
            top[k // 2 * half : (k // 2 + 1) * half, :] = terms[:half, :]
            end[k % 2 * half : (k % 2 + 1) * half, :] = terms[half:, :]
        else:
            outs[k][...] = terms


def weight_terms(groups, order, rows, *refs):
    attention, grads, tap_ref = refs[:3]
    outs = refs[3:5]
    terms = refs[5]
    me = lax.axis_index("frame")
    depth = attention.shape[1] // groups
    half = len(order) // 2
    for k in range(groups):
        terms[...] = product(attention[:, k * depth : (k + 1) * depth], grads[...], 0, 0)
        for i, n in enumerate(order):
            there = pl.ds(pl.multiple_of((me ^ n) * rows, rows), rows)
            at = TAPS + ((i % half) * groups + k) * rows
            outs[i // half][at : at + rows, :] = terms[there, :].astype(BF16)
    for out in outs:
        out[0:TAPS, :] = tap_ref[...].astype(BF16)


def plain_terms(attention, grads, out):
    out[...] = product(attention[...], grads[...], 0, 0).astype(BF16)


def add_halves(mine, other, *outs):
    total = mine[...].astype(F32) + other[...].astype(F32)
    share = (total.shape[0] - TAPS) // len(outs)
    for k, out in enumerate(outs):
        at = TAPS + k * share
        out[0:TAPS, :] = total[0:TAPS, :].astype(BF16)
        out[TAPS:, :] = total[at : at + share, :].astype(BF16)


def fold(mine, other, stays, goes):
    total = (mine[...].astype(F32) + other[...].astype(F32)).astype(BF16)
    half = stays.shape[0]
    stays[...] = total[:half, :]
    goes[...] = total[half:, :]


def attend_back(groups, *refs):
    rows_ref = refs[0]
    upstream = refs[1 : groups + 1]
    outs = refs[groups + 1 : -2]
    grads, result = refs[-2:]
    me = lax.axis_index("fsdp")
    width = upstream[0].shape[1]
    local = outs[0].shape[0]
    if groups == 4:
        half = upstream[0].shape[0]
        for i in range(2):
            total = upstream[2 * i][...].astype(F32) + upstream[2 * i + 1][...].astype(F32)
            grads[i * half : (i + 1) * half, :] = total.astype(BF16)
    else:
        grads[...] = tree_sum([ref[...].astype(F32) for ref in upstream]).astype(BF16)
    for head in range(width // HDIM):
        at = head * HDIM
        queries = rows_ref[:, at : at + HDIM]
        keys = rows_ref[:, width + at : width + at + HDIM]
        values = rows_ref[:, 2 * width + at : 2 * width + at + HDIM]
        above = grads[:, at : at + HDIM]
        scores = product(queries, keys, 1, 1) * ROOT
        exponent = jnp.exp(scores - jnp.max(scores, axis=1, keepdims=True))
        weights = exponent * (1.0 / jnp.sum(exponent, axis=1, keepdims=True))
        slopes = product(above, values, 1, 1)
        row_dot = jnp.sum(weights * slopes, axis=1, keepdims=True)
        grad_scores = (weights * (slopes - row_dot)).astype(BF16)
        result[:, at : at + HDIM] = (product(grad_scores, keys, 1, 0) * ROOT).astype(BF16)
        result[:, width + at : width + at + HDIM] = (
            product(grad_scores, queries, 0, 0) * ROOT
        ).astype(BF16)
        result[:, 2 * width + at : 2 * width + at + HDIM] = product(
            weights.astype(BF16), above, 0, 0
        ).astype(BF16)
    for k in range(groups):
        piece = result[block(me ^ k, local, local), :]
        if groups == 4:
            split_up(outs, k, local, slice(None), piece)
        else:
            outs[k][...] = piece


def join_all(groups, scale, *refs):
    folded = groups == 4
    count = 5 if folded else groups
    ahead = refs[: (len(refs) - count - 9) // 2]
    sums = refs[len(ahead) : -count - 9]
    pieces = refs[-count - 9 : -9]
    outs = refs[-9:-3]
    weight_ref, tap_ref, sent = refs[-3:]
    me = lax.axis_index("fsdp")
    copies = []

    def store(source, target):
        copy = pltpu.make_async_copy(source, target, sent.at[len(copies)])
        copy.start()
        copies.append(copy)

    local, width = pieces[0].shape
    width //= 3
    if folded:
        share = local // 2
        own, beside, later_across, across, later_beside = pieces
        ends = ((own, beside, later_across), (own, across, later_beside))
        found = [(k, i * share, share, x, at) for k, i, x, at in places(*ends, share) if k]
        found.append((0, 0, local, own, 0))
    else:
        found = [(k, 0, local, pieces[k], 0) for k in range(groups)]
    for k, start, size, source, first in found:
        columns = block(me ^ k, width, LANES)
        for at in range(3):
            part = source.at[first : first + size, at * width : (at + 1) * width]
            store(part, outs[1 + at].at[0, start : start + size, columns])
    rows, channels = sums[0].shape
    for k in range(groups):
        columns = block(me ^ k, channels, LANES)
        i = min(k, len(ahead) - 1)
        at = local if k > i else 0
        store(ahead[i].at[at : at + local], outs[0].at[0, :, columns])
        at = rows if k > i else 0
        tap_ref[:, columns] = sums[i][at : at + KERNEL, :].astype(F32) * scale
        weight_ref[:, columns] = sums[i][at + TAPS : at + rows, :].astype(F32) * scale
    store(weight_ref, outs[4])
    store(tap_ref, outs[5])
    for copy in copies:
        copy.wait()


def stack(*arrays, after=()):
    shape = (sum(x.shape[0] for x in arrays),) + arrays[0].shape[1:]
    return call(stack_all, [(shape, arrays[0].dtype)], *arrays, after=after)[0]


def exchange_split(sent, after=()):
    if len(sent) != 5:
        return exchange(sent)
    own, beside, across, later_across, later_beside = sent
    shape = [(beside.shape, beside.dtype)]
    beside, across = swap(beside, "fsdp", 1), swap(across, "fsdp", 2)
    (later_across,) = call(stack_parts, shape, later_across, beside, after=after)
    (later_beside,) = call(stack_parts, shape, later_beside, across, after=after)
    return [own, beside, swap(later_across, "fsdp", 2), across, swap(later_beside, "fsdp", 1)]


def turn(sent):
    if len(sent) != 4:
        return exchange(sent)
    rows = sent[0].shape[0]
    first = swap(stack(sent[1], sent[3]), "fsdp", 1)
    second = swap(call(stack_parts, [((2 * rows, sent[0].shape[1]), BF16)], sent[2], first)[0], "fsdp", 2)
    return [sent[0], first, second]


def gather_weight(gathered, masks, groups, count, after):
    rows, channels = gathered.shape[0] * 2 ** (len(masks) + 1) // (groups * count), gathered.shape[1]
    for mask in masks:
        gathered = stack(gathered, swap(gathered, "frame", mask), after=after)
    other = swap(gathered, "frame", 1)
    if rows % 16 == 0:
        return call(
            functools.partial(join_weight, groups, count),
            [((groups * count * rows, channels), BF16)],
            gathered,
            other,
        )[0]
    me = lax.axis_index("frame")
    order = order_of(count)
    place = jnp.array([order.index(n) for n in range(count)])
    both = jnp.concatenate([gathered, other], axis=0).reshape(count, groups, rows, channels)
    ordered = jnp.take(both, place[me ^ jnp.arange(count)], axis=0)
    return ordered.transpose(1, 0, 2, 3).reshape(groups * count * rows, channels)


def weight_halves(attention, grads, tap_terms, groups, count, rows):
    channels = grads.shape[1]
    depth = attention.shape[1] // groups
    share = count // 2 * groups * rows
    bits = count.bit_length() - 1
    order = [sum((i >> b & 1) << (bits - 1 - b) for b in range(bits)) for i in range(count)]
    if rows % 16 == 0:
        halves = call(
            functools.partial(weight_terms, groups, order, rows),
            [((TAPS + share, channels), BF16)] * 2,
            attention,
            grads,
            tap_terms,
            scratch=[pltpu.VMEM((depth, channels), F32)],
        )
    else:
        (terms,) = call(plain_terms, [((groups * depth, channels), BF16)], attention, grads)
        me = lax.axis_index("frame")
        terms = terms.reshape(groups, count, rows, channels)
        terms = jnp.take(terms, me ^ jnp.array(order), axis=1)
        terms = terms.transpose(1, 0, 2, 3).reshape(2, share, channels)
        halves = [jnp.concatenate([tap_terms.astype(BF16), x], axis=0) for x in terms]
    return halves


def add_up(halves, mask, pieces):
    mine, other = halves
    share = (mine.shape[0] - TAPS) // pieces
    return call(
        add_halves,
        [((TAPS + share, mine.shape[1]), BF16)] * pieces,
        mine,
        swap(other, "frame", mask),
    )


def shards(queries, key_rows, value_rows, out_weight, conv_weight, grad_out):
    local, inner = queries.shape[1:]
    rows, model = out_weight.shape
    groups = lax.axis_size("fsdp")
    count = lax.axis_size("frame")
    frames = local * groups
    width = inner // groups
    channels = model // groups
    scale = 1.0 / math.sqrt(frames * count)
    conv_flops = CONV_COST * KERNEL * frames * channels

    folded = groups == 4
    def split(size):
        shape, small = ((local, size), BF16), ((local // 2, size), BF16)
        return [shape, shape, shape, small, small] if folded else [shape] * groups

    sent = call(
        functools.partial(pack_rows, groups),
        split(3 * width + channels) + [((rows, channels), BF16)] * groups,
        queries[0],
        key_rows[0],
        value_rows[0],
        grad_out[0],
        out_weight,
        near=False,
        limit=PACK_LIMIT,
        scratch=[pltpu.VMEM((local, inner), BF16)] * 3
        + [pltpu.VMEM((local, model), BF16), pltpu.VMEM((rows, model), BF16)]
        + [pltpu.SemaphoreType.DMA((5,))],
    )
    gathered = stack(*exchange(sent[-groups:]))
    pieces = exchange_split(sent[:-groups], after=[gathered])
    first, *masks = reversed(masks_of(count)[1:])
    gathered = stack(gathered, swap(gathered, "frame", first))
    held, upstream, *own = call(
        functools.partial(attend, groups),
        [((frames, 3 * width), BF16), ((frames, channels), BF16)]
        + ([((frames // 2, width), BF16)] * 2 if folded else [((frames, width), BF16)]),
        *pieces,
        flops=ATTEND_COST * frames * frames * width,
        after=[gathered],
    )
    gathered = stack(gathered, after=own[:1])
    if folded:
        top, end = own
        beside, across = swap(top, "fsdp", 1), swap(end, "fsdp", 2)
        attention = [top, beside, swap(stack(top, beside), "fsdp", 2)]
        attention += [end, across, swap(stack(end, across), "fsdp", 1)]
        weight = gather_weight(gathered, masks, groups, count, [beside, across])
    else:
        attention = exchange(own * groups)
        weight = gather_weight(gathered, masks, groups, count, attention[1:2])

    outs = call(
        functools.partial(convolve, groups),
        [((frames, inner), BF16), ((frames, channels), BF16), ((frames, channels), F32)]
        + [((local, channels), BF16)] * groups,
        *attention,
        weight,
        conv_weight,
        scratch=[
            pltpu.VMEM((frames + 32, LANES), F32),
            pltpu.VMEM((TAPS, LANES), F32),
            pltpu.VMEM((frames, LANES), F32),
        ],
        flops=conv_flops,
    )
    whole, projected, slope = outs[:3]
    ahead = turn(outs[3:])

    outs = call(
        functools.partial(convolve_back, groups),
        [((frames, channels), BF16), ((TAPS, channels), F32)] + [((frames, width), BF16)] * groups,
        upstream,
        projected,
        slope,
        weight,
        conv_weight,
        scratch=[
            pltpu.VMEM((frames + 32, LANES), F32),
            pltpu.VMEM((TAPS, LANES), F32),
            pltpu.VMEM((frames, LANES), F32),
            pltpu.VMEM((8 * TAPS, LANES), F32),
        ],
        flops=conv_flops * 3 // 2,
    )
    grads, tap_terms = outs[:2]
    if folded:
        stay_top, go_top, stay_end, go_end = outs[2:]
        shapes = [((frames // 2, width), BF16)] * 2
        stay_top, go_top = call(fold, shapes, stay_top, swap(go_top, "fsdp", 1))
        stay_end, go_end = call(fold, shapes, stay_end, swap(go_end, "fsdp", 2))
        above = [stay_top, swap(go_top, "fsdp", 2), stay_end, swap(go_end, "fsdp", 1)]
    else:
        above = exchange(outs[2:])
    halves = weight_halves(whole, grads, tap_terms, groups, count, rows)
    masks = masks_of(count)
    for mask in masks[:-1]:
        halves = add_up(halves, mask, 2)
    sent = call(
        functools.partial(attend_back, groups),
        split(3 * width),
        held,
        *above,
        scratch=[pltpu.VMEM((frames, width), BF16), pltpu.VMEM((frames, 3 * width), BF16)],
        flops=BACK_COST * frames * frames * width,
        after=[halves[1]],
    )
    pieces = exchange_split(sent)
    sums = turn(add_up(halves, masks[-1], groups))
    return tuple(
        call(
            functools.partial(join_all, groups, scale),
            [((1, local, model), BF16)]
            + [((1, local, inner), BF16)] * 3
            + [((rows, model), F32), ((KERNEL, model), F32)],
            *ahead,
            *sums,
            *pieces,
            stored=True,
            scratch=[
                pltpu.VMEM((rows, model), F32),
                pltpu.VMEM((KERNEL, model), F32),
                pltpu.SemaphoreType.DMA((8 * groups,)),
            ],
        )
    )


def solution(mesh):
    return jax.shard_map(
        shards,
        mesh=mesh,
        in_specs=(
            P("frame", "fsdp", None),
            P("frame", "fsdp", None),
            P("frame", "fsdp", None),
            P(("fsdp", "frame"), None),
            P(),
            P("frame", "fsdp", None),
        ),
        out_specs=(
            P("frame", "fsdp", None),
            P("frame", "fsdp", None),
            P("frame", "fsdp", None),
            P("frame", "fsdp", None),
            P(("fsdp", "frame"), None),
            P(),
        ),
        check_vma=False,
    )
```

```python
import functools
import math

import jax
import jax.numpy as jnp
from jax import lax
from jax.experimental import pallas as pl
from jax.experimental.pallas import tpu as pltpu
from jax.sharding import PartitionSpec as P

HDIM = 128
KERNEL = 31
LANES = 128
TILE = 64
TAPS = 32
CONV_COST = 600
ATTEND_COST = 24
BACK_COST = 48
PACK_LIMIT = 60
F32 = jnp.float32
BF16 = jnp.bfloat16
ROOT = 1.0 / math.sqrt(HDIM)


def swap(cells, axis, mask):
    count = lax.axis_size(axis)
    return lax.ppermute(cells, axis, [(i, i ^ mask) for i in range(count)])


def exchange(sent):
    return [sent[0]] + [swap(sent[k], "fsdp", k) for k in range(1, len(sent))]


def masks_of(count):
    return [1 << i for i in range(count.bit_length() - 1)]


def order_of(count):
    order = [0]
    for mask in reversed(masks_of(count)):
        order += [n ^ mask for n in order]
    return order


def call(body, outs, *operands, scratch=(), flops=0, near=True, stored=False, after=(), limit=40, pinned=False):
    vmem = pl.BlockSpec(memory_space=pltpu.VMEM)
    hbm = pl.BlockSpec(memory_space=pltpu.HBM)
    count = len(operands)
    moved = sum(x.size * x.dtype.itemsize for x in operands)
    moved += sum(math.prod(s) * jnp.dtype(t).itemsize for s, t in outs)
    return pl.pallas_call(
        lambda *refs: body(*refs[:count], *refs[count + len(after) :]),
        out_shape=[(pltpu.VMEM if pinned else jax.ShapeDtypeStruct)(s, t) for s, t in outs],
        in_specs=[vmem if near else hbm] * count + [pl.BlockSpec(memory_space=pl.ANY)] * len(after),
        out_specs=[hbm if stored else vmem] * len(outs),
        scratch_shapes=list(scratch),
        cost_estimate=pl.CostEstimate(flops=flops, bytes_accessed=moved, transcendentals=0),
        compiler_params=pltpu.CompilerParams(vmem_limit_bytes=limit * 1024 * 1024),
    )(*operands, *after)


def block(index, size, unit):
    return pl.ds(pl.multiple_of(index * size, unit), size)


def product(left, right, left_dim, right_dim):
    return lax.dot_general(
        left, right, (((left_dim,), (right_dim,)), ((), ())), preferred_element_type=F32
    )


def tree_sum(terms):
    while len(terms) > 1:
        terms = [terms[i] + terms[i + 1] for i in range(0, len(terms), 2)]
    return terms[0]


def places(top, end, rows):
    return (
        (0, 0, top[0], 0),
        (1, 0, top[1], 0),
        (2, 0, top[2], 0),
        (3, 0, top[2], rows),
        (0, 1, end[0], 0),
        (2, 1, end[1], 0),
        (1, 1, end[2], 0),
        (3, 1, end[2], rows),
    )


def split_up(outs, k, rows, columns, cells):
    own, beside, across, later_across, later_beside = outs
    half = rows // 2
    top, end = cells[:half, :], cells[half:, :]
    if k == 0:
        own[:, columns] = cells
    elif k == 1:
        beside[:half, columns] = top
        later_beside[:, columns] = end
    elif k == 2:
        later_across[:, columns] = top
        across[:half, columns] = end
    else:
        beside[half:, columns] = top
        across[half:, columns] = end


def pack_rows(groups, *refs):
    sources = refs[:4]
    outs = refs[4 : 4 + groups]
    weight_outs = refs[4 + groups : -5]
    held = refs[-5:-1]
    arrived = refs[-1]
    copies = [pltpu.make_async_copy(sources[i], held[i], arrived.at[i]) for i in range(4)]
    for copy in copies:
        copy.start()
    for copy in copies:
        copy.wait()
    me = lax.axis_index("fsdp")
    local, inner = held[0].shape
    rows, model = held[3].shape
    width, channels = inner // groups, model // groups
    for k in range(groups):
        columns = block(me ^ k, width, LANES)
        for at in range(3):
            outs[k][:local, at * width : (at + 1) * width] = held[at][:, columns]
        cells = held[3][:, block(me ^ k, channels, LANES)]
        if weight_outs:
            weight_outs[k][...] = cells
        else:
            half = rows // 2
            outs[k][local : local + half, :channels] = cells[:half, :]
            outs[k][local : local + half, channels:] = cells[half:, :width]
            outs[k][local + half : local + rows, :width] = cells[half:, width:]


def pack_columns(groups, *refs):
    source = refs[0]
    me = lax.axis_index("fsdp")
    width = source.shape[1] // groups
    for k in range(groups):
        refs[1 + k][...] = source[:, block(me ^ k, width, LANES)]


def stack_parts(mine, other, out):
    rows = mine.shape[0]
    out[:rows, :] = mine[...]
    out[rows:, :] = other[rows:, :]


def stack_all(*refs):
    at = 0
    for source in refs[:-1]:
        refs[-1][at : at + source.shape[0], :] = source[...]
        at += source.shape[0]


def attend(groups, *refs):
    pieces = refs[:groups]
    rows_ref = refs[groups]
    outs = refs[groups + 1 : 3 + groups if groups == 4 else 2 + groups]
    weight_refs = refs[groups + 1 + len(outs) :]
    me = lax.axis_index("fsdp")
    local = rows_ref.shape[0] // groups
    half, width = outs[0].shape
    for k in range(groups):
        rows_ref[block(me ^ k, local, local), :] = pieces[k][:local, :]
    if weight_refs:
        rows = pieces[0].shape[0] - local
        share = rows // 2
        channels = weight_refs[0].shape[1]
        for k in range(groups):
            at = k * rows
            top, end = pieces[k][local : local + share, :], pieces[k][local + share :, :]
            weight_refs[0][at : at + share, :] = top[:, :channels]
            weight_refs[0][at + share : at + rows, :width] = top[:, channels:]
            weight_refs[0][at + share : at + rows, width:] = end[:, :width]
    for head in range(width // HDIM):
        at = head * HDIM
        queries = rows_ref[:, at : at + HDIM]
        keys = rows_ref[:, width + at : width + at + HDIM]
        values = rows_ref[:, 2 * width + at : 2 * width + at + HDIM]
        scores = product(queries, keys, 1, 1) * ROOT
        exponent = jnp.exp(scores - jnp.max(scores, axis=1, keepdims=True))
        probs = exponent * (1.0 / jnp.sum(exponent, axis=1, keepdims=True))
        mixed = product(probs.astype(BF16), values, 1, 0).astype(BF16)
        for i, out in enumerate(outs):
            out[:, at : at + HDIM] = mixed[i * half : (i + 1) * half, :]


def join_weight(groups, count, mine, other, out):
    me = lax.axis_index("frame")
    rows = mine.shape[0] // (count // 2 * groups)
    width = rows * count
    for i, n in enumerate(order_of(count)[: count // 2]):
        for k in range(groups):
            at = (i * groups + k) * rows
            for core, source in enumerate((mine, other)):
                start = pl.multiple_of(k * width + (me ^ n ^ core) * rows, rows)
                out[pl.ds(start, rows), :] = source[at : at + rows, :]


def shifted(padded, start, tile):
    for residue in range(8):
        taps = range(residue, KERNEL, 8)
        reach = 8 * (len(taps) - 1)
        rows = padded[start + 1 + residue : start + 1 + residue + tile + reach, :]
        yield taps, rows


def convolve(groups, *refs):
    count = 6 if groups == 4 else groups
    pieces = refs[:count]
    weight, taps_ref, attention, projected_ref, slope_ref = refs[count : count + 5]
    ahead = refs[count + 5 : -3]
    padded, taps, result = refs[-3:]
    me = lax.axis_index("fsdp")
    frames = attention.shape[0]
    channels = weight.shape[1]
    local = frames // groups
    padded[0:16, :] = jnp.zeros((16, LANES), F32)
    padded[frames + 16 : frames + 32, :] = jnp.zeros((16, LANES), F32)
    if groups == 4:
        half, depth = pieces[0].shape
        for k, i, source, at in places(pieces[:3], pieces[3:], half):
            start = i * half
            attention[start : start + half, k * depth : (k + 1) * depth] = source[at : at + half, :]
    else:
        depth = pieces[0].shape[1]
        for k in range(groups):
            attention[:, k * depth : (k + 1) * depth] = pieces[k][...]
    projected_ref[...] = product(attention[...], weight[...], 1, 0).astype(BF16)

    def lane_block(c, carry):
        columns = block(c, LANES, LANES)
        padded[16 : frames + 16, :] = projected_ref[:, columns].astype(F32)
        taps[0:KERNEL, :] = taps_ref[:, block(me * (channels // LANES) + c, LANES, LANES)].astype(F32)
        for start in range(0, frames, TILE):
            conv = jnp.zeros((TILE, LANES), F32)
            for indices, rows in shifted(padded, start, TILE):
                for at, j in enumerate(indices):
                    conv += taps[j : j + 1, :] * rows[8 * at : 8 * at + TILE, :]
            gate = 1.0 / (1.0 + jnp.exp(-conv))
            own = padded[start + 16 : start + 16 + TILE, :]
            result[start : start + TILE, :] = own + conv * gate
            slope_ref[start : start + TILE, columns] = gate * (1.0 + conv * (1.0 - gate))
        for k in range(groups):
            cells = result[block(me ^ k, local, local), :].astype(BF16)
            if groups == 4:
                split_up(ahead, k, local, columns, cells)
            else:
                ahead[k][:, columns] = cells
        return carry

    lax.fori_loop(0, channels // LANES, lane_block, 0)


def convolve_back(groups, *refs):
    upstream = refs[:groups]
    projected_ref, slope_ref, weight, taps_ref, grad_ref, tap_ref = refs[groups : groups + 6]
    outs = refs[-groups - 4 : -4]
    padded, taps, above, sums = refs[-4:]
    me = lax.axis_index("fsdp")
    frames, channels = projected_ref.shape
    local = frames // groups
    depth = weight.shape[0] // groups
    padded[0:16, :] = jnp.zeros((16, LANES), F32)
    padded[frames + 16 : frames + 32, :] = jnp.zeros((16, LANES), F32)

    def lane_block(c, carry):
        columns = block(c, LANES, LANES)
        for k in range(groups):
            above[block(me ^ k, local, local), :] = upstream[k][:, columns].astype(F32)
        taps[0:KERNEL, :] = taps_ref[:, block(me * (channels // LANES) + c, LANES, LANES)].astype(F32)
        padded[16 : frames + 16, :] = (above[...] * slope_ref[:, columns]).astype(BF16).astype(F32)
        sums[...] = jnp.zeros(sums.shape, F32)
        for start in range(0, frames, TILE):
            total = above[start : start + TILE, :]
            own = projected_ref[start : start + TILE, columns].astype(F32)
            for indices, rows in shifted(padded, start, TILE):
                for at, j in enumerate(indices):
                    part = rows[8 * at : 8 * at + TILE, :]
                    tap = KERNEL - 1 - j
                    total += taps[tap : tap + 1, :] * part
                    terms = own * part
                    sums[8 * tap : 8 * tap + 8, :] += tree_sum(
                        [terms[8 * i : 8 * i + 8, :] for i in range(TILE // 8)]
                    )
            grad_ref[start : start + TILE, columns] = total.astype(BF16)
        tap_ref[:, columns] = jnp.sum(sums[...].reshape(TAPS, 8, LANES), axis=1)
        return carry

    lax.fori_loop(0, channels // LANES, lane_block, 0)
    grads = grad_ref[...]
    for k in range(groups):
        terms = product(grads, weight[k * depth : (k + 1) * depth, :], 1, 1).astype(BF16)
        if groups == 4:
            half = frames // 2
            top, end = outs[k % 2], outs[2 + k // 2]
            top[k // 2 * half : (k // 2 + 1) * half, :] = terms[:half, :]
            end[k % 2 * half : (k % 2 + 1) * half, :] = terms[half:, :]
        else:
            outs[k][...] = terms


def weight_terms(groups, order, rows, *refs):
    attention, grads, tap_ref = refs[:3]
    outs = refs[3:5]
    terms = refs[5]
    me = lax.axis_index("frame")
    depth = attention.shape[1] // groups
    half = len(order) // 2
    for k in range(groups):
        terms[...] = product(attention[:, k * depth : (k + 1) * depth], grads[...], 0, 0)
        for i, n in enumerate(order):
            there = pl.ds(pl.multiple_of((me ^ n) * rows, rows), rows)
            at = TAPS + ((i % half) * groups + k) * rows
            outs[i // half][at : at + rows, :] = terms[there, :].astype(BF16)
    for out in outs:
        out[0:TAPS, :] = tap_ref[...].astype(BF16)


def plain_terms(attention, grads, out):
    out[...] = product(attention[...], grads[...], 0, 0).astype(BF16)


def add_halves(mine, other, *outs):
    total = mine[...].astype(F32) + other[...].astype(F32)
    share = (total.shape[0] - TAPS) // len(outs)
    for k, out in enumerate(outs):
        at = TAPS + k * share
        out[0:TAPS, :] = total[0:TAPS, :].astype(BF16)
        out[TAPS:, :] = total[at : at + share, :].astype(BF16)


def fold(mine, other, stays, goes):
    total = (mine[...].astype(F32) + other[...].astype(F32)).astype(BF16)
    half = stays.shape[0]
    stays[...] = total[:half, :]
    goes[...] = total[half:, :]


def attend_back(groups, *refs):
    rows_ref = refs[0]
    upstream = refs[1 : groups + 1]
    outs = refs[groups + 1 : -2]
    grads, result = refs[-2:]
    me = lax.axis_index("fsdp")
    width = upstream[0].shape[1]
    local = outs[0].shape[0]
    if groups == 4:
        half = upstream[0].shape[0]
        for i in range(2):
            total = upstream[2 * i][...].astype(F32) + upstream[2 * i + 1][...].astype(F32)
            grads[i * half : (i + 1) * half, :] = total.astype(BF16)
    else:
        grads[...] = tree_sum([ref[...].astype(F32) for ref in upstream]).astype(BF16)
    for head in range(width // HDIM):
        at = head * HDIM
        queries = rows_ref[:, at : at + HDIM]
        keys = rows_ref[:, width + at : width + at + HDIM]
        values = rows_ref[:, 2 * width + at : 2 * width + at + HDIM]
        above = grads[:, at : at + HDIM]
        scores = product(queries, keys, 1, 1) * ROOT
        exponent = jnp.exp(scores - jnp.max(scores, axis=1, keepdims=True))
        weights = exponent * (1.0 / jnp.sum(exponent, axis=1, keepdims=True))
        slopes = product(above, values, 1, 1)
        row_dot = jnp.sum(weights * slopes, axis=1, keepdims=True)
        grad_scores = (weights * (slopes - row_dot)).astype(BF16)
        result[:, at : at + HDIM] = (product(grad_scores, keys, 1, 0) * ROOT).astype(BF16)
        result[:, width + at : width + at + HDIM] = (
            product(grad_scores, queries, 0, 0) * ROOT
        ).astype(BF16)
        result[:, 2 * width + at : 2 * width + at + HDIM] = product(
            weights.astype(BF16), above, 0, 0
        ).astype(BF16)
    for k in range(groups):
        piece = result[block(me ^ k, local, local), :]
        if groups == 4:
            split_up(outs, k, local, slice(None), piece)
        else:
            outs[k][...] = piece


def join_all(groups, scale, *refs):
    count = 5 if groups == 4 else groups
    ahead = refs[:count]
    sums = refs[count : -count - 9]
    pieces = refs[-count - 9 : -9]
    outs = refs[-9:-3]
    weight_ref, tap_ref, sent = refs[-3:]
    me = lax.axis_index("fsdp")
    copies = []

    def store(source, target):
        copy = pltpu.make_async_copy(source, target, sent.at[len(copies)])
        copy.start()
        copies.append(copy)

    local, width = pieces[0].shape
    width //= 3
    channels = sums[0].shape[1]

    def found(arrays):
        if groups != 4:
            return [(k, 0, local, arrays[k], 0) for k in range(groups)]
        share = local // 2
        ends = ((arrays[0], arrays[1], arrays[2]), (arrays[0], arrays[3], arrays[4]))
        parts = [(k, i * share, share, x, at) for k, i, x, at in places(*ends, share) if k]
        return parts + [(0, 0, local, arrays[0], 0)]

    for k, start, size, source, first in found(ahead):
        there = outs[0].at[0, start : start + size, block(me ^ k, channels, LANES)]
        store(source.at[first : first + size], there)
    for k, start, size, source, first in found(pieces):
        columns = block(me ^ k, width, LANES)
        for at in range(3):
            part = source.at[first : first + size, at * width : (at + 1) * width]
            store(part, outs[1 + at].at[0, start : start + size, columns])
    for k in range(groups):
        columns = block(me ^ k, channels, LANES)
        i = min(k, len(sums) - 1)
        first = sums[0].shape[0] if k > i else 0
        last = first + sums[0].shape[0]
        tap_ref[:, columns] = sums[i][first : first + KERNEL, :].astype(F32) * scale
        weight_ref[:, columns] = sums[i][first + TAPS : last, :].astype(F32) * scale
    store(weight_ref, outs[4])
    store(tap_ref, outs[5])
    for copy in copies:
        copy.wait()


def stack(*arrays, after=()):
    shape = (sum(x.shape[0] for x in arrays),) + arrays[0].shape[1:]
    return call(stack_all, [(shape, arrays[0].dtype)], *arrays, after=after)[0]


def exchange_split(sent, after=()):
    if len(sent) != 5:
        return exchange(sent)
    own, beside, across, later_across, later_beside = sent
    shape = [(beside.shape, beside.dtype)]
    beside, across = swap(beside, "fsdp", 1), swap(across, "fsdp", 2)
    (later_across,) = call(stack_parts, shape, later_across, beside, after=after)
    (later_beside,) = call(stack_parts, shape, later_beside, across, after=after)
    return [own, beside, swap(later_across, "fsdp", 2), across, swap(later_beside, "fsdp", 1)]


def turn(sent):
    if len(sent) != 4:
        return exchange(sent)
    shape = [((2 * sent[0].shape[0], sent[0].shape[1]), BF16)]
    first = swap(stack(sent[1], sent[3]), "fsdp", 1)
    second = swap(call(stack_parts, shape, sent[2], first)[0], "fsdp", 2)
    return [sent[0], first, second]


def gather_weight(gathered, masks, groups, count, after):
    rows, channels = gathered.shape[0] * 2 ** (len(masks) + 1) // (groups * count), gathered.shape[1]
    for mask in masks:
        gathered = stack(gathered, swap(gathered, "frame", mask), after=after)
    other = swap(gathered, "frame", 1)
    if rows % 16 == 0:
        return call(
            functools.partial(join_weight, groups, count),
            [((groups * count * rows, channels), BF16)],
            gathered,
            other,
        )[0]
    me = lax.axis_index("frame")
    order = order_of(count)
    place = jnp.array([order.index(n) for n in range(count)])
    both = jnp.concatenate([gathered, other], axis=0).reshape(count, groups, rows, channels)
    ordered = jnp.take(both, place[me ^ jnp.arange(count)], axis=0)
    return ordered.transpose(1, 0, 2, 3).reshape(groups * count * rows, channels)


def weight_halves(attention, grads, tap_terms, groups, count, rows, after):
    channels = grads.shape[1]
    depth = attention.shape[1] // groups
    share = count // 2 * groups * rows
    bits = count.bit_length() - 1
    order = [sum((i >> b & 1) << (bits - 1 - b) for b in range(bits)) for i in range(count)]
    if rows % 16 == 0:
        halves = call(
            functools.partial(weight_terms, groups, order, rows),
            [((TAPS + share, channels), BF16)] * 2,
            attention,
            grads,
            tap_terms,
            scratch=[pltpu.VMEM((depth, channels), F32)],
            after=after,
        )
    else:
        (terms,) = call(plain_terms, [((groups * depth, channels), BF16)], attention, grads)
        me = lax.axis_index("frame")
        terms = terms.reshape(groups, count, rows, channels)
        terms = jnp.take(terms, me ^ jnp.array(order), axis=1)
        terms = terms.transpose(1, 0, 2, 3).reshape(2, share, channels)
        halves = [jnp.concatenate([tap_terms.astype(BF16), x], axis=0) for x in terms]
    return halves


def add_up(halves, mask, pieces):
    mine, other = halves
    share = (mine.shape[0] - TAPS) // pieces
    return call(
        add_halves,
        [((TAPS + share, mine.shape[1]), BF16)] * pieces,
        mine,
        swap(other, "frame", mask),
    )


def shards(queries, key_rows, value_rows, out_weight, conv_weight, grad_out):
    local, inner = queries.shape[1:]
    rows, model = out_weight.shape
    groups = lax.axis_size("fsdp")
    count = lax.axis_size("frame")
    frames = local * groups
    width = inner // groups
    channels = model // groups
    scale = 1.0 / math.sqrt(frames * count)
    conv_flops = CONV_COST * KERNEL * frames * channels

    folded = groups == 4
    def split(size):
        shape, small = ((local, size), BF16), ((local // 2, size), BF16)
        return [shape, shape, shape, small, small] if folded else [shape] * groups

    merged = folded and rows % 32 == 0 and channels == 2 * width
    whole = (groups * rows, channels)
    sent = call(
        functools.partial(pack_rows, groups),
        [((local + (rows if merged else 0), 3 * width), BF16)] * groups
        + ([] if merged else [((rows, channels), BF16)] * groups),
        queries[0],
        key_rows[0],
        value_rows[0],
        out_weight,
        near=False,
        limit=PACK_LIMIT,
        pinned=True,
        scratch=[pltpu.VMEM((local, inner), BF16)] * 3
        + [pltpu.VMEM((rows, model), BF16), pltpu.SemaphoreType.DMA((4,))],
    )
    half = ((frames // 2, width), BF16)
    held, *own = call(
        functools.partial(attend, groups),
        [((frames, 3 * width), BF16)]
        + ([half, half] if folded else [((frames, width), BF16)])
        + ([(whole, BF16)] if merged else []),
        *exchange(sent[:groups]),
        flops=ATTEND_COST * frames * frames * width,
    )
    gathered = own.pop() if merged else stack(*exchange(sent[groups:]))
    first, *masks = reversed(masks_of(count)[1:])
    if folded:
        top, end = own
        beside, across = swap(top, "fsdp", 1), swap(end, "fsdp", 2)
        step = [beside, across]
        attention = [top, beside, swap(stack(top, beside), "fsdp", 2)]
        attention += [end, across, swap(stack(end, across), "fsdp", 1)]
        last = [attention[2], attention[5]]
    else:
        attention = exchange(own * groups)
        step = last = attention[1:2]
    gathered = stack(gathered, swap(gathered, "frame", first), after=step)
    sent = call(
        functools.partial(pack_columns, groups),
        [((local, channels), BF16)] * groups,
        grad_out[0],
        after=step,
    )
    upstream = exchange(sent)
    weight = gather_weight(gathered, masks, groups, count, last + upstream[1:3])

    outs = call(
        functools.partial(convolve, groups),
        [((frames, inner), BF16), ((frames, channels), BF16), ((frames, channels), F32)]
        + split(channels),
        *attention,
        weight,
        conv_weight,
        scratch=[
            pltpu.VMEM((frames + 32, LANES), F32),
            pltpu.VMEM((TAPS, LANES), F32),
            pltpu.VMEM((frames, LANES), F32),
        ],
        flops=conv_flops,
    )
    whole, projected, slope = outs[:3]
    ahead = exchange_split(outs[3:])

    outs = call(
        functools.partial(convolve_back, groups),
        [((frames, channels), BF16), ((TAPS, channels), F32)] + [((frames, width), BF16)] * groups,
        *upstream,
        projected,
        slope,
        weight,
        conv_weight,
        scratch=[
            pltpu.VMEM((frames + 32, LANES), F32),
            pltpu.VMEM((TAPS, LANES), F32),
            pltpu.VMEM((frames, LANES), F32),
            pltpu.VMEM((8 * TAPS, LANES), F32),
        ],
        flops=conv_flops * 3 // 2,
    )
    grads, tap_terms = outs[:2]
    if folded:
        stay_top, go_top, stay_end, go_end = outs[2:]
        shapes = [((frames // 2, width), BF16)] * 2
        stay_top, go_top = call(fold, shapes, stay_top, swap(go_top, "fsdp", 1))
        stay_end, go_end = call(fold, shapes, stay_end, swap(go_end, "fsdp", 2))
        above = [stay_top, swap(go_top, "fsdp", 2), stay_end, swap(go_end, "fsdp", 1)]
    else:
        above = exchange(outs[2:])
    halves = weight_halves(whole, grads, tap_terms, groups, count, rows, ahead[1:4:2])
    masks = masks_of(count)
    for mask in masks[:-1]:
        halves = add_up(halves, mask, 2)
    sent = call(
        functools.partial(attend_back, groups),
        split(3 * width),
        held,
        *above,
        scratch=[pltpu.VMEM((frames, width), BF16), pltpu.VMEM((frames, 3 * width), BF16)],
        flops=BACK_COST * frames * frames * width,
        after=[halves[1], *(ahead[2:5:2] if folded else ())],
    )
    pieces = exchange_split(sent)
    sums = turn(add_up(halves, masks[-1], groups))
    return tuple(
        call(
            functools.partial(join_all, groups, scale),
            [((1, local, model), BF16)]
            + [((1, local, inner), BF16)] * 3
            + [((rows, model), F32), ((KERNEL, model), F32)],
            *ahead,
            *sums,
            *pieces,
            stored=True,
            scratch=[
                pltpu.VMEM((rows, model), F32),
                pltpu.VMEM((KERNEL, model), F32),
                pltpu.SemaphoreType.DMA((8 * groups + 2,)),
            ],
        )
    )


def solution(mesh):
    return jax.shard_map(
        shards,
        mesh=mesh,
        in_specs=(
            P("frame", "fsdp", None),
            P("frame", "fsdp", None),
            P("frame", "fsdp", None),
            P(("fsdp", "frame"), None),
            P(),
            P("frame", "fsdp", None),
        ),
        out_specs=(
            P("frame", "fsdp", None),
            P("frame", "fsdp", None),
            P("frame", "fsdp", None),
            P("frame", "fsdp", None),
            P(("fsdp", "frame"), None),
            P(),
        ),
        check_vma=False,
    )
```

```python
import functools
import math

import jax
import jax.numpy as jnp
from jax import lax
from jax.experimental import pallas as pl
from jax.experimental.pallas import tpu as pltpu
from jax.sharding import PartitionSpec as P

HDIM = 128
KERNEL = 31
LANES = 128
TILE = 64
TAPS = 32
FOLD = 32
CONV_COST = 600
ATTEND_COST = 24
BACK_COST = 48
PACK_LIMIT = 60
F32 = jnp.float32
BF16 = jnp.bfloat16
ROOT = 1.0 / math.sqrt(HDIM)


def swap(cells, axis, mask):
    count = lax.axis_size(axis)
    return lax.ppermute(cells, axis, [(i, i ^ mask) for i in range(count)])


def exchange(sent):
    return [sent[0]] + [swap(sent[k], "fsdp", k) for k in range(1, len(sent))]


def masks_of(count):
    return [1 << i for i in range(count.bit_length() - 1)]


def order_of(count):
    order = [0]
    for mask in reversed(masks_of(count)):
        order += [n ^ mask for n in order]
    return order


def call(body, outs, *operands, scratch=(), flops=0, near=True, stored=False, after=(), limit=40, pinned=False):
    vmem = pl.BlockSpec(memory_space=pltpu.VMEM)
    hbm = pl.BlockSpec(memory_space=pltpu.HBM)
    count = len(operands)
    moved = sum(x.size * x.dtype.itemsize for x in operands)
    moved += sum(math.prod(s) * jnp.dtype(t).itemsize for s, t in outs)
    return pl.pallas_call(
        lambda *refs: body(*refs[:count], *refs[count + len(after) :]),
        out_shape=[(pltpu.VMEM if pinned else jax.ShapeDtypeStruct)(s, t) for s, t in outs],
        in_specs=[vmem if near else hbm] * count + [pl.BlockSpec(memory_space=pl.ANY)] * len(after),
        out_specs=[hbm if stored else vmem] * len(outs),
        scratch_shapes=list(scratch),
        cost_estimate=pl.CostEstimate(flops=flops, bytes_accessed=moved, transcendentals=0),
        compiler_params=pltpu.CompilerParams(vmem_limit_bytes=limit * 1024 * 1024),
    )(*operands, *after)


def block(index, size, unit):
    return pl.ds(pl.multiple_of(index * size, unit), size)


def product(left, right, left_dim, right_dim):
    return lax.dot_general(
        left, right, (((left_dim,), (right_dim,)), ((), ())), preferred_element_type=F32
    )


def tree_sum(terms):
    while len(terms) > 1:
        terms = [terms[i] + terms[i + 1] for i in range(0, len(terms), 2)]
    return terms[0]


def places(top, end, rows):
    return (
        (0, 0, top[0], 0),
        (1, 0, top[1], 0),
        (2, 0, top[2], 0),
        (3, 0, top[2], rows),
        (0, 1, end[0], 0),
        (2, 1, end[1], 0),
        (1, 1, end[2], 0),
        (3, 1, end[2], rows),
    )


def split_up(outs, k, rows, columns, cells):
    own, beside, across, later_across, later_beside = outs
    half = rows // 2
    top, end = cells[:half, :], cells[half:, :]
    if k == 0:
        own[:, columns] = cells
    elif k == 1:
        beside[:half, columns] = top
        later_beside[:, columns] = end
    elif k == 2:
        later_across[:, columns] = top
        across[:half, columns] = end
    else:
        beside[half:, columns] = top
        across[half:, columns] = end


def pack_rows(groups, *refs):
    sources = refs[:4]
    outs = refs[4 : 4 + groups]
    weight_outs = refs[4 + groups : -5]
    held = refs[-5:-1]
    arrived = refs[-1]
    copies = [pltpu.make_async_copy(sources[i], held[i], arrived.at[i]) for i in range(4)]
    for copy in copies:
        copy.start()
    for copy in copies:
        copy.wait()
    me = lax.axis_index("fsdp")
    local, inner = held[0].shape
    rows, model = held[3].shape
    width, channels = inner // groups, model // groups
    for k in range(groups):
        columns = block(me ^ k, width, LANES)
        cells = held[3][:, block(me ^ k, channels, LANES)]
        if weight_outs:
            weight_outs[k][...] = cells
            for at in range(3):
                outs[k][:, at * width : (at + 1) * width] = held[at][:, columns]
        else:
            for at, start, there, column in folds(local, width):
                outs[k][there : there + FOLD, column : column + width] = held[at][start : start + FOLD, columns]
            below = outs[k].shape[0] - rows // 2
            outs[k][below:, :channels] = cells[: rows // 2, :]
            outs[k][below:, channels:] = cells[rows // 2 :, :]


def folds(local, width):
    tall = 3 * local // 4
    for start in range(0, 3 * local, FOLD):
        yield start // local, start % local, start % tall, start // tall * width


def pack_columns(groups, *refs):
    source = refs[0]
    me = lax.axis_index("fsdp")
    width = source.shape[1] // groups
    for k in range(groups):
        refs[1 + k][...] = source[:, block(me ^ k, width, LANES)]


def stack_parts(mine, other, out):
    rows = mine.shape[0]
    out[:rows, :] = mine[...]
    out[rows:, :] = other[rows:, :]


def stack_all(*refs):
    at = 0
    for source in refs[:-1]:
        refs[-1][at : at + source.shape[0], :] = source[...]
        at += source.shape[0]


def attend(groups, *refs):
    pieces = refs[:groups]
    rows_ref = refs[groups]
    outs = refs[groups + 1 : 3 + groups if groups == 4 else 2 + groups]
    weight_refs = refs[groups + 1 + len(outs) :]
    me = lax.axis_index("fsdp")
    local = rows_ref.shape[0] // groups
    half, width = outs[0].shape
    for k in range(groups):
        if weight_refs:
            for at, start, there, column in folds(local, width):
                first = pl.multiple_of((me ^ k) * local + start, FOLD)
                cells = pieces[k][there : there + FOLD, column : column + width]
                rows_ref[pl.ds(first, FOLD), at * width : (at + 1) * width] = cells
            channels = weight_refs[0].shape[1]
            rows = weight_refs[0].shape[0] // groups
            at, share = k * rows, rows // 2
            below = pieces[k].shape[0] - share
            weight_refs[0][at : at + share, :] = pieces[k][below:, :channels]
            weight_refs[0][at + share : at + rows, :] = pieces[k][below:, channels:]
        else:
            rows_ref[block(me ^ k, local, local), :] = pieces[k][...]
    for head in range(width // HDIM):
        at = head * HDIM
        queries = rows_ref[:, at : at + HDIM]
        keys = rows_ref[:, width + at : width + at + HDIM]
        values = rows_ref[:, 2 * width + at : 2 * width + at + HDIM]
        scores = product(queries, keys, 1, 1) * ROOT
        exponent = jnp.exp(scores - jnp.max(scores, axis=1, keepdims=True))
        probs = exponent * (1.0 / jnp.sum(exponent, axis=1, keepdims=True))
        mixed = product(probs.astype(BF16), values, 1, 0).astype(BF16)
        for i, out in enumerate(outs):
            out[:, at : at + HDIM] = mixed[i * half : (i + 1) * half, :]


def join_weight(groups, count, mine, other, out):
    me = lax.axis_index("frame")
    rows = mine.shape[0] // (count // 2 * groups)
    width = rows * count
    for i, n in enumerate(order_of(count)[: count // 2]):
        for k in range(groups):
            at = (i * groups + k) * rows
            for core, source in enumerate((mine, other)):
                start = pl.multiple_of(k * width + (me ^ n ^ core) * rows, rows)
                out[pl.ds(start, rows), :] = source[at : at + rows, :]


def shifted(padded, start, tile):
    for residue in range(8):
        taps = range(residue, KERNEL, 8)
        reach = 8 * (len(taps) - 1)
        rows = padded[start + 1 + residue : start + 1 + residue + tile + reach, :]
        yield taps, rows


def convolve(groups, *refs):
    count = 6 if groups == 4 else groups
    pieces = refs[:count]
    weight, taps_ref, attention, projected_ref, slope_ref = refs[count : count + 5]
    ahead = refs[count + 5 : -3]
    padded, taps, result = refs[-3:]
    me = lax.axis_index("fsdp")
    frames = attention.shape[0]
    channels = weight.shape[1]
    local = frames // groups
    padded[0:16, :] = jnp.zeros((16, LANES), F32)
    padded[frames + 16 : frames + 32, :] = jnp.zeros((16, LANES), F32)
    if groups == 4:
        half, depth = pieces[0].shape
        for k, i, source, at in places(pieces[:3], pieces[3:], half):
            start = i * half
            attention[start : start + half, k * depth : (k + 1) * depth] = source[at : at + half, :]
    else:
        depth = pieces[0].shape[1]
        for k in range(groups):
            attention[:, k * depth : (k + 1) * depth] = pieces[k][...]
    projected_ref[...] = product(attention[...], weight[...], 1, 0).astype(BF16)

    def lane_block(c, carry):
        columns = block(c, LANES, LANES)
        padded[16 : frames + 16, :] = projected_ref[:, columns].astype(F32)
        taps[0:KERNEL, :] = taps_ref[:, block(me * (channels // LANES) + c, LANES, LANES)].astype(F32)
        for start in range(0, frames, TILE):
            conv = jnp.zeros((TILE, LANES), F32)
            for indices, rows in shifted(padded, start, TILE):
                for at, j in enumerate(indices):
                    conv += taps[j : j + 1, :] * rows[8 * at : 8 * at + TILE, :]
            gate = 1.0 / (1.0 + jnp.exp(-conv))
            own = padded[start + 16 : start + 16 + TILE, :]
            result[start : start + TILE, :] = own + conv * gate
            slope_ref[start : start + TILE, columns] = gate * (1.0 + conv * (1.0 - gate))
        for k in range(groups):
            cells = result[block(me ^ k, local, local), :].astype(BF16)
            if groups == 4:
                split_up(ahead, k, local, columns, cells)
            else:
                ahead[k][:, columns] = cells
        return carry

    lax.fori_loop(0, channels // LANES, lane_block, 0)


def convolve_back(groups, *refs):
    upstream = refs[:groups]
    projected_ref, slope_ref, weight, taps_ref, grad_ref, tap_ref = refs[groups : groups + 6]
    outs = refs[-groups - 4 : -4]
    padded, taps, above, sums = refs[-4:]
    me = lax.axis_index("fsdp")
    frames, channels = projected_ref.shape
    local = frames // groups
    depth = weight.shape[0] // groups
    padded[0:16, :] = jnp.zeros((16, LANES), F32)
    padded[frames + 16 : frames + 32, :] = jnp.zeros((16, LANES), F32)

    def lane_block(c, carry):
        columns = block(c, LANES, LANES)
        for k in range(groups):
            above[block(me ^ k, local, local), :] = upstream[k][:, columns].astype(F32)
        taps[0:KERNEL, :] = taps_ref[:, block(me * (channels // LANES) + c, LANES, LANES)].astype(F32)
        padded[16 : frames + 16, :] = (above[...] * slope_ref[:, columns]).astype(BF16).astype(F32)
        sums[...] = jnp.zeros(sums.shape, F32)
        for start in range(0, frames, TILE):
            total = above[start : start + TILE, :]
            own = projected_ref[start : start + TILE, columns].astype(F32)
            for indices, rows in shifted(padded, start, TILE):
                for at, j in enumerate(indices):
                    part = rows[8 * at : 8 * at + TILE, :]
                    tap = KERNEL - 1 - j
                    total += taps[tap : tap + 1, :] * part
                    terms = own * part
                    sums[8 * tap : 8 * tap + 8, :] += tree_sum(
                        [terms[8 * i : 8 * i + 8, :] for i in range(TILE // 8)]
                    )
            grad_ref[start : start + TILE, columns] = total.astype(BF16)
        tap_ref[:, columns] = jnp.sum(sums[...].reshape(TAPS, 8, LANES), axis=1)
        return carry

    lax.fori_loop(0, channels // LANES, lane_block, 0)
    grads = grad_ref[...]
    for k in range(groups):
        terms = product(grads, weight[k * depth : (k + 1) * depth, :], 1, 1).astype(BF16)
        if groups == 4:
            half = frames // 2
            top, end = outs[k % 2], outs[2 + k // 2]
            top[k // 2 * half : (k // 2 + 1) * half, :] = terms[:half, :]
            end[k % 2 * half : (k % 2 + 1) * half, :] = terms[half:, :]
        else:
            outs[k][...] = terms


def weight_terms(groups, order, rows, *refs):
    attention, grads, tap_ref = refs[:3]
    outs = refs[3:5]
    terms = refs[5]
    me = lax.axis_index("frame")
    depth = attention.shape[1] // groups
    half = len(order) // 2
    for k in range(groups):
        terms[...] = product(attention[:, k * depth : (k + 1) * depth], grads[...], 0, 0)
        for i, n in enumerate(order):
            there = pl.ds(pl.multiple_of((me ^ n) * rows, rows), rows)
            at = TAPS + ((i % half) * groups + k) * rows
            outs[i // half][at : at + rows, :] = terms[there, :].astype(BF16)
    for out in outs:
        out[0:TAPS, :] = tap_ref[...].astype(BF16)


def plain_terms(attention, grads, out):
    out[...] = product(attention[...], grads[...], 0, 0).astype(BF16)


def add_halves(mine, other, *outs):
    total = mine[...].astype(F32) + other[...].astype(F32)
    share = (total.shape[0] - TAPS) // len(outs)
    for k, out in enumerate(outs):
        at = TAPS + k * share
        out[0:TAPS, :] = total[0:TAPS, :].astype(BF16)
        out[TAPS:, :] = total[at : at + share, :].astype(BF16)


def fold(mine, other, stays, goes):
    total = (mine[...].astype(F32) + other[...].astype(F32)).astype(BF16)
    half = stays.shape[0]
    stays[...] = total[:half, :]
    goes[...] = total[half:, :]


def weigh(rows_ref, out):
    width = rows_ref.shape[1] // 3
    for head in range(width // HDIM):
        at = head * HDIM
        queries = rows_ref[:, at : at + HDIM]
        keys = rows_ref[:, width + at : width + at + HDIM]
        scores = product(queries, keys, 1, 1) * ROOT
        exponent = jnp.exp(scores - jnp.max(scores, axis=1, keepdims=True))
        out[head] = exponent * (1.0 / jnp.sum(exponent, axis=1, keepdims=True))


def attend_back(groups, *refs):
    rows_ref, weights_ref = refs[:2]
    upstream = refs[2 : groups + 2]
    outs = refs[groups + 2 : -2]
    grads, result = refs[-2:]
    me = lax.axis_index("fsdp")
    width = upstream[0].shape[1]
    local = outs[0].shape[0]
    if groups == 4:
        half = upstream[0].shape[0]
        for i in range(2):
            total = upstream[2 * i][...].astype(F32) + upstream[2 * i + 1][...].astype(F32)
            grads[i * half : (i + 1) * half, :] = total.astype(BF16)
    else:
        grads[...] = tree_sum([ref[...].astype(F32) for ref in upstream]).astype(BF16)
    for head in range(width // HDIM):
        at = head * HDIM
        queries = rows_ref[:, at : at + HDIM]
        keys = rows_ref[:, width + at : width + at + HDIM]
        values = rows_ref[:, 2 * width + at : 2 * width + at + HDIM]
        above = grads[:, at : at + HDIM]
        weights = weights_ref[head]
        slopes = product(above, values, 1, 1)
        row_dot = jnp.sum(weights * slopes, axis=1, keepdims=True)
        grad_scores = (weights * (slopes - row_dot)).astype(BF16)
        result[:, at : at + HDIM] = (product(grad_scores, keys, 1, 0) * ROOT).astype(BF16)
        result[:, width + at : width + at + HDIM] = (
            product(grad_scores, queries, 0, 0) * ROOT
        ).astype(BF16)
        result[:, 2 * width + at : 2 * width + at + HDIM] = product(
            weights.astype(BF16), above, 0, 0
        ).astype(BF16)
    for k in range(groups):
        piece = result[block(me ^ k, local, local), :]
        if groups == 4:
            split_up(outs, k, local, slice(None), piece)
        else:
            outs[k][...] = piece


def join_all(groups, scale, *refs):
    count = 5 if groups == 4 else groups
    ahead = refs[:count]
    sums = refs[count : -count - 9]
    pieces = refs[-count - 9 : -9]
    outs = refs[-9:-3]
    weight_ref, tap_ref, sent = refs[-3:]
    me = lax.axis_index("fsdp")
    copies = []

    def store(source, target):
        copy = pltpu.make_async_copy(source, target, sent.at[len(copies)])
        copy.start()
        copies.append(copy)

    local, width = pieces[0].shape
    width //= 3
    channels = sums[0].shape[1]

    def found(arrays):
        if groups != 4:
            return [(k, 0, local, arrays[k], 0) for k in range(groups)]
        share = local // 2
        ends = ((arrays[0], arrays[1], arrays[2]), (arrays[0], arrays[3], arrays[4]))
        parts = [(k, i * share, share, x, at) for k, i, x, at in places(*ends, share) if k]
        return parts + [(0, 0, local, arrays[0], 0)]

    for k, start, size, source, first in found(ahead):
        there = outs[0].at[0, start : start + size, block(me ^ k, channels, LANES)]
        store(source.at[first : first + size], there)
    for k, start, size, source, first in found(pieces):
        columns = block(me ^ k, width, LANES)
        for at in range(3):
            part = source.at[first : first + size, at * width : (at + 1) * width]
            store(part, outs[1 + at].at[0, start : start + size, columns])
    for k in range(groups):
        columns = block(me ^ k, channels, LANES)
        i = min(k, len(sums) - 1)
        first = sums[0].shape[0] if k > i else 0
        last = first + sums[0].shape[0]
        tap_ref[:, columns] = sums[i][first : first + KERNEL, :].astype(F32) * scale
        weight_ref[:, columns] = sums[i][first + TAPS : last, :].astype(F32) * scale
    store(weight_ref, outs[4])
    store(tap_ref, outs[5])
    for copy in copies:
        copy.wait()


def stack(*arrays, after=()):
    shape = (sum(x.shape[0] for x in arrays),) + arrays[0].shape[1:]
    return call(stack_all, [(shape, arrays[0].dtype)], *arrays, after=after)[0]


def exchange_split(sent, after=()):
    if len(sent) != 5:
        return exchange(sent)
    own, beside, across, later_across, later_beside = sent
    shape = [(beside.shape, beside.dtype)]
    beside, across = swap(beside, "fsdp", 1), swap(across, "fsdp", 2)
    (later_across,) = call(stack_parts, shape, later_across, beside, after=after)
    (later_beside,) = call(stack_parts, shape, later_beside, across, after=after)
    return [own, beside, swap(later_across, "fsdp", 2), across, swap(later_beside, "fsdp", 1)]


def turn(sent):
    if len(sent) != 4:
        return exchange(sent)
    shape = [((2 * sent[0].shape[0], sent[0].shape[1]), BF16)]
    first = swap(stack(sent[1], sent[3]), "fsdp", 1)
    second = swap(call(stack_parts, shape, sent[2], first)[0], "fsdp", 2)
    return [sent[0], first, second]


def gather_weight(mine, groups, count, after):
    rows, channels = mine.shape[0] // groups, mine.shape[1]
    pieces = [mine]
    for mask in reversed(masks_of(count)[1:]):
        pieces += [swap(piece, "frame", mask) for piece in pieces]
    gathered = stack(*pieces, after=after)
    other = swap(gathered, "frame", 1)
    if rows % 16 == 0:
        return call(
            functools.partial(join_weight, groups, count),
            [((groups * count * rows, channels), BF16)],
            gathered,
            other,
        )[0]
    me = lax.axis_index("frame")
    order = order_of(count)
    place = jnp.array([order.index(n) for n in range(count)])
    both = jnp.concatenate([gathered, other], axis=0).reshape(count, groups, rows, channels)
    ordered = jnp.take(both, place[me ^ jnp.arange(count)], axis=0)
    return ordered.transpose(1, 0, 2, 3).reshape(groups * count * rows, channels)


def weight_halves(attention, grads, tap_terms, groups, count, rows, after):
    channels = grads.shape[1]
    depth = attention.shape[1] // groups
    share = count // 2 * groups * rows
    bits = count.bit_length() - 1
    order = [sum((i >> b & 1) << (bits - 1 - b) for b in range(bits)) for i in range(count)]
    if rows % 16 == 0:
        halves = call(
            functools.partial(weight_terms, groups, order, rows),
            [((TAPS + share, channels), BF16)] * 2,
            attention,
            grads,
            tap_terms,
            scratch=[pltpu.VMEM((depth, channels), F32)],
            after=after,
        )
    else:
        (terms,) = call(plain_terms, [((groups * depth, channels), BF16)], attention, grads)
        me = lax.axis_index("frame")
        terms = terms.reshape(groups, count, rows, channels)
        terms = jnp.take(terms, me ^ jnp.array(order), axis=1)
        terms = terms.transpose(1, 0, 2, 3).reshape(2, share, channels)
        halves = [jnp.concatenate([tap_terms.astype(BF16), x], axis=0) for x in terms]
    return halves


def add_up(halves, mask, pieces):
    mine, other = halves
    share = (mine.shape[0] - TAPS) // pieces
    return call(
        add_halves,
        [((TAPS + share, mine.shape[1]), BF16)] * pieces,
        mine,
        swap(other, "frame", mask),
    )


def shards(queries, key_rows, value_rows, out_weight, conv_weight, grad_out):
    local, inner = queries.shape[1:]
    rows, model = out_weight.shape
    groups = lax.axis_size("fsdp")
    count = lax.axis_size("frame")
    frames = local * groups
    width = inner // groups
    channels = model // groups
    scale = 1.0 / math.sqrt(frames * count)
    conv_flops = CONV_COST * KERNEL * frames * channels

    folded = groups == 4
    def split(size):
        shape, small = ((local, size), BF16), ((local // 2, size), BF16)
        return [shape, shape, shape, small, small] if folded else [shape] * groups

    merged = folded and rows % 32 == 0 and channels == 2 * width and local % (4 * FOLD) == 0
    shape = (3 * local // 4 + rows // 2, 4 * width) if merged else (local, 3 * width)
    whole = (groups * rows, channels)
    sent = call(
        functools.partial(pack_rows, groups),
        [(shape, BF16)] * groups
        + ([] if merged else [((rows, channels), BF16)] * groups),
        queries[0],
        key_rows[0],
        value_rows[0],
        out_weight,
        near=False,
        limit=PACK_LIMIT,
        pinned=True,
        scratch=[pltpu.VMEM((local, inner), BF16)] * 3
        + [pltpu.VMEM((rows, model), BF16), pltpu.SemaphoreType.DMA((4,))],
    )
    half = ((frames // 2, width), BF16)
    held, *own = call(
        functools.partial(attend, groups),
        [((frames, 3 * width), BF16)]
        + ([half, half] if folded else [((frames, width), BF16)])
        + ([(whole, BF16)] if merged else []),
        *exchange(sent[:groups]),
        flops=ATTEND_COST * frames * frames * width,
    )
    gathered = own.pop() if merged else stack(*exchange(sent[groups:]))
    if folded:
        top, end = own
        beside, across = swap(top, "fsdp", 1), swap(end, "fsdp", 2)
        step = [beside, across]
        attention = [top, beside, swap(stack(top, beside), "fsdp", 2)]
        attention += [end, across, swap(stack(end, across), "fsdp", 1)]
        last = [attention[2], attention[5]]
    else:
        attention = exchange(own * groups)
        step = last = attention[1:2]
    sent = call(
        functools.partial(pack_columns, groups),
        [((local, channels), BF16)] * groups,
        grad_out[0],
        after=step,
    )
    upstream = exchange(sent)
    weight = gather_weight(gathered, groups, count, last + upstream[1:3])

    outs = call(
        functools.partial(convolve, groups),
        [((frames, inner), BF16), ((frames, channels), BF16), ((frames, channels), F32)]
        + split(channels),
        *attention,
        weight,
        conv_weight,
        scratch=[
            pltpu.VMEM((frames + 32, LANES), F32),
            pltpu.VMEM((TAPS, LANES), F32),
            pltpu.VMEM((frames, LANES), F32),
        ],
        flops=conv_flops,
    )
    whole, projected, slope = outs[:3]
    (weights,) = call(weigh, [((width // HDIM, frames, frames), F32)], held)
    ahead = exchange_split(outs[3:], after=[weights])

    outs = call(
        functools.partial(convolve_back, groups),
        [((frames, channels), BF16), ((TAPS, channels), F32)] + [((frames, width), BF16)] * groups,
        *upstream,
        projected,
        slope,
        weight,
        conv_weight,
        scratch=[
            pltpu.VMEM((frames + 32, LANES), F32),
            pltpu.VMEM((TAPS, LANES), F32),
            pltpu.VMEM((frames, LANES), F32),
            pltpu.VMEM((8 * TAPS, LANES), F32),
        ],
        flops=conv_flops * 3 // 2,
    )
    grads, tap_terms = outs[:2]
    if folded:
        stay_top, go_top, stay_end, go_end = outs[2:]
        shapes = [((frames // 2, width), BF16)] * 2
        stay_top, go_top = call(fold, shapes, stay_top, swap(go_top, "fsdp", 1))
        stay_end, go_end = call(fold, shapes, stay_end, swap(go_end, "fsdp", 2))
        above = [stay_top, swap(go_top, "fsdp", 2), stay_end, swap(go_end, "fsdp", 1)]
    else:
        above = exchange(outs[2:])
    halves = weight_halves(whole, grads, tap_terms, groups, count, rows, ahead[1:4:2])
    masks = masks_of(count)
    for mask in masks[:-1]:
        halves = add_up(halves, mask, 2)
    sent = call(
        functools.partial(attend_back, groups),
        split(3 * width),
        held,
        weights,
        *above,
        scratch=[pltpu.VMEM((frames, width), BF16), pltpu.VMEM((frames, 3 * width), BF16)],
        flops=BACK_COST * frames * frames * width,
        after=[halves[1], *(ahead[2:5:2] if folded else ())],
    )
    pieces = exchange_split(sent)
    sums = turn(add_up(halves, masks[-1], groups))
    return tuple(
        call(
            functools.partial(join_all, groups, scale),
            [((1, local, model), BF16)]
            + [((1, local, inner), BF16)] * 3
            + [((rows, model), F32), ((KERNEL, model), F32)],
            *ahead,
            *sums,
            *pieces,
            stored=True,
            scratch=[
                pltpu.VMEM((rows, model), F32),
                pltpu.VMEM((KERNEL, model), F32),
                pltpu.SemaphoreType.DMA((8 * groups + 2,)),
            ],
        )
    )


def solution(mesh):
    return jax.shard_map(
        shards,
        mesh=mesh,
        in_specs=(
            P("frame", "fsdp", None),
            P("frame", "fsdp", None),
            P("frame", "fsdp", None),
            P(("fsdp", "frame"), None),
            P(),
            P("frame", "fsdp", None),
        ),
        out_specs=(
            P("frame", "fsdp", None),
            P("frame", "fsdp", None),
            P("frame", "fsdp", None),
            P("frame", "fsdp", None),
            P(("fsdp", "frame"), None),
            P(),
        ),
        check_vma=False,
    )
```

```python
import functools
import math

import jax
import jax.numpy as jnp
from jax import lax
from jax.experimental import pallas as pl
from jax.experimental.pallas import tpu as pltpu
from jax.sharding import PartitionSpec as P

HDIM = 128
KERNEL = 31
LANES = 128
TILE = 64
TAPS = 32
FOLD = 32
CONV_COST = 600
ATTEND_COST = 24
BACK_COST = 48
SPLIT_BACK = False
PAD = 32
PACK_LIMIT = 60
F32 = jnp.float32
BF16 = jnp.bfloat16
ROOT = 1.0 / math.sqrt(HDIM)


def swap(cells, axis, mask):
    count = lax.axis_size(axis)
    return lax.ppermute(cells, axis, [(i, i ^ mask) for i in range(count)])


def exchange(sent):
    return [sent[0]] + [swap(sent[k], "fsdp", k) for k in range(1, len(sent))]


def masks_of(count):
    return [1 << i for i in range(count.bit_length() - 1)]


def order_of(count):
    order = [0]
    for mask in reversed(masks_of(count)):
        order += [n ^ mask for n in order]
    return order


def call(body, outs, *operands, scratch=(), flops=0, near=True, stored=False, after=(), limit=40, pinned=False):
    vmem = pl.BlockSpec(memory_space=pltpu.VMEM)
    hbm = pl.BlockSpec(memory_space=pltpu.HBM)
    count = len(operands)
    moved = sum(x.size * x.dtype.itemsize for x in operands)
    moved += sum(math.prod(s) * jnp.dtype(t).itemsize for s, t in outs)
    return pl.pallas_call(
        lambda *refs: body(*refs[:count], *refs[count + len(after) :]),
        out_shape=[(pltpu.VMEM if pinned else jax.ShapeDtypeStruct)(s, t) for s, t in outs],
        in_specs=[vmem if near else hbm] * count + [pl.BlockSpec(memory_space=pl.ANY)] * len(after),
        out_specs=[hbm if stored else vmem] * len(outs),
        scratch_shapes=list(scratch),
        cost_estimate=pl.CostEstimate(flops=flops, bytes_accessed=moved, transcendentals=0),
        compiler_params=pltpu.CompilerParams(vmem_limit_bytes=limit * 1024 * 1024),
    )(*operands, *after)


def block(index, size, unit):
    return pl.ds(pl.multiple_of(index * size, unit), size)


def product(left, right, left_dim, right_dim):
    return lax.dot_general(
        left, right, (((left_dim,), (right_dim,)), ((), ())), preferred_element_type=F32
    )


def tree_sum(terms):
    while len(terms) > 1:
        terms = [terms[i] + terms[i + 1] for i in range(0, len(terms), 2)]
    return terms[0]


def places(top, end, rows):
    return (
        (0, 0, top[0], 0),
        (1, 0, top[1], 0),
        (2, 0, top[2], 0),
        (3, 0, top[2], rows),
        (0, 1, end[0], 0),
        (2, 1, end[1], 0),
        (1, 1, end[2], 0),
        (3, 1, end[2], rows),
    )


def split_up(outs, k, rows, columns, cells):
    own, beside, across, later_across, later_beside = outs
    half = rows // 2
    top, end = cells[:half, :], cells[half:, :]
    if k == 0:
        own[:, columns] = cells
    elif k == 1:
        beside[:half, columns] = top
        later_beside[:, columns] = end
    elif k == 2:
        later_across[:, columns] = top
        across[:half, columns] = end
    else:
        beside[half:, columns] = top
        across[half:, columns] = end


def pack_rows(groups, *refs):
    sources = refs[:4]
    outs = refs[4 : 4 + groups]
    weight_outs = refs[4 + groups : -5]
    held = refs[-5:-1]
    arrived = refs[-1]
    copies = [pltpu.make_async_copy(sources[i], held[i], arrived.at[i]) for i in range(4)]
    for copy in copies:
        copy.start()
    for copy in copies:
        copy.wait()
    me = lax.axis_index("fsdp")
    local, inner = held[0].shape
    rows, model = held[3].shape
    width, channels = inner // groups, model // groups
    for k in range(groups):
        columns = block(me ^ k, width, LANES)
        cells = held[3][:, block(me ^ k, channels, LANES)]
        if weight_outs:
            weight_outs[k][...] = cells
            for at in range(3):
                outs[k][:, at * width : (at + 1) * width] = held[at][:, columns]
        else:
            for at, start, there, column in folds(local, width):
                outs[k][there : there + FOLD, column : column + width] = held[at][start : start + FOLD, columns]
            below = outs[k].shape[0] - rows // 2
            outs[k][below:, :channels] = cells[: rows // 2, :]
            outs[k][below:, channels:] = cells[rows // 2 :, :]


def folds(local, width):
    tall = 3 * local // 4
    for start in range(0, 3 * local, FOLD):
        yield start // local, start % local, start % tall, start // tall * width


def pack_columns(groups, *refs):
    source = refs[0]
    me = lax.axis_index("fsdp")
    width = source.shape[1] // groups
    for k in range(groups):
        refs[1 + k][...] = source[:, block(me ^ k, width, LANES)]


def stack_parts(mine, other, out):
    rows = mine.shape[0]
    out[:rows, :] = mine[...]
    out[rows:, :] = other[rows:, :]


def stack_all(*refs):
    at = 0
    for source in refs[:-1]:
        refs[-1][at : at + source.shape[0], :] = source[...]
        at += source.shape[0]


def attend(groups, *refs):
    pieces = refs[:groups]
    rows_ref = refs[groups]
    outs = refs[groups + 1 : 3 + groups if groups == 4 else 2 + groups]
    weight_refs = refs[groups + 1 + len(outs) :]
    me = lax.axis_index("fsdp")
    local = rows_ref.shape[0] // groups
    half, width = outs[0].shape
    for k in range(groups):
        if weight_refs:
            for at, start, there, column in folds(local, width):
                first = pl.multiple_of((me ^ k) * local + start, FOLD)
                cells = pieces[k][there : there + FOLD, column : column + width]
                rows_ref[pl.ds(first, FOLD), at * width : (at + 1) * width] = cells
            channels = weight_refs[0].shape[1]
            rows = weight_refs[0].shape[0] // groups
            at, share = k * rows, rows // 2
            below = pieces[k].shape[0] - share
            weight_refs[0][at : at + share, :] = pieces[k][below:, :channels]
            weight_refs[0][at + share : at + rows, :] = pieces[k][below:, channels:]
        else:
            rows_ref[block(me ^ k, local, local), :] = pieces[k][...]
    for head in range(width // HDIM):
        at = head * HDIM
        queries = rows_ref[:, at : at + HDIM]
        keys = rows_ref[:, width + at : width + at + HDIM]
        values = rows_ref[:, 2 * width + at : 2 * width + at + HDIM]
        scores = product(queries, keys, 1, 1) * ROOT
        exponent = jnp.exp(scores - jnp.max(scores, axis=1, keepdims=True))
        probs = exponent * (1.0 / jnp.sum(exponent, axis=1, keepdims=True))
        mixed = product(probs.astype(BF16), values, 1, 0).astype(BF16)
        for i, out in enumerate(outs):
            out[:, at : at + HDIM] = mixed[i * half : (i + 1) * half, :]


def join_weight(groups, count, mine, other, out):
    me = lax.axis_index("frame")
    rows = mine.shape[0] // (count // 2 * groups)
    width = rows * count
    for i, n in enumerate(order_of(count)[: count // 2]):
        for k in range(groups):
            at = (i * groups + k) * rows
            for core, source in enumerate((mine, other)):
                start = pl.multiple_of(k * width + (me ^ n ^ core) * rows, rows)
                out[pl.ds(start, rows), :] = source[at : at + rows, :]


def shifted(padded, start, tile):
    for residue in range(8):
        taps = range(residue, KERNEL, 8)
        reach = 8 * (len(taps) - 1)
        rows = padded[start + 1 + residue : start + 1 + residue + tile + reach, :]
        yield taps, rows


def convolve(groups, *refs):
    count = 6 if groups == 4 else groups
    pieces = refs[:count]
    weight, taps_ref, attention, projected_ref, slope_ref = refs[count : count + 5]
    ahead = refs[count + 5 : -3]
    padded, taps, result = refs[-3:]
    me = lax.axis_index("fsdp")
    frames = attention.shape[0]
    channels = weight.shape[1]
    local = frames // groups
    padded[0:16, :] = jnp.zeros((16, LANES), F32)
    padded[frames + 16 : frames + 32, :] = jnp.zeros((16, LANES), F32)
    if groups == 4:
        half, depth = pieces[0].shape
        for k, i, source, at in places(pieces[:3], pieces[3:], half):
            start = i * half
            attention[start : start + half, k * depth : (k + 1) * depth] = source[at : at + half, :]
    else:
        depth = pieces[0].shape[1]
        for k in range(groups):
            attention[:, k * depth : (k + 1) * depth] = pieces[k][...]
    projected_ref[...] = product(attention[...], weight[...], 1, 0).astype(BF16)

    def lane_block(c, carry):
        columns = block(c, LANES, LANES)
        padded[16 : frames + 16, :] = projected_ref[:, columns].astype(F32)
        taps[0:KERNEL, :] = taps_ref[:, block(me * (channels // LANES) + c, LANES, LANES)].astype(F32)
        for start in range(0, frames, TILE):
            conv = jnp.zeros((TILE, LANES), F32)
            for indices, rows in shifted(padded, start, TILE):
                for at, j in enumerate(indices):
                    conv += taps[j : j + 1, :] * rows[8 * at : 8 * at + TILE, :]
            gate = 1.0 / (1.0 + jnp.exp(-conv))
            own = padded[start + 16 : start + 16 + TILE, :]
            result[start : start + TILE, :] = own + conv * gate
            slope_ref[start : start + TILE, columns] = gate * (1.0 + conv * (1.0 - gate))
        for k in range(groups):
            cells = result[block(me ^ k, local, local), :].astype(BF16)
            if groups == 4:
                split_up(ahead, k, local, columns, cells)
            else:
                ahead[k][:, columns] = cells
        return carry

    lax.fori_loop(0, channels // LANES, lane_block, 0)


def convolve_back(groups, *refs):
    upstream = refs[:groups]
    projected_ref, slope_ref, weight, taps_ref, grad_ref, tap_ref = refs[groups : groups + 6]
    outs = refs[-groups - 4 : -4]
    padded, taps, above, sums = refs[-4:]
    me = lax.axis_index("fsdp")
    frames, channels = projected_ref.shape
    local = frames // groups
    depth = weight.shape[0] // groups
    padded[0:16, :] = jnp.zeros((16, LANES), F32)
    padded[frames + 16 : frames + 32, :] = jnp.zeros((16, LANES), F32)

    def lane_block(c, carry):
        columns = block(c, LANES, LANES)
        for k in range(groups):
            above[block(me ^ k, local, local), :] = upstream[k][:, columns].astype(F32)
        taps[0:KERNEL, :] = taps_ref[:, block(me * (channels // LANES) + c, LANES, LANES)].astype(F32)
        padded[16 : frames + 16, :] = (above[...] * slope_ref[:, columns]).astype(BF16).astype(F32)
        sums[...] = jnp.zeros(sums.shape, F32)
        for start in range(0, frames, TILE):
            total = above[start : start + TILE, :]
            own = projected_ref[start : start + TILE, columns].astype(F32)
            for indices, rows in shifted(padded, start, TILE):
                for at, j in enumerate(indices):
                    part = rows[8 * at : 8 * at + TILE, :]
                    tap = KERNEL - 1 - j
                    total += taps[tap : tap + 1, :] * part
                    terms = own * part
                    sums[8 * tap : 8 * tap + 8, :] += tree_sum(
                        [terms[8 * i : 8 * i + 8, :] for i in range(TILE // 8)]
                    )
            grad_ref[start : start + TILE, columns] = total.astype(BF16)
        tap_ref[:, columns] = jnp.sum(sums[...].reshape(TAPS, 8, LANES), axis=1)
        return carry

    lax.fori_loop(0, channels // LANES, lane_block, 0)
    grads = grad_ref[...]
    for k in range(groups):
        terms = product(grads, weight[k * depth : (k + 1) * depth, :], 1, 1).astype(BF16)
        if groups == 4:
            half = frames // 2
            top, end = outs[k % 2], outs[2 + k // 2]
            top[k // 2 * half : (k // 2 + 1) * half, :] = terms[:half, :]
            end[k % 2 * half : (k % 2 + 1) * half, :] = terms[half:, :]
        else:
            outs[k][...] = terms


def weight_terms(groups, order, rows, *refs):
    attention, grads, tap_ref = refs[:3]
    outs = refs[3:5]
    terms = refs[5]
    me = lax.axis_index("frame")
    depth = attention.shape[1] // groups
    half = len(order) // 2
    for k in range(groups):
        terms[...] = product(attention[:, k * depth : (k + 1) * depth], grads[...], 0, 0)
        for i, n in enumerate(order):
            there = pl.ds(pl.multiple_of((me ^ n) * rows, rows), rows)
            at = TAPS + ((i % half) * groups + k) * rows
            outs[i // half][at : at + rows, :] = terms[there, :].astype(BF16)
    for out in outs:
        out[0:TAPS, :] = tap_ref[...].astype(BF16)


def plain_terms(attention, grads, out):
    out[...] = product(attention[...], grads[...], 0, 0).astype(BF16)


def add_halves(mine, other, *outs):
    height = mine.shape[0]
    total = mine[...].astype(F32) + other[0:height, :].astype(F32)
    share = (height - TAPS) // len(outs)
    for k, out in enumerate(outs):
        at = TAPS + k * share
        out[0:TAPS, :] = total[0:TAPS, :].astype(BF16)
        out[TAPS : TAPS + share, :] = total[at : at + share, :].astype(BF16)
        if out.shape[0] > TAPS + share:
            out[TAPS + share :, :] = jnp.zeros((out.shape[0] - TAPS - share, out.shape[1]), BF16)


def fold(mine, other, stays, goes):
    total = (mine[...].astype(F32) + other[...].astype(F32)).astype(BF16)
    half = stays.shape[0]
    stays[...] = total[:half, :]
    goes[...] = total[half:, :]


def weigh(rows_ref, out):
    width = rows_ref.shape[1] // 3
    for head in range(width // HDIM):
        at = head * HDIM
        queries = rows_ref[:, at : at + HDIM]
        keys = rows_ref[:, width + at : width + at + HDIM]
        scores = product(queries, keys, 1, 1) * ROOT
        exponent = jnp.exp(scores - jnp.max(scores, axis=1, keepdims=True))
        out[head] = exponent * (1.0 / jnp.sum(exponent, axis=1, keepdims=True))


def attend_back(groups, *refs):
    rows_ref, weights_ref = refs[:2]
    upstream = refs[2 : groups + 2]
    outs = refs[groups + 2 : -2]
    grads, result = refs[-2:]
    me = lax.axis_index("fsdp")
    width = upstream[0].shape[1]
    local = outs[0].shape[0]
    if groups == 4:
        half = upstream[0].shape[0]
        for i in range(2):
            total = upstream[2 * i][...].astype(F32) + upstream[2 * i + 1][...].astype(F32)
            grads[i * half : (i + 1) * half, :] = total.astype(BF16)
    else:
        grads[...] = tree_sum([ref[...].astype(F32) for ref in upstream]).astype(BF16)
    for head in range(width // HDIM):
        at = head * HDIM
        queries = rows_ref[:, at : at + HDIM]
        keys = rows_ref[:, width + at : width + at + HDIM]
        values = rows_ref[:, 2 * width + at : 2 * width + at + HDIM]
        above = grads[:, at : at + HDIM]
        weights = weights_ref[head]
        slopes = product(above, values, 1, 1)
        row_dot = jnp.sum(weights * slopes, axis=1, keepdims=True)
        grad_scores = (weights * (slopes - row_dot)).astype(BF16)
        result[:, at : at + HDIM] = (product(grad_scores, keys, 1, 0) * ROOT).astype(BF16)
        result[:, width + at : width + at + HDIM] = (
            product(grad_scores, queries, 0, 0) * ROOT
        ).astype(BF16)
        result[:, 2 * width + at : 2 * width + at + HDIM] = product(
            weights.astype(BF16), above, 0, 0
        ).astype(BF16)
    for k in range(groups):
        piece = result[block(me ^ k, local, local), :]
        if len(outs) != groups:
            split_up(outs, k, local, slice(None), piece)
        else:
            outs[k][...] = piece


def scale_sums(groups, scale, *refs):
    sums = refs[:-2]
    weight_ref, tap_ref = refs[-2:]
    me = lax.axis_index("fsdp")
    channels = sums[0].shape[1]
    for k in range(groups):
        columns = block(me ^ k, channels, LANES)
        if len(sums) == groups:
            tap_ref[:, columns] = sums[k][0:KERNEL, :].astype(F32) * scale
            weight_ref[:, columns] = sums[k][TAPS:, :].astype(F32) * scale
    if len(sums) != groups:
        ends = ((sums[0], sums[1], sums[2]), (sums[0], sums[3], sums[4]))
        for k, i, source, at in places(*ends, TAPS):
            at += TAPS if k == 0 and i else 0
            columns = block(me ^ k, channels, LANES)
            if i:
                weight_ref[:, columns] = source[at : at + TAPS, :].astype(F32) * scale
            else:
                tap_ref[:, columns] = source[at : at + KERNEL, :].astype(F32) * scale


def join_all(groups, several, *refs):
    count = 5 if groups == 4 else groups
    ahead = refs[:count]
    pieces = refs[count : count + several]
    weight_ref, tap_ref = refs[count + several : -7]
    outs = refs[-7:-1]
    sent = refs[-1]
    me = lax.axis_index("fsdp")
    copies = []

    def store(source, target):
        copy = pltpu.make_async_copy(source, target, sent.at[len(copies)])
        copy.start()
        copies.append(copy)

    local, width = pieces[0].shape
    width //= 3
    channels = ahead[0].shape[1]

    def found(arrays):
        if len(arrays) == groups:
            return [(k, 0, local, arrays[k], 0) for k in range(groups)]
        share = local // 2
        ends = ((arrays[0], arrays[1], arrays[2]), (arrays[0], arrays[3], arrays[4]))
        parts = [(k, i * share, share, x, at) for k, i, x, at in places(*ends, share) if k]
        return parts + [(0, 0, local, arrays[0], 0)]

    for k, start, size, source, first in found(ahead):
        there = outs[0].at[0, start : start + size, block(me ^ k, channels, LANES)]
        store(source.at[first : first + size], there)
    for k, start, size, source, first in found(pieces):
        columns = block(me ^ k, width, LANES)
        for at in range(3):
            part = source.at[first : first + size, at * width : (at + 1) * width]
            store(part, outs[1 + at].at[0, start : start + size, columns])
    store(weight_ref, outs[4])
    store(tap_ref, outs[5])
    for copy in copies:
        copy.wait()


def stack(*arrays, after=()):
    shape = (sum(x.shape[0] for x in arrays),) + arrays[0].shape[1:]
    return call(stack_all, [(shape, arrays[0].dtype)], *arrays, after=after)[0]


def exchange_split(sent, after=()):
    if len(sent) != 5:
        return exchange(sent)
    own, beside, across, later_across, later_beside = sent
    shape = [(beside.shape, beside.dtype)]
    beside, across = swap(beside, "fsdp", 1), swap(across, "fsdp", 2)
    (later_across,) = call(stack_parts, shape, later_across, beside, after=after)
    (later_beside,) = call(stack_parts, shape, later_beside, across, after=after)
    return [own, beside, swap(later_across, "fsdp", 2), across, swap(later_beside, "fsdp", 1)]


def gather_weight(mine, groups, count, after):
    rows, channels = mine.shape[0] // groups, mine.shape[1]
    pieces = [mine]
    for mask in reversed(masks_of(count)[1:]):
        pieces += [swap(piece, "frame", mask) for piece in pieces]
    gathered = stack(*pieces, after=after)
    other = swap(gathered, "frame", 1)
    if rows % 16 == 0:
        return call(
            functools.partial(join_weight, groups, count),
            [((groups * count * rows, channels), BF16)],
            gathered,
            other,
        )[0]
    me = lax.axis_index("frame")
    order = order_of(count)
    place = jnp.array([order.index(n) for n in range(count)])
    both = jnp.concatenate([gathered, other], axis=0).reshape(count, groups, rows, channels)
    ordered = jnp.take(both, place[me ^ jnp.arange(count)], axis=0)
    return ordered.transpose(1, 0, 2, 3).reshape(groups * count * rows, channels)


def weight_halves(attention, grads, tap_terms, groups, count, rows, after):
    channels = grads.shape[1]
    depth = attention.shape[1] // groups
    share = count // 2 * groups * rows
    bits = count.bit_length() - 1
    order = [sum((i >> b & 1) << (bits - 1 - b) for b in range(bits)) for i in range(count)]
    if rows % 16 == 0:
        halves = call(
            functools.partial(weight_terms, groups, order, rows),
            [((TAPS + share, channels), BF16)] * 2,
            attention,
            grads,
            tap_terms,
            scratch=[pltpu.VMEM((depth, channels), F32)],
            after=after,
        )
    else:
        (terms,) = call(plain_terms, [((groups * depth, channels), BF16)], attention, grads)
        me = lax.axis_index("frame")
        terms = terms.reshape(groups, count, rows, channels)
        terms = jnp.take(terms, me ^ jnp.array(order), axis=1)
        terms = terms.transpose(1, 0, 2, 3).reshape(2, share, channels)
        halves = [jnp.concatenate([tap_terms.astype(BF16), x], axis=0) for x in terms]
    return halves


def add_up(halves, mask, spare):
    mine, other = halves
    height = TAPS + (mine.shape[0] - TAPS) // 2
    shapes = [((height, mine.shape[1]), BF16), ((height + spare, mine.shape[1]), BF16)]
    return call(add_halves, shapes, mine, swap(other, "frame", mask))


def shards(queries, key_rows, value_rows, out_weight, conv_weight, grad_out):
    local, inner = queries.shape[1:]
    rows, model = out_weight.shape
    groups = lax.axis_size("fsdp")
    count = lax.axis_size("frame")
    frames = local * groups
    width = inner // groups
    channels = model // groups
    scale = 1.0 / math.sqrt(frames * count)
    conv_flops = CONV_COST * KERNEL * frames * channels

    folded = groups == 4
    def split(size):
        shape, small = ((local, size), BF16), ((local // 2, size), BF16)
        return [shape, shape, shape, small, small] if folded else [shape] * groups

    merged = folded and rows % 32 == 0 and channels == 2 * width and local % (4 * FOLD) == 0
    shape = (3 * local // 4 + rows // 2, 4 * width) if merged else (local, 3 * width)
    whole = (groups * rows, channels)
    sent = call(
        functools.partial(pack_rows, groups),
        [(shape, BF16)] * groups
        + ([] if merged else [((rows, channels), BF16)] * groups),
        queries[0],
        key_rows[0],
        value_rows[0],
        out_weight,
        near=False,
        limit=PACK_LIMIT,
        pinned=True,
        scratch=[pltpu.VMEM((local, inner), BF16)] * 3
        + [pltpu.VMEM((rows, model), BF16), pltpu.SemaphoreType.DMA((4,))],
    )
    half = ((frames // 2, width), BF16)
    held, *own = call(
        functools.partial(attend, groups),
        [((frames, 3 * width), BF16)]
        + ([half, half] if folded else [((frames, width), BF16)])
        + ([(whole, BF16)] if merged else []),
        *exchange(sent[:groups]),
        flops=ATTEND_COST * frames * frames * width,
    )
    gathered = own.pop() if merged else stack(*exchange(sent[groups:]))
    if folded:
        top, end = own
        beside, across = swap(top, "fsdp", 1), swap(end, "fsdp", 2)
        step = [beside, across]
        attention = [top, beside, swap(stack(top, beside), "fsdp", 2)]
        attention += [end, across, swap(stack(end, across), "fsdp", 1)]
        last = [attention[2], attention[5]]
    else:
        attention = exchange(own * groups)
        step = last = attention[1:2]
    sent = call(
        functools.partial(pack_columns, groups),
        [((local, channels), BF16)] * groups,
        grad_out[0],
        after=step,
    )
    upstream = exchange(sent)
    weight = gather_weight(gathered, groups, count, last + upstream[1:3])

    outs = call(
        functools.partial(convolve, groups),
        [((frames, inner), BF16), ((frames, channels), BF16), ((frames, channels), F32)]
        + split(channels),
        *attention,
        weight,
        conv_weight,
        scratch=[
            pltpu.VMEM((frames + 32, LANES), F32),
            pltpu.VMEM((TAPS, LANES), F32),
            pltpu.VMEM((frames, LANES), F32),
        ],
        flops=conv_flops,
    )
    whole, projected, slope = outs[:3]
    (weights,) = call(weigh, [((width // HDIM, frames, frames), F32)], held)
    ahead = exchange_split(outs[3:], after=[weights])

    outs = call(
        functools.partial(convolve_back, groups),
        [((frames, channels), BF16), ((TAPS, channels), F32)] + [((frames, width), BF16)] * groups,
        *upstream,
        projected,
        slope,
        weight,
        conv_weight,
        scratch=[
            pltpu.VMEM((frames + 32, LANES), F32),
            pltpu.VMEM((TAPS, LANES), F32),
            pltpu.VMEM((frames, LANES), F32),
            pltpu.VMEM((8 * TAPS, LANES), F32),
        ],
        flops=conv_flops * 3 // 2,
    )
    grads, tap_terms = outs[:2]
    if folded:
        stay_top, go_top, stay_end, go_end = outs[2:]
        shapes = [((frames // 2, width), BF16)] * 2
        stay_top, go_top = call(fold, shapes, stay_top, swap(go_top, "fsdp", 1))
        stay_end, go_end = call(fold, shapes, stay_end, swap(go_end, "fsdp", 2))
        above = [stay_top, swap(go_top, "fsdp", 2), stay_end, swap(go_end, "fsdp", 1)]
    else:
        above = exchange(outs[2:])
    halves = weight_halves(whole, grads, tap_terms, groups, count, rows, ahead[1:4:2])
    masks = masks_of(count)
    for mask in masks[:-1]:
        halves = add_up(halves, mask, PAD if mask == masks[-2] and rows % 16 == 0 else 0)
    sent = call(
        functools.partial(attend_back, groups),
        split(3 * width) if SPLIT_BACK else [((local, 3 * width), BF16)] * groups,
        held,
        weights,
        *above,
        scratch=[pltpu.VMEM((frames, width), BF16), pltpu.VMEM((frames, 3 * width), BF16)],
        flops=BACK_COST * frames * frames * width,
        after=[halves[1], *(ahead[2:5:2] if folded else ())],
    )
    pieces = exchange_split(sent)
    shapes = [((TAPS + rows, channels), BF16)] * groups
    sums = list(call(add_halves, shapes, halves[0], swap(halves[1], "frame", masks[-1])))
    sums[-1] = stack(sums[-1], after=pieces[2:3])
    sums = exchange(sums)
    shapes = [((rows, model), F32), ((KERNEL, model), F32)]
    sums = call(functools.partial(scale_sums, groups, scale), shapes, *sums)
    return tuple(
        call(
            functools.partial(join_all, groups, len(pieces)),
            [((1, local, model), BF16)]
            + [((1, local, inner), BF16)] * 3
            + [((rows, model), F32), ((KERNEL, model), F32)],
            *ahead,
            *pieces,
            *sums,
            stored=True,
            scratch=[pltpu.SemaphoreType.DMA((8 * groups + 2,))],
        )
    )


def solution(mesh):
    return jax.shard_map(
        shards,
        mesh=mesh,
        in_specs=(
            P("frame", "fsdp", None),
            P("frame", "fsdp", None),
            P("frame", "fsdp", None),
            P(("fsdp", "frame"), None),
            P(),
            P("frame", "fsdp", None),
        ),
        out_specs=(
            P("frame", "fsdp", None),
            P("frame", "fsdp", None),
            P("frame", "fsdp", None),
            P("frame", "fsdp", None),
            P(("fsdp", "frame"), None),
            P(),
        ),
        check_vma=False,
    )
```

```python
import functools
import math

import jax
import jax.numpy as jnp
from jax import lax
from jax.experimental import pallas as pl
from jax.experimental.pallas import tpu as pltpu
from jax.sharding import PartitionSpec as P

HDIM = 128
KERNEL = 31
LANES = 128
TILE = 64
BACK_TILE = 32
TAPS = 32
FOLD = 32
CONV_COST = 600
ATTEND_COST = 24
BACK_COST = 48
SPLIT_BACK = False
PAD = 48
PACK_LIMIT = 60
F32 = jnp.float32
BF16 = jnp.bfloat16
ROOT = 1.0 / math.sqrt(HDIM)


def swap(cells, axis, mask):
    count = lax.axis_size(axis)
    return lax.ppermute(cells, axis, [(i, i ^ mask) for i in range(count)])


def exchange(sent):
    return [sent[0]] + [swap(sent[k], "fsdp", k) for k in range(1, len(sent))]


def masks_of(count):
    return [1 << i for i in range(count.bit_length() - 1)]


def order_of(count):
    order = [0]
    for mask in reversed(masks_of(count)):
        order += [n ^ mask for n in order]
    return order


def call(body, outs, *operands, scratch=(), flops=0, near=True, stored=0, after=(), limit=40, pinned=False):
    vmem = pl.BlockSpec(memory_space=pltpu.VMEM)
    hbm = pl.BlockSpec(memory_space=pltpu.HBM)
    count = len(operands)
    moved = sum(x.size * x.dtype.itemsize for x in operands)
    moved += sum(math.prod(s) * jnp.dtype(t).itemsize for s, t in outs)
    return pl.pallas_call(
        lambda *refs: body(*refs[:count], *refs[count + len(after) :]),
        out_shape=[(pltpu.VMEM if pinned else jax.ShapeDtypeStruct)(s, t) for s, t in outs],
        in_specs=[vmem if near else hbm] * count + [pl.BlockSpec(memory_space=pl.ANY)] * len(after),
        out_specs=[hbm if i < stored else vmem for i in range(len(outs))],
        scratch_shapes=list(scratch),
        cost_estimate=pl.CostEstimate(flops=flops, bytes_accessed=moved, transcendentals=0),
        compiler_params=pltpu.CompilerParams(vmem_limit_bytes=limit * 1024 * 1024),
    )(*operands, *after)


def block(index, size, unit):
    return pl.ds(pl.multiple_of(index * size, unit), size)


def product(left, right, left_dim, right_dim):
    return lax.dot_general(
        left, right, (((left_dim,), (right_dim,)), ((), ())), preferred_element_type=F32
    )


def tree_sum(terms):
    while len(terms) > 1:
        terms = [terms[i] + terms[i + 1] for i in range(0, len(terms), 2)]
    return terms[0]


def places(top, end, rows):
    return (
        (0, 0, top[0], 0),
        (1, 0, top[1], 0),
        (2, 0, top[2], 0),
        (3, 0, top[2], rows),
        (0, 1, end[0], 0),
        (2, 1, end[1], 0),
        (1, 1, end[2], 0),
        (3, 1, end[2], rows),
    )


def split_up(outs, k, rows, columns, cells):
    own, beside, across, later_across, later_beside = outs
    half = rows // 2
    top, end = cells[:half, :], cells[half:, :]
    if k == 0:
        own[:, columns] = cells
    elif k == 1:
        beside[:half, columns] = top
        later_beside[:, columns] = end
    elif k == 2:
        later_across[:, columns] = top
        across[:half, columns] = end
    else:
        beside[half:, columns] = top
        across[half:, columns] = end


def pack_rows(groups, *refs):
    sources = refs[:4]
    outs = refs[4 : 4 + groups]
    weight_outs = refs[4 + groups : -5]
    held = refs[-5:-1]
    arrived = refs[-1]
    copies = [pltpu.make_async_copy(sources[i], held[i], arrived.at[i]) for i in range(4)]
    for copy in copies:
        copy.start()
    for copy in copies:
        copy.wait()
    me = lax.axis_index("fsdp")
    local, inner = held[0].shape
    rows, model = held[3].shape
    width, channels = inner // groups, model // groups
    for k in range(groups):
        columns = block(me ^ k, width, LANES)
        cells = held[3][:, block(me ^ k, channels, LANES)]
        if weight_outs:
            weight_outs[k][...] = cells
            for at in range(3):
                outs[k][:, at * width : (at + 1) * width] = held[at][:, columns]
        else:
            for at, start, there, column in folds(local, width):
                outs[k][there : there + FOLD, column : column + width] = held[at][start : start + FOLD, columns]
            below = outs[k].shape[0] - rows // 2
            outs[k][below:, :channels] = cells[: rows // 2, :]
            outs[k][below:, channels:] = cells[rows // 2 :, :]


def folds(local, width):
    tall = 3 * local // 4
    for start in range(0, 3 * local, FOLD):
        yield start // local, start % local, start % tall, start // tall * width


def pack_columns(groups, *refs):
    source = refs[0]
    me = lax.axis_index("fsdp")
    width = source.shape[1] // groups
    for k in range(groups):
        refs[1 + k][...] = source[:, block(me ^ k, width, LANES)]


def stack_parts(mine, other, out):
    rows = mine.shape[0]
    out[:rows, :] = mine[...]
    out[rows:, :] = other[rows:, :]


def stack_all(*refs):
    at = 0
    for source in refs[:-1]:
        refs[-1][at : at + source.shape[0], :] = source[...]
        at += source.shape[0]


def attend(groups, *refs):
    pieces = refs[:groups]
    rows_ref = refs[groups]
    outs = refs[groups + 1 : 3 + groups if groups == 4 else 2 + groups]
    weight_refs = refs[groups + 1 + len(outs) :]
    me = lax.axis_index("fsdp")
    local = rows_ref.shape[0] // groups
    half, width = outs[0].shape
    for k in range(groups):
        if weight_refs:
            for at, start, there, column in folds(local, width):
                first = pl.multiple_of((me ^ k) * local + start, FOLD)
                cells = pieces[k][there : there + FOLD, column : column + width]
                rows_ref[pl.ds(first, FOLD), at * width : (at + 1) * width] = cells
            channels = weight_refs[0].shape[1]
            rows = weight_refs[0].shape[0] // groups
            at, share = k * rows, rows // 2
            below = pieces[k].shape[0] - share
            weight_refs[0][at : at + share, :] = pieces[k][below:, :channels]
            weight_refs[0][at + share : at + rows, :] = pieces[k][below:, channels:]
        else:
            rows_ref[block(me ^ k, local, local), :] = pieces[k][...]
    for head in range(width // HDIM):
        at = head * HDIM
        queries = rows_ref[:, at : at + HDIM]
        keys = rows_ref[:, width + at : width + at + HDIM]
        values = rows_ref[:, 2 * width + at : 2 * width + at + HDIM]
        scores = product(queries, keys, 1, 1) * ROOT
        exponent = jnp.exp(scores - jnp.max(scores, axis=1, keepdims=True))
        probs = exponent * (1.0 / jnp.sum(exponent, axis=1, keepdims=True))
        mixed = product(probs.astype(BF16), values, 1, 0).astype(BF16)
        for i, out in enumerate(outs):
            out[:, at : at + HDIM] = mixed[i * half : (i + 1) * half, :]


def join_weight(groups, count, mine, other, out):
    me = lax.axis_index("frame")
    rows = mine.shape[0] // (count // 2 * groups)
    width = rows * count
    for i, n in enumerate(order_of(count)[: count // 2]):
        for k in range(groups):
            at = (i * groups + k) * rows
            for core, source in enumerate((mine, other)):
                start = pl.multiple_of(k * width + (me ^ n ^ core) * rows, rows)
                out[pl.ds(start, rows), :] = source[at : at + rows, :]


def shifted(padded, start, tile):
    for residue in range(8):
        taps = range(residue, KERNEL, 8)
        reach = 8 * (len(taps) - 1)
        rows = padded[start + 1 + residue : start + 1 + residue + tile + reach, :]
        yield taps, rows


def convolve(groups, *refs):
    count = 6 if groups == 4 else groups
    pieces = refs[:count]
    weight, taps_ref, attention, projected_ref, slope_ref = refs[count : count + 5]
    ahead = refs[count + 5 : -3]
    padded, taps, result = refs[-3:]
    me = lax.axis_index("fsdp")
    frames = attention.shape[0]
    channels = weight.shape[1]
    local = frames // groups
    padded[0:16, :] = jnp.zeros((16, LANES), F32)
    padded[frames + 16 : frames + 32, :] = jnp.zeros((16, LANES), F32)
    if groups == 4:
        half, depth = pieces[0].shape
        for k, i, source, at in places(pieces[:3], pieces[3:], half):
            start = i * half
            attention[start : start + half, k * depth : (k + 1) * depth] = source[at : at + half, :]
    else:
        depth = pieces[0].shape[1]
        for k in range(groups):
            attention[:, k * depth : (k + 1) * depth] = pieces[k][...]
    projected_ref[...] = product(attention[...], weight[...], 1, 0).astype(BF16)

    def lane_block(c, carry):
        columns = block(c, LANES, LANES)
        padded[16 : frames + 16, :] = projected_ref[:, columns].astype(F32)
        taps[0:KERNEL, :] = taps_ref[:, block(me * (channels // LANES) + c, LANES, LANES)].astype(F32)
        for start in range(0, frames, TILE):
            conv = jnp.zeros((TILE, LANES), F32)
            for indices, rows in shifted(padded, start, TILE):
                for at, j in enumerate(indices):
                    conv += taps[j : j + 1, :] * rows[8 * at : 8 * at + TILE, :]
            gate = 1.0 / (1.0 + jnp.exp(-conv))
            own = padded[start + 16 : start + 16 + TILE, :]
            result[start : start + TILE, :] = own + conv * gate
            slope_ref[start : start + TILE, columns] = gate * (1.0 + conv * (1.0 - gate))
        for k in range(groups):
            cells = result[block(me ^ k, local, local), :].astype(BF16)
            if groups == 4:
                split_up(ahead, k, local, columns, cells)
            else:
                ahead[k][:, columns] = cells
        return carry

    lax.fori_loop(0, channels // LANES, lane_block, 0)


def convolve_back(groups, *refs):
    upstream = refs[:groups]
    projected_ref, slope_ref, weight, taps_ref, grad_ref, tap_ref = refs[groups : groups + 6]
    outs = refs[-groups - 4 : -4]
    padded, taps, above, sums = refs[-4:]
    me = lax.axis_index("fsdp")
    frames, channels = projected_ref.shape
    local = frames // groups
    depth = weight.shape[0] // groups
    padded[0:16, :] = jnp.zeros((16, LANES), F32)
    padded[frames + 16 : frames + 32, :] = jnp.zeros((16, LANES), F32)

    def lane_block(c, carry):
        columns = block(c, LANES, LANES)
        for k in range(groups):
            above[block(me ^ k, local, local), :] = upstream[k][:, columns].astype(F32)
        taps[0:KERNEL, :] = taps_ref[:, block(me * (channels // LANES) + c, LANES, LANES)].astype(F32)
        padded[16 : frames + 16, :] = (above[...] * slope_ref[:, columns]).astype(BF16).astype(F32)
        sums[...] = jnp.zeros(sums.shape, F32)
        for start in range(0, frames, BACK_TILE):
            total = above[start : start + BACK_TILE, :]
            own = projected_ref[start : start + BACK_TILE, columns].astype(F32)
            for indices, rows in shifted(padded, start, BACK_TILE):
                for at, j in enumerate(indices):
                    part = rows[8 * at : 8 * at + BACK_TILE, :]
                    tap = KERNEL - 1 - j
                    total += taps[tap : tap + 1, :] * part
                    terms = own * part
                    sums[8 * tap : 8 * tap + 8, :] += tree_sum(
                        [terms[8 * i : 8 * i + 8, :] for i in range(BACK_TILE // 8)]
                    )
            grad_ref[start : start + BACK_TILE, columns] = total.astype(BF16)
        tap_ref[:, columns] = jnp.sum(sums[...].reshape(TAPS, 8, LANES), axis=1)
        return carry

    lax.fori_loop(0, channels // LANES, lane_block, 0)
    grads = grad_ref[...]
    for k in range(groups):
        terms = product(grads, weight[k * depth : (k + 1) * depth, :], 1, 1).astype(BF16)
        if groups == 4:
            half = frames // 2
            top, end = outs[k % 2], outs[2 + k // 2]
            top[k // 2 * half : (k // 2 + 1) * half, :] = terms[:half, :]
            end[k % 2 * half : (k % 2 + 1) * half, :] = terms[half:, :]
        else:
            outs[k][...] = terms


def weight_terms(groups, order, rows, *refs):
    attention, grads, tap_ref = refs[:3]
    outs = refs[3:5]
    terms = refs[5]
    me = lax.axis_index("frame")
    depth = attention.shape[1] // groups
    half = len(order) // 2
    for k in range(groups):
        cells = product(attention[:, k * depth : (k + 1) * depth], grads[...], 0, 0)
        terms[...] = cells.astype(BF16)
        for i, n in enumerate(order):
            there = pl.ds(pl.multiple_of((me ^ n) * rows, rows), rows)
            at = TAPS + ((i % half) * groups + k) * rows
            outs[i // half][at : at + rows, :] = terms[there, :]
    for out in outs:
        out[0:TAPS, :] = tap_ref[...].astype(BF16)


def plain_terms(attention, grads, out):
    out[...] = product(attention[...], grads[...], 0, 0).astype(BF16)


def add_halves(mine, other, *outs):
    height = mine.shape[0]
    total = mine[...].astype(F32) + other[0:height, :].astype(F32)
    share = (height - TAPS) // len(outs)
    for k, out in enumerate(outs):
        at = TAPS + k * share
        out[0:TAPS, :] = total[0:TAPS, :].astype(BF16)
        out[TAPS : TAPS + share, :] = total[at : at + share, :].astype(BF16)
        if out.shape[0] > TAPS + share:
            out[TAPS + share :, :] = jnp.zeros((out.shape[0] - TAPS - share, out.shape[1]), BF16)


def fold(mine, other, stays, goes):
    total = (mine[...].astype(F32) + other[...].astype(F32)).astype(BF16)
    half = stays.shape[0]
    stays[...] = total[:half, :]
    goes[...] = total[half:, :]


def weigh(rows_ref, out):
    width = rows_ref.shape[1] // 3
    for head in range(width // HDIM):
        at = head * HDIM
        queries = rows_ref[:, at : at + HDIM]
        keys = rows_ref[:, width + at : width + at + HDIM]
        scores = product(queries, keys, 1, 1) * ROOT
        exponent = jnp.exp(scores - jnp.max(scores, axis=1, keepdims=True))
        out[head] = exponent * (1.0 / jnp.sum(exponent, axis=1, keepdims=True))


def attend_back(groups, *refs):
    rows_ref, weights_ref = refs[:2]
    upstream = refs[2 : groups + 2]
    outs = refs[groups + 2 : -2]
    grads, result = refs[-2:]
    me = lax.axis_index("fsdp")
    width = upstream[0].shape[1]
    local = outs[0].shape[0]
    if groups == 4:
        half = upstream[0].shape[0]
        for i in range(2):
            total = upstream[2 * i][...].astype(F32) + upstream[2 * i + 1][...].astype(F32)
            grads[i * half : (i + 1) * half, :] = total.astype(BF16)
    else:
        grads[...] = tree_sum([ref[...].astype(F32) for ref in upstream]).astype(BF16)
    for head in range(width // HDIM):
        at = head * HDIM
        queries = rows_ref[:, at : at + HDIM]
        keys = rows_ref[:, width + at : width + at + HDIM]
        values = rows_ref[:, 2 * width + at : 2 * width + at + HDIM]
        above = grads[:, at : at + HDIM]
        weights = weights_ref[head]
        slopes = product(above, values, 1, 1)
        row_dot = jnp.sum(weights * slopes, axis=1, keepdims=True)
        grad_scores = (weights * (slopes - row_dot)).astype(BF16)
        result[:, at : at + HDIM] = (product(grad_scores, keys, 1, 0) * ROOT).astype(BF16)
        result[:, width + at : width + at + HDIM] = (
            product(grad_scores, queries, 0, 0) * ROOT
        ).astype(BF16)
        result[:, 2 * width + at : 2 * width + at + HDIM] = product(
            weights.astype(BF16), above, 0, 0
        ).astype(BF16)
    for k in range(groups):
        piece = result[block(me ^ k, local, local), :]
        if len(outs) != groups:
            split_up(outs, k, local, slice(None), piece)
        else:
            outs[k][...] = piece


def scale_sums(groups, scale, *refs):
    sums = refs[:-2]
    weight_ref, tap_ref = refs[-2:]
    me = lax.axis_index("fsdp")
    channels = sums[0].shape[1]
    for k in range(groups):
        columns = block(me ^ k, channels, LANES)
        if len(sums) == groups:
            tap_ref[:, columns] = sums[k][0:KERNEL, :].astype(F32) * scale
            weight_ref[:, columns] = sums[k][TAPS:, :].astype(F32) * scale
    if len(sums) != groups:
        ends = ((sums[0], sums[1], sums[2]), (sums[0], sums[3], sums[4]))
        for k, i, source, at in places(*ends, TAPS):
            at += TAPS if k == 0 and i else 0
            columns = block(me ^ k, channels, LANES)
            if i:
                weight_ref[:, columns] = source[at : at + TAPS, :].astype(F32) * scale
            else:
                tap_ref[:, columns] = source[at : at + KERNEL, :].astype(F32) * scale


def join_ahead(groups, *refs):
    ahead = refs[:-3]
    out, written, sent = refs[-3:]
    me = lax.axis_index("fsdp")
    local, channels = ahead[0].shape
    copies = []
    for i, (k, start, size, source, first) in enumerate(found(groups, local, ahead)):
        there = out.at[0, start : start + size, block(me ^ k, channels, LANES)]
        copies.append(pltpu.make_async_copy(source.at[first : first + size], there, sent.at[i]))
        copies[-1].start()
    for copy in copies:
        copy.wait()
    written[...] = jnp.zeros(written.shape, F32)


def found(groups, local, arrays):
    if len(arrays) == groups:
        return [(k, 0, local, arrays[k], 0) for k in range(groups)]
    share = local // 2
    ends = ((arrays[0], arrays[1], arrays[2]), (arrays[0], arrays[3], arrays[4]))
    parts = [(k, i * share, share, x, at) for k, i, x, at in places(*ends, share) if k]
    return parts + [(0, 0, local, arrays[0], 0)]


def join_all(groups, several, *refs):
    pieces = refs[:several]
    weight_ref, tap_ref = refs[several : several + 2]
    outs = refs[several + 2 : -1]
    sent = refs[-1]
    me = lax.axis_index("fsdp")
    copies = []

    def store(source, target):
        copy = pltpu.make_async_copy(source, target, sent.at[len(copies)])
        copy.start()
        copies.append(copy)

    local, width = pieces[0].shape
    width //= 3
    for k, start, size, source, first in found(groups, local, pieces):
        columns = block(me ^ k, width, LANES)
        for at in range(3):
            part = source.at[first : first + size, at * width : (at + 1) * width]
            store(part, outs[at].at[0, start : start + size, columns])
    store(weight_ref, outs[3])
    store(tap_ref, outs[4])
    for copy in copies:
        copy.wait()


def stack(*arrays, after=()):
    shape = (sum(x.shape[0] for x in arrays),) + arrays[0].shape[1:]
    return call(stack_all, [(shape, arrays[0].dtype)], *arrays, after=after)[0]


def exchange_split(sent, after=()):
    if len(sent) != 5:
        return exchange(sent)
    own, beside, across, later_across, later_beside = sent
    shape = [(beside.shape, beside.dtype)]
    beside, across = swap(beside, "fsdp", 1), swap(across, "fsdp", 2)
    (later_across,) = call(stack_parts, shape, later_across, beside, after=after)
    (later_beside,) = call(stack_parts, shape, later_beside, across, after=after)
    return [own, beside, swap(later_across, "fsdp", 2), across, swap(later_beside, "fsdp", 1)]


def gather_weight(mine, groups, count, after):
    rows, channels = mine.shape[0] // groups, mine.shape[1]
    pieces = [mine]
    for mask in reversed(masks_of(count)[1:]):
        pieces += [swap(piece, "frame", mask) for piece in pieces]
    gathered = stack(*pieces, after=after)
    other = swap(gathered, "frame", 1)
    if rows % 16 == 0:
        return call(
            functools.partial(join_weight, groups, count),
            [((groups * count * rows, channels), BF16)],
            gathered,
            other,
        )[0]
    me = lax.axis_index("frame")
    order = order_of(count)
    place = jnp.array([order.index(n) for n in range(count)])
    both = jnp.concatenate([gathered, other], axis=0).reshape(count, groups, rows, channels)
    ordered = jnp.take(both, place[me ^ jnp.arange(count)], axis=0)
    return ordered.transpose(1, 0, 2, 3).reshape(groups * count * rows, channels)


def weight_halves(attention, grads, tap_terms, groups, count, rows, after):
    channels = grads.shape[1]
    depth = attention.shape[1] // groups
    share = count // 2 * groups * rows
    bits = count.bit_length() - 1
    order = [sum((i >> b & 1) << (bits - 1 - b) for b in range(bits)) for i in range(count)]
    if rows % 16 == 0:
        halves = call(
            functools.partial(weight_terms, groups, order, rows),
            [((TAPS + share, channels), BF16)] * 2,
            attention,
            grads,
            tap_terms,
            scratch=[pltpu.VMEM((depth, channels), BF16)],
            after=after,
        )
    else:
        (terms,) = call(plain_terms, [((groups * depth, channels), BF16)], attention, grads)
        me = lax.axis_index("frame")
        terms = terms.reshape(groups, count, rows, channels)
        terms = jnp.take(terms, me ^ jnp.array(order), axis=1)
        terms = terms.transpose(1, 0, 2, 3).reshape(2, share, channels)
        halves = [jnp.concatenate([tap_terms.astype(BF16), x], axis=0) for x in terms]
    return halves


def add_up(halves, mask, spare):
    mine, other = halves
    height = TAPS + (mine.shape[0] - TAPS) // 2
    shapes = [((height, mine.shape[1]), BF16), ((height + spare, mine.shape[1]), BF16)]
    return call(add_halves, shapes, mine, swap(other, "frame", mask))


def shards(queries, key_rows, value_rows, out_weight, conv_weight, grad_out):
    local, inner = queries.shape[1:]
    rows, model = out_weight.shape
    groups = lax.axis_size("fsdp")
    count = lax.axis_size("frame")
    frames = local * groups
    width = inner // groups
    channels = model // groups
    scale = 1.0 / math.sqrt(frames * count)
    conv_flops = CONV_COST * KERNEL * frames * channels

    folded = groups == 4
    def split(size):
        shape, small = ((local, size), BF16), ((local // 2, size), BF16)
        return [shape, shape, shape, small, small] if folded else [shape] * groups

    merged = folded and rows % 32 == 0 and channels == 2 * width and local % (4 * FOLD) == 0
    shape = (3 * local // 4 + rows // 2, 4 * width) if merged else (local, 3 * width)
    whole = (groups * rows, channels)
    sent = call(
        functools.partial(pack_rows, groups),
        [(shape, BF16)] * groups
        + ([] if merged else [((rows, channels), BF16)] * groups),
        queries[0],
        key_rows[0],
        value_rows[0],
        out_weight,
        near=False,
        limit=PACK_LIMIT,
        pinned=True,
        scratch=[pltpu.VMEM((local, inner), BF16)] * 3
        + [pltpu.VMEM((rows, model), BF16), pltpu.SemaphoreType.DMA((4,))],
    )
    half = ((frames // 2, width), BF16)
    held, *own = call(
        functools.partial(attend, groups),
        [((frames, 3 * width), BF16)]
        + ([half, half] if folded else [((frames, width), BF16)])
        + ([(whole, BF16)] if merged else []),
        *exchange(sent[:groups]),
        flops=ATTEND_COST * frames * frames * width,
    )
    gathered = own.pop() if merged else stack(*exchange(sent[groups:]))
    if folded:
        top, end = own
        beside, across = swap(top, "fsdp", 1), swap(end, "fsdp", 2)
        step = [beside, across]
        attention = [top, beside, swap(stack(top, beside), "fsdp", 2)]
        attention += [end, across, swap(stack(end, across), "fsdp", 1)]
        last = [attention[2], attention[5]]
    else:
        attention = exchange(own * groups)
        step = last = attention[1:2]
    sent = call(
        functools.partial(pack_columns, groups),
        [((local, channels), BF16)] * groups,
        grad_out[0],
        after=step,
    )
    upstream = exchange(sent)
    weight = gather_weight(gathered, groups, count, last + upstream[1:3])

    outs = call(
        functools.partial(convolve, groups),
        [((frames, inner), BF16), ((frames, channels), BF16), ((frames, channels), F32)]
        + split(channels),
        *attention,
        weight,
        conv_weight,
        scratch=[
            pltpu.VMEM((frames + 32, LANES), F32),
            pltpu.VMEM((TAPS, LANES), F32),
            pltpu.VMEM((frames, LANES), F32),
        ],
        flops=conv_flops,
    )
    whole, projected, slope = outs[:3]
    (weights,) = call(weigh, [((width // HDIM, frames, frames), F32)], held)
    ahead = exchange_split(outs[3:], after=[weights])

    outs = call(
        functools.partial(convolve_back, groups),
        [((frames, channels), BF16), ((TAPS, channels), F32)] + [((frames, width), BF16)] * groups,
        *upstream,
        projected,
        slope,
        weight,
        conv_weight,
        scratch=[
            pltpu.VMEM((frames + 32, LANES), F32),
            pltpu.VMEM((TAPS, LANES), F32),
            pltpu.VMEM((frames, LANES), F32),
            pltpu.VMEM((8 * TAPS, LANES), F32),
        ],
        flops=conv_flops * 3 // 2,
    )
    grads, tap_terms = outs[:2]
    if folded:
        stay_top, go_top, stay_end, go_end = outs[2:]
        shapes = [((frames // 2, width), BF16)] * 2
        stay_top, go_top = call(fold, shapes, stay_top, swap(go_top, "fsdp", 1))
        stay_end, go_end = call(fold, shapes, stay_end, swap(go_end, "fsdp", 2))
        above = [stay_top, swap(go_top, "fsdp", 2), stay_end, swap(go_end, "fsdp", 1)]
    else:
        above = exchange(outs[2:])
    halves = weight_halves(whole, grads, tap_terms, groups, count, rows, ahead[1:4:2])
    masks = masks_of(count)
    for mask in masks[:-1]:
        halves = add_up(halves, mask, PAD if mask == masks[-2] and rows % 16 == 0 else 0)
    sent = call(
        functools.partial(attend_back, groups),
        split(3 * width) if SPLIT_BACK else [((local, 3 * width), BF16)] * groups,
        held,
        weights,
        *above,
        scratch=[pltpu.VMEM((frames, width), BF16), pltpu.VMEM((frames, 3 * width), BF16)],
        flops=BACK_COST * frames * frames * width,
        after=[halves[1], *(ahead[2:5:2] if folded else ())],
    )
    pieces = exchange_split(sent)
    block_out, written = call(
        functools.partial(join_ahead, groups),
        [((1, local, model), BF16), ((8, LANES), F32)],
        *ahead,
        stored=1,
        scratch=[pltpu.SemaphoreType.DMA((2 * groups,))],
    )
    shapes = [((TAPS + rows, channels), BF16)] * groups
    other = swap(halves[1], "frame", masks[-1])
    sums = list(call(add_halves, shapes, halves[0], other, after=[written]))
    sums[-1] = stack(sums[-1], after=pieces[2:3])
    sums = exchange(sums)
    shapes = [((rows, model), F32), ((KERNEL, model), F32)]
    sums = call(functools.partial(scale_sums, groups, scale), shapes, *sums)
    joined = call(
        functools.partial(join_all, groups, len(pieces)),
        [((1, local, inner), BF16)] * 3 + [((rows, model), F32), ((KERNEL, model), F32)],
        *pieces,
        *sums,
        stored=5,
        scratch=[pltpu.SemaphoreType.DMA((8 * groups + 2,))],
    )
    return (block_out, *joined)


def solution(mesh):
    return jax.shard_map(
        shards,
        mesh=mesh,
        in_specs=(
            P("frame", "fsdp", None),
            P("frame", "fsdp", None),
            P("frame", "fsdp", None),
            P(("fsdp", "frame"), None),
            P(),
            P("frame", "fsdp", None),
        ),
        out_specs=(
            P("frame", "fsdp", None),
            P("frame", "fsdp", None),
            P("frame", "fsdp", None),
            P("frame", "fsdp", None),
            P(("fsdp", "frame"), None),
            P(),
        ),
        check_vma=False,
    )
```

```python
import functools
import math

import jax
import jax.numpy as jnp
from jax import lax
from jax.experimental import pallas as pl
from jax.experimental.pallas import tpu as pltpu
from jax.sharding import PartitionSpec as P

HDIM = 128
KERNEL = 31
LANES = 128
TILE = 64
BACK_TILE = 32
TAPS = 32
FOLD = 32
CONV_COST = 600
ATTEND_COST = 24
BACK_COST = 48
SPLIT_BACK = False
PAD = 0
PACK_LIMIT = 60
F32 = jnp.float32
BF16 = jnp.bfloat16
ROOT = 1.0 / math.sqrt(HDIM)


def swap(cells, axis, mask):
    count = lax.axis_size(axis)
    return lax.ppermute(cells, axis, [(i, i ^ mask) for i in range(count)])


def exchange(sent):
    return [sent[0]] + [swap(sent[k], "fsdp", k) for k in range(1, len(sent))]


def masks_of(count):
    return [1 << i for i in range(count.bit_length() - 1)]


def order_of(count):
    order = [0]
    for mask in reversed(masks_of(count)):
        order += [n ^ mask for n in order]
    return order


def call(body, outs, *operands, scratch=(), flops=0, near=True, stored=0, after=(), limit=40, pinned=False):
    vmem = pl.BlockSpec(memory_space=pltpu.VMEM)
    hbm = pl.BlockSpec(memory_space=pltpu.HBM)
    count = len(operands)
    moved = sum(x.size * x.dtype.itemsize for x in operands)
    moved += sum(math.prod(s) * jnp.dtype(t).itemsize for s, t in outs)
    return pl.pallas_call(
        lambda *refs: body(*refs[:count], *refs[count + len(after) :]),
        out_shape=[(pltpu.VMEM if pinned else jax.ShapeDtypeStruct)(s, t) for s, t in outs],
        in_specs=[vmem if near else hbm] * count + [pl.BlockSpec(memory_space=pl.ANY)] * len(after),
        out_specs=[hbm if i < stored else vmem for i in range(len(outs))],
        scratch_shapes=list(scratch),
        cost_estimate=pl.CostEstimate(flops=flops, bytes_accessed=moved, transcendentals=0),
        compiler_params=pltpu.CompilerParams(vmem_limit_bytes=limit * 1024 * 1024),
    )(*operands, *after)


def block(index, size, unit):
    return pl.ds(pl.multiple_of(index * size, unit), size)


def product(left, right, left_dim, right_dim):
    return lax.dot_general(
        left, right, (((left_dim,), (right_dim,)), ((), ())), preferred_element_type=F32
    )


def tree_sum(terms):
    while len(terms) > 1:
        terms = [terms[i] + terms[i + 1] for i in range(0, len(terms), 2)]
    return terms[0]


def places(top, end, rows):
    return (
        (0, 0, top[0], 0),
        (1, 0, top[1], 0),
        (2, 0, top[2], 0),
        (3, 0, top[2], rows),
        (0, 1, end[0], 0),
        (2, 1, end[1], 0),
        (1, 1, end[2], 0),
        (3, 1, end[2], rows),
    )


def split_up(outs, k, rows, columns, cells):
    own, beside, across, later_across, later_beside = outs
    half = rows // 2
    top, end = cells[:half, :], cells[half:, :]
    if k == 0:
        own[:, columns] = cells
    elif k == 1:
        beside[:half, columns] = top
        later_beside[:, columns] = end
    elif k == 2:
        later_across[:, columns] = top
        across[:half, columns] = end
    else:
        beside[half:, columns] = top
        across[half:, columns] = end


def pack_rows(groups, *refs):
    sources = refs[:4]
    outs = refs[4 : 4 + groups]
    weight_outs = refs[4 + groups : -5]
    held = refs[-5:-1]
    arrived = refs[-1]
    copies = [pltpu.make_async_copy(sources[i], held[i], arrived.at[i]) for i in range(4)]
    for copy in copies:
        copy.start()
    for copy in copies:
        copy.wait()
    me = lax.axis_index("fsdp")
    local, inner = held[0].shape
    rows, model = held[3].shape
    width, channels = inner // groups, model // groups
    for k in range(groups):
        columns = block(me ^ k, width, LANES)
        cells = held[3][:, block(me ^ k, channels, LANES)]
        if weight_outs:
            weight_outs[k][...] = cells
            for at in range(3):
                outs[k][:, at * width : (at + 1) * width] = held[at][:, columns]
        else:
            for at, start, there, column in folds(local, width):
                outs[k][there : there + FOLD, column : column + width] = held[at][start : start + FOLD, columns]
            below = outs[k].shape[0] - rows // 2
            outs[k][below:, :channels] = cells[: rows // 2, :]
            outs[k][below:, channels:] = cells[rows // 2 :, :]


def folds(local, width):
    tall = 3 * local // 4
    for start in range(0, 3 * local, FOLD):
        yield start // local, start % local, start % tall, start // tall * width


def pack_columns(groups, *refs):
    source = refs[0]
    me = lax.axis_index("fsdp")
    width = source.shape[1] // groups
    for k in range(groups):
        refs[1 + k][...] = source[:, block(me ^ k, width, LANES)]


def stack_parts(mine, other, out):
    rows = mine.shape[0]
    out[:rows, :] = mine[...]
    out[rows:, :] = other[rows:, :]


def stack_all(*refs):
    at = 0
    for source in refs[:-1]:
        refs[-1][at : at + source.shape[0], :] = source[...]
        at += source.shape[0]


def attend(groups, *refs):
    pieces = refs[:groups]
    rows_ref = refs[groups]
    outs = refs[groups + 1 : 3 + groups if groups == 4 else 2 + groups]
    weight_refs = refs[groups + 1 + len(outs) :]
    me = lax.axis_index("fsdp")
    local = rows_ref.shape[0] // groups
    half, width = outs[0].shape
    for k in range(groups):
        if weight_refs:
            for at, start, there, column in folds(local, width):
                first = pl.multiple_of((me ^ k) * local + start, FOLD)
                cells = pieces[k][there : there + FOLD, column : column + width]
                rows_ref[pl.ds(first, FOLD), at * width : (at + 1) * width] = cells
            channels = weight_refs[0].shape[1]
            rows = weight_refs[0].shape[0] // groups
            at, share = k * rows, rows // 2
            below = pieces[k].shape[0] - share
            weight_refs[0][at : at + share, :] = pieces[k][below:, :channels]
            weight_refs[0][at + share : at + rows, :] = pieces[k][below:, channels:]
        else:
            rows_ref[block(me ^ k, local, local), :] = pieces[k][...]
    for head in range(width // HDIM):
        at = head * HDIM
        queries = rows_ref[:, at : at + HDIM]
        keys = rows_ref[:, width + at : width + at + HDIM]
        values = rows_ref[:, 2 * width + at : 2 * width + at + HDIM]
        scores = product(queries, keys, 1, 1) * ROOT
        exponent = jnp.exp(scores - jnp.max(scores, axis=1, keepdims=True))
        probs = exponent * (1.0 / jnp.sum(exponent, axis=1, keepdims=True))
        mixed = product(probs.astype(BF16), values, 1, 0).astype(BF16)
        for i, out in enumerate(outs):
            out[:, at : at + HDIM] = mixed[i * half : (i + 1) * half, :]


def join_weight(groups, count, mine, other, out):
    me = lax.axis_index("frame")
    rows = mine.shape[0] // (count // 2 * groups)
    width = rows * count
    for i, n in enumerate(order_of(count)[: count // 2]):
        for k in range(groups):
            at = (i * groups + k) * rows
            for core, source in enumerate((mine, other)):
                start = pl.multiple_of(k * width + (me ^ n ^ core) * rows, rows)
                out[pl.ds(start, rows), :] = source[at : at + rows, :]


def shifted(padded, start, tile):
    for residue in range(8):
        taps = range(residue, KERNEL, 8)
        reach = 8 * (len(taps) - 1)
        rows = padded[start + 1 + residue : start + 1 + residue + tile + reach, :]
        yield taps, rows


def convolve(groups, *refs):
    count = 6 if groups == 4 else groups
    pieces = refs[:count]
    weight, taps_ref, attention, projected_ref, slope_ref = refs[count : count + 5]
    ahead = refs[count + 5 : -3]
    padded, taps, result = refs[-3:]
    me = lax.axis_index("fsdp")
    frames = attention.shape[0]
    channels = weight.shape[1]
    local = frames // groups
    padded[0:16, :] = jnp.zeros((16, LANES), F32)
    padded[frames + 16 : frames + 32, :] = jnp.zeros((16, LANES), F32)
    if groups == 4:
        half, depth = pieces[0].shape
        for k, i, source, at in places(pieces[:3], pieces[3:], half):
            start = i * half
            attention[start : start + half, k * depth : (k + 1) * depth] = source[at : at + half, :]
    else:
        depth = pieces[0].shape[1]
        for k in range(groups):
            attention[:, k * depth : (k + 1) * depth] = pieces[k][...]
    projected_ref[...] = product(attention[...], weight[...], 1, 0).astype(BF16)

    def lane_block(c, carry):
        columns = block(c, LANES, LANES)
        padded[16 : frames + 16, :] = projected_ref[:, columns].astype(F32)
        taps[0:KERNEL, :] = taps_ref[:, block(me * (channels // LANES) + c, LANES, LANES)].astype(F32)
        for start in range(0, frames, TILE):
            conv = jnp.zeros((TILE, LANES), F32)
            for indices, rows in shifted(padded, start, TILE):
                for at, j in enumerate(indices):
                    conv += taps[j : j + 1, :] * rows[8 * at : 8 * at + TILE, :]
            gate = 1.0 / (1.0 + jnp.exp(-conv))
            own = padded[start + 16 : start + 16 + TILE, :]
            result[start : start + TILE, :] = own + conv * gate
            slope_ref[start : start + TILE, columns] = gate * (1.0 + conv * (1.0 - gate))
        for k in range(groups):
            cells = result[block(me ^ k, local, local), :].astype(BF16)
            if groups == 4:
                split_up(ahead, k, local, columns, cells)
            else:
                ahead[k][:, columns] = cells
        return carry

    lax.fori_loop(0, channels // LANES, lane_block, 0)


def convolve_back(groups, *refs):
    upstream = refs[:groups]
    projected_ref, slope_ref, weight, taps_ref, grad_ref, tap_ref = refs[groups : groups + 6]
    outs = refs[-groups - 4 : -4]
    padded, taps, above, sums = refs[-4:]
    me = lax.axis_index("fsdp")
    frames, channels = projected_ref.shape
    local = frames // groups
    depth = weight.shape[0] // groups
    padded[0:16, :] = jnp.zeros((16, LANES), F32)
    padded[frames + 16 : frames + 32, :] = jnp.zeros((16, LANES), F32)

    def lane_block(c, carry):
        columns = block(c, LANES, LANES)
        for k in range(groups):
            above[block(me ^ k, local, local), :] = upstream[k][:, columns].astype(F32)
        taps[0:KERNEL, :] = taps_ref[:, block(me * (channels // LANES) + c, LANES, LANES)].astype(F32)
        padded[16 : frames + 16, :] = (above[...] * slope_ref[:, columns]).astype(BF16).astype(F32)
        sums[...] = jnp.zeros(sums.shape, F32)
        for start in range(0, frames, BACK_TILE):
            total = above[start : start + BACK_TILE, :]
            own = projected_ref[start : start + BACK_TILE, columns].astype(F32)
            for indices, rows in shifted(padded, start, BACK_TILE):
                for at, j in enumerate(indices):
                    part = rows[8 * at : 8 * at + BACK_TILE, :]
                    tap = KERNEL - 1 - j
                    total += taps[tap : tap + 1, :] * part
                    terms = own * part
                    sums[8 * tap : 8 * tap + 8, :] += tree_sum(
                        [terms[8 * i : 8 * i + 8, :] for i in range(BACK_TILE // 8)]
                    )
            grad_ref[start : start + BACK_TILE, columns] = total.astype(BF16)
        tap_ref[:, columns] = jnp.sum(sums[...].reshape(TAPS, 8, LANES), axis=1)
        return carry

    lax.fori_loop(0, channels // LANES, lane_block, 0)
    grads = grad_ref[...]
    for k in range(groups):
        terms = product(grads, weight[k * depth : (k + 1) * depth, :], 1, 1).astype(BF16)
        if groups == 4:
            half = frames // 2
            top, end = outs[k % 2], outs[2 + k // 2]
            top[k // 2 * half : (k // 2 + 1) * half, :] = terms[:half, :]
            end[k % 2 * half : (k % 2 + 1) * half, :] = terms[half:, :]
        else:
            outs[k][...] = terms


def weight_terms(groups, order, rows, *refs):
    attention, grads, tap_ref = refs[:3]
    outs = refs[3:5]
    terms = refs[5]
    me = lax.axis_index("frame")
    depth = attention.shape[1] // groups
    half = len(order) // 2
    for k in range(groups):
        cells = product(attention[:, k * depth : (k + 1) * depth], grads[...], 0, 0)
        terms[...] = cells.astype(BF16)
        for i, n in enumerate(order):
            there = pl.ds(pl.multiple_of((me ^ n) * rows, rows), rows)
            at = TAPS + ((i % half) * groups + k) * rows
            outs[i // half][at : at + rows, :] = terms[there, :]
    for out in outs:
        out[0:TAPS, :] = tap_ref[...].astype(BF16)


def plain_terms(attention, grads, out):
    out[...] = product(attention[...], grads[...], 0, 0).astype(BF16)


def add_halves(mine, other, *outs):
    height = mine.shape[0]
    total = mine[...].astype(F32) + other[0:height, :].astype(F32)
    share = (height - TAPS) // len(outs)
    for k, out in enumerate(outs):
        at = TAPS + k * share
        out[0:TAPS, :] = total[0:TAPS, :].astype(BF16)
        out[TAPS : TAPS + share, :] = total[at : at + share, :].astype(BF16)
        if out.shape[0] > TAPS + share:
            out[TAPS + share :, :] = jnp.zeros((out.shape[0] - TAPS - share, out.shape[1]), BF16)


def fold(mine, other, stays, goes):
    total = (mine[...].astype(F32) + other[...].astype(F32)).astype(BF16)
    half = stays.shape[0]
    stays[...] = total[:half, :]
    goes[...] = total[half:, :]


def weigh(rows_ref, out):
    width = rows_ref.shape[1] // 3
    for head in range(width // HDIM):
        at = head * HDIM
        queries = rows_ref[:, at : at + HDIM]
        keys = rows_ref[:, width + at : width + at + HDIM]
        scores = product(queries, keys, 1, 1) * ROOT
        exponent = jnp.exp(scores - jnp.max(scores, axis=1, keepdims=True))
        out[head] = exponent * (1.0 / jnp.sum(exponent, axis=1, keepdims=True))


def attend_back(groups, *refs):
    rows_ref, weights_ref = refs[:2]
    upstream = refs[2 : groups + 2]
    outs = refs[groups + 2 : -2]
    grads, result = refs[-2:]
    me = lax.axis_index("fsdp")
    width = upstream[0].shape[1]
    local = outs[0].shape[0]
    if groups == 4:
        half = upstream[0].shape[0]
        for i in range(2):
            total = upstream[2 * i][...].astype(F32) + upstream[2 * i + 1][...].astype(F32)
            grads[i * half : (i + 1) * half, :] = total.astype(BF16)
    else:
        grads[...] = tree_sum([ref[...].astype(F32) for ref in upstream]).astype(BF16)
    for head in range(width // HDIM):
        at = head * HDIM
        queries = rows_ref[:, at : at + HDIM]
        keys = rows_ref[:, width + at : width + at + HDIM]
        values = rows_ref[:, 2 * width + at : 2 * width + at + HDIM]
        above = grads[:, at : at + HDIM]
        weights = weights_ref[head]
        slopes = product(above, values, 1, 1)
        row_dot = jnp.sum(weights * slopes, axis=1, keepdims=True)
        grad_scores = (weights * (slopes - row_dot)).astype(BF16)
        result[:, at : at + HDIM] = (product(grad_scores, keys, 1, 0) * ROOT).astype(BF16)
        result[:, width + at : width + at + HDIM] = (
            product(grad_scores, queries, 0, 0) * ROOT
        ).astype(BF16)
        result[:, 2 * width + at : 2 * width + at + HDIM] = product(
            weights.astype(BF16), above, 0, 0
        ).astype(BF16)
    for k in range(groups):
        piece = result[block(me ^ k, local, local), :]
        if len(outs) != groups:
            split_up(outs, k, local, slice(None), piece)
        else:
            outs[k][...] = piece


def scale_sums(groups, scale, *refs):
    sums = refs[:-2]
    weight_ref, tap_ref = refs[-2:]
    me = lax.axis_index("fsdp")
    channels = sums[0].shape[1]
    for k in range(groups):
        columns = block(me ^ k, channels, LANES)
        if len(sums) == groups:
            tap_ref[:, columns] = sums[k][0:KERNEL, :].astype(F32) * scale
            weight_ref[:, columns] = sums[k][TAPS:, :].astype(F32) * scale
    if len(sums) != groups:
        ends = ((sums[0], sums[1], sums[2]), (sums[0], sums[3], sums[4]))
        for k, i, source, at in places(*ends, TAPS):
            at += TAPS if k == 0 and i else 0
            columns = block(me ^ k, channels, LANES)
            if i:
                weight_ref[:, columns] = source[at : at + TAPS, :].astype(F32) * scale
            else:
                tap_ref[:, columns] = source[at : at + KERNEL, :].astype(F32) * scale


def join_ahead(groups, *refs):
    ahead = refs[:-3]
    out, written, sent = refs[-3:]
    me = lax.axis_index("fsdp")
    local, channels = ahead[0].shape
    copies = []
    for i, (k, start, size, source, first) in enumerate(found(groups, local, ahead)):
        there = out.at[0, start : start + size, block(me ^ k, channels, LANES)]
        copies.append(pltpu.make_async_copy(source.at[first : first + size], there, sent.at[i]))
        copies[-1].start()
    for copy in copies:
        copy.wait()
    written[...] = jnp.zeros(written.shape, F32)


def found(groups, local, arrays):
    if len(arrays) == groups:
        return [(k, 0, local, arrays[k], 0) for k in range(groups)]
    share = local // 2
    ends = ((arrays[0], arrays[1], arrays[2]), (arrays[0], arrays[3], arrays[4]))
    parts = [(k, i * share, share, x, at) for k, i, x, at in places(*ends, share) if k]
    return parts + [(0, 0, local, arrays[0], 0)]


def join_all(groups, several, *refs):
    pieces = refs[:several]
    weight_ref, tap_ref = refs[several : several + 2]
    outs = refs[several + 2 : -1]
    sent = refs[-1]
    me = lax.axis_index("fsdp")
    copies = []

    def store(source, target):
        copy = pltpu.make_async_copy(source, target, sent.at[len(copies)])
        copy.start()
        copies.append(copy)

    local, width = pieces[0].shape
    width //= 3
    for k, start, size, source, first in found(groups, local, pieces):
        columns = block(me ^ k, width, LANES)
        for at in range(3):
            part = source.at[first : first + size, at * width : (at + 1) * width]
            store(part, outs[at].at[0, start : start + size, columns])
    store(weight_ref, outs[3])
    store(tap_ref, outs[4])
    for copy in copies:
        copy.wait()


def stack(*arrays, after=()):
    shape = (sum(x.shape[0] for x in arrays),) + arrays[0].shape[1:]
    return call(stack_all, [(shape, arrays[0].dtype)], *arrays, after=after)[0]


def exchange_split(sent, after=()):
    if len(sent) != 5:
        return exchange(sent)
    own, beside, across, later_across, later_beside = sent
    shape = [(beside.shape, beside.dtype)]
    beside, across = swap(beside, "fsdp", 1), swap(across, "fsdp", 2)
    (later_across,) = call(stack_parts, shape, later_across, beside, after=after)
    (later_beside,) = call(stack_parts, shape, later_beside, across, after=after)
    return [own, beside, swap(later_across, "fsdp", 2), across, swap(later_beside, "fsdp", 1)]


def gather_weight(mine, groups, count, after):
    rows, channels = mine.shape[0] // groups, mine.shape[1]
    pieces = [mine]
    for mask in reversed(masks_of(count)[1:]):
        pieces += [swap(piece, "frame", mask) for piece in pieces]
    gathered = stack(*pieces, after=after)
    other = swap(gathered, "frame", 1)
    if rows % 16 == 0:
        return call(
            functools.partial(join_weight, groups, count),
            [((groups * count * rows, channels), BF16)],
            gathered,
            other,
        )[0]
    me = lax.axis_index("frame")
    order = order_of(count)
    place = jnp.array([order.index(n) for n in range(count)])
    both = jnp.concatenate([gathered, other], axis=0).reshape(count, groups, rows, channels)
    ordered = jnp.take(both, place[me ^ jnp.arange(count)], axis=0)
    return ordered.transpose(1, 0, 2, 3).reshape(groups * count * rows, channels)


def weight_halves(attention, grads, tap_terms, groups, count, rows, after):
    channels = grads.shape[1]
    depth = attention.shape[1] // groups
    share = count // 2 * groups * rows
    bits = count.bit_length() - 1
    order = [sum((i >> b & 1) << (bits - 1 - b) for b in range(bits)) for i in range(count)]
    if rows % 16 == 0:
        halves = call(
            functools.partial(weight_terms, groups, order, rows),
            [((TAPS + share, channels), BF16)] * 2,
            attention,
            grads,
            tap_terms,
            scratch=[pltpu.VMEM((depth, channels), BF16)],
            after=after,
        )
    else:
        (terms,) = call(plain_terms, [((groups * depth, channels), BF16)], attention, grads)
        me = lax.axis_index("frame")
        terms = terms.reshape(groups, count, rows, channels)
        terms = jnp.take(terms, me ^ jnp.array(order), axis=1)
        terms = terms.transpose(1, 0, 2, 3).reshape(2, share, channels)
        halves = [jnp.concatenate([tap_terms.astype(BF16), x], axis=0) for x in terms]
    return halves


def add_up(halves, mask, spare):
    mine, other = halves
    height = TAPS + (mine.shape[0] - TAPS) // 2
    shapes = [((height, mine.shape[1]), BF16), ((height + spare, mine.shape[1]), BF16)]
    return call(add_halves, shapes, mine, swap(other, "frame", mask))


def shards(queries, key_rows, value_rows, out_weight, conv_weight, grad_out):
    local, inner = queries.shape[1:]
    rows, model = out_weight.shape
    groups = lax.axis_size("fsdp")
    count = lax.axis_size("frame")
    frames = local * groups
    width = inner // groups
    channels = model // groups
    scale = 1.0 / math.sqrt(frames * count)
    conv_flops = CONV_COST * KERNEL * frames * channels

    folded = groups == 4
    def split(size):
        shape, small = ((local, size), BF16), ((local // 2, size), BF16)
        return [shape, shape, shape, small, small] if folded else [shape] * groups

    merged = folded and rows % 32 == 0 and channels == 2 * width and local % (4 * FOLD) == 0
    shape = (3 * local // 4 + rows // 2, 4 * width) if merged else (local, 3 * width)
    whole = (groups * rows, channels)
    sent = call(
        functools.partial(pack_rows, groups),
        [(shape, BF16)] * groups
        + ([] if merged else [((rows, channels), BF16)] * groups),
        queries[0],
        key_rows[0],
        value_rows[0],
        out_weight,
        near=False,
        limit=PACK_LIMIT,
        pinned=True,
        scratch=[pltpu.VMEM((local, inner), BF16)] * 3
        + [pltpu.VMEM((rows, model), BF16), pltpu.SemaphoreType.DMA((4,))],
    )
    half = ((frames // 2, width), BF16)
    held, *own = call(
        functools.partial(attend, groups),
        [((frames, 3 * width), BF16)]
        + ([half, half] if folded else [((frames, width), BF16)])
        + ([(whole, BF16)] if merged else []),
        *exchange(sent[:groups]),
        flops=ATTEND_COST * frames * frames * width,
    )
    gathered = own.pop() if merged else stack(*exchange(sent[groups:]))
    if folded:
        top, end = own
        beside, across = swap(top, "fsdp", 1), swap(end, "fsdp", 2)
        step = [beside, across]
        attention = [top, beside, swap(stack(top, beside), "fsdp", 2)]
        attention += [end, across, swap(stack(end, across), "fsdp", 1)]
        last = [attention[2], attention[5]]
    else:
        attention = exchange(own * groups)
        step = last = attention[1:2]
    sent = call(
        functools.partial(pack_columns, groups),
        [((local, channels), BF16)] * groups,
        grad_out[0],
        after=step,
    )
    upstream = exchange(sent)
    weight = gather_weight(gathered, groups, count, last + upstream[1:3])

    outs = call(
        functools.partial(convolve, groups),
        [((frames, inner), BF16), ((frames, channels), BF16), ((frames, channels), F32)]
        + split(channels),
        *attention,
        weight,
        conv_weight,
        scratch=[
            pltpu.VMEM((frames + 32, LANES), F32),
            pltpu.VMEM((TAPS, LANES), F32),
            pltpu.VMEM((frames, LANES), F32),
        ],
        flops=conv_flops,
    )
    whole, projected, slope = outs[:3]
    (weights,) = call(weigh, [((width // HDIM, frames, frames), F32)], held)
    ahead = exchange_split(outs[3:], after=[weights])

    outs = call(
        functools.partial(convolve_back, groups),
        [((frames, channels), BF16), ((TAPS, channels), F32)] + [((frames, width), BF16)] * groups,
        *upstream,
        projected,
        slope,
        weight,
        conv_weight,
        scratch=[
            pltpu.VMEM((frames + 32, LANES), F32),
            pltpu.VMEM((TAPS, LANES), F32),
            pltpu.VMEM((frames, LANES), F32),
            pltpu.VMEM((8 * TAPS, LANES), F32),
        ],
        flops=conv_flops * 3 // 2,
    )
    grads, tap_terms = outs[:2]
    if folded:
        stay_top, go_top, stay_end, go_end = outs[2:]
        shapes = [((frames // 2, width), BF16)] * 2
        stay_top, go_top = call(fold, shapes, stay_top, swap(go_top, "fsdp", 1))
        stay_end, go_end = call(fold, shapes, stay_end, swap(go_end, "fsdp", 2))
        above = [stay_top, swap(go_top, "fsdp", 2), stay_end, swap(go_end, "fsdp", 1)]
    else:
        above = exchange(outs[2:])
    halves = weight_halves(whole, grads, tap_terms, groups, count, rows, ahead[1:4:2])
    masks = masks_of(count)
    for mask in masks[:-1]:
        halves = add_up(halves, mask, PAD if mask == masks[-2] and rows % 16 == 0 else 0)
    sent = call(
        functools.partial(attend_back, groups),
        split(3 * width) if SPLIT_BACK else [((local, 3 * width), BF16)] * groups,
        held,
        weights,
        *above,
        scratch=[pltpu.VMEM((frames, width), BF16), pltpu.VMEM((frames, 3 * width), BF16)],
        flops=BACK_COST * frames * frames * width,
        after=[halves[1], *(ahead[2:5:2] if folded else ())],
    )
    pieces = exchange_split(sent)
    block_out, written = call(
        functools.partial(join_ahead, groups),
        [((1, local, model), BF16), ((8, LANES), F32)],
        *ahead,
        stored=1,
        scratch=[pltpu.SemaphoreType.DMA((2 * groups,))],
    )
    shapes = [((TAPS + rows, channels), BF16)] * groups
    other = swap(halves[1], "frame", masks[-1])
    sums = list(call(add_halves, shapes, halves[0], other, after=[written]))
    first = swap(sums[0], "frame", 1)
    sums[-1] = stack(sums[-1], after=[first, pieces[2]])
    sums = exchange(sums)
    shapes = [((rows, model), F32), ((KERNEL, model), F32)]
    sums = call(functools.partial(scale_sums, groups, scale), shapes, *sums)
    joined = call(
        functools.partial(join_all, groups, len(pieces)),
        [((1, local, inner), BF16)] * 3 + [((rows, model), F32), ((KERNEL, model), F32)],
        *pieces,
        *sums,
        stored=5,
        scratch=[pltpu.SemaphoreType.DMA((8 * groups + 2,))],
    )
    return (block_out, *joined)


def solution(mesh):
    return jax.shard_map(
        shards,
        mesh=mesh,
        in_specs=(
            P("frame", "fsdp", None),
            P("frame", "fsdp", None),
            P("frame", "fsdp", None),
            P(("fsdp", "frame"), None),
            P(),
            P("frame", "fsdp", None),
        ),
        out_specs=(
            P("frame", "fsdp", None),
            P("frame", "fsdp", None),
            P("frame", "fsdp", None),
            P("frame", "fsdp", None),
            P(("fsdp", "frame"), None),
            P(),
        ),
        check_vma=False,
    )
```

```python
import functools
import math

import jax
import jax.numpy as jnp
from jax import lax
from jax.experimental import pallas as pl
from jax.experimental.pallas import tpu as pltpu
from jax.sharding import PartitionSpec as P

HDIM = 128
KERNEL = 31
LANES = 128
TILE = 64
BACK_TILE = 32
TAPS = 32
FOLD = 32
CONV_COST = 600
ATTEND_COST = 24
BACK_COST = 48
SPLIT_BACK = False
PAD = 0
PACK_LIMIT = 60
F32 = jnp.float32
BF16 = jnp.bfloat16
ROOT = 1.0 / math.sqrt(HDIM)


def swap(cells, axis, mask):
    count = lax.axis_size(axis)
    return lax.ppermute(cells, axis, [(i, i ^ mask) for i in range(count)])


def exchange(sent):
    return [sent[0]] + [swap(sent[k], "fsdp", k) for k in range(1, len(sent))]


def masks_of(count):
    return [1 << i for i in range(count.bit_length() - 1)]


def order_of(count):
    order = [0]
    for mask in reversed(masks_of(count)):
        order += [n ^ mask for n in order]
    return order


def call(body, outs, *operands, scratch=(), flops=0, near=True, stored=0, after=(), limit=40, pinned=False):
    vmem = pl.BlockSpec(memory_space=pltpu.VMEM)
    hbm = pl.BlockSpec(memory_space=pltpu.HBM)
    count = len(operands)
    moved = sum(x.size * x.dtype.itemsize for x in operands)
    moved += sum(math.prod(s) * jnp.dtype(t).itemsize for s, t in outs)
    return pl.pallas_call(
        lambda *refs: body(*refs[:count], *refs[count + len(after) :]),
        out_shape=[(pltpu.VMEM if pinned else jax.ShapeDtypeStruct)(s, t) for s, t in outs],
        in_specs=[vmem if near else hbm] * count + [pl.BlockSpec(memory_space=pl.ANY)] * len(after),
        out_specs=[hbm if i < stored else vmem for i in range(len(outs))],
        scratch_shapes=list(scratch),
        cost_estimate=pl.CostEstimate(flops=flops, bytes_accessed=moved, transcendentals=0),
        compiler_params=pltpu.CompilerParams(vmem_limit_bytes=limit * 1024 * 1024),
    )(*operands, *after)


def block(index, size, unit):
    return pl.ds(pl.multiple_of(index * size, unit), size)


def product(left, right, left_dim, right_dim):
    return lax.dot_general(
        left, right, (((left_dim,), (right_dim,)), ((), ())), preferred_element_type=F32
    )


def tree_sum(terms):
    while len(terms) > 1:
        terms = [terms[i] + terms[i + 1] for i in range(0, len(terms), 2)]
    return terms[0]


def places(top, end, rows):
    return (
        (0, 0, top[0], 0),
        (1, 0, top[1], 0),
        (2, 0, top[2], 0),
        (3, 0, top[2], rows),
        (0, 1, end[0], 0),
        (2, 1, end[1], 0),
        (1, 1, end[2], 0),
        (3, 1, end[2], rows),
    )


def split_up(outs, k, rows, columns, cells):
    own, beside, across, later_across, later_beside = outs
    half = rows // 2
    top, end = cells[:half, :], cells[half:, :]
    if k == 0:
        own[:, columns] = cells
    elif k == 1:
        beside[:half, columns] = top
        later_beside[:, columns] = end
    elif k == 2:
        later_across[:, columns] = top
        across[:half, columns] = end
    else:
        beside[half:, columns] = top
        across[half:, columns] = end


def pack_rows(groups, *refs):
    sources = refs[:4]
    outs = refs[4 : 4 + groups]
    weight_outs = refs[4 + groups : -5]
    held = refs[-5:-1]
    arrived = refs[-1]
    copies = [pltpu.make_async_copy(sources[i], held[i], arrived.at[i]) for i in range(4)]
    for copy in copies:
        copy.start()
    for copy in copies:
        copy.wait()
    me = lax.axis_index("fsdp")
    local, inner = held[0].shape
    rows, model = held[3].shape
    width, channels = inner // groups, model // groups
    for k in range(groups):
        columns = block(me ^ k, width, LANES)
        cells = held[3][:, block(me ^ k, channels, LANES)]
        if weight_outs:
            weight_outs[k][...] = cells
            for at in range(3):
                outs[k][:, at * width : (at + 1) * width] = held[at][:, columns]
        else:
            for at, start, there, column in folds(local, width):
                outs[k][there : there + FOLD, column : column + width] = held[at][start : start + FOLD, columns]
            below = outs[k].shape[0] - rows // 2
            outs[k][below:, :channels] = cells[: rows // 2, :]
            outs[k][below:, channels:] = cells[rows // 2 :, :]


def folds(local, width):
    tall = 3 * local // 4
    for start in range(0, 3 * local, FOLD):
        yield start // local, start % local, start % tall, start // tall * width


def pack_columns(groups, *refs):
    source = refs[0]
    me = lax.axis_index("fsdp")
    width = source.shape[1] // groups
    for k in range(groups):
        refs[1 + k][...] = source[:, block(me ^ k, width, LANES)]


def stack_parts(mine, other, out):
    rows = mine.shape[0]
    out[:rows, :] = mine[...]
    out[rows:, :] = other[rows:, :]


def stack_all(*refs):
    at = 0
    for source in refs[:-1]:
        refs[-1][at : at + source.shape[0], :] = source[...]
        at += source.shape[0]


def attend(groups, *refs):
    pieces = refs[:groups]
    rows_ref = refs[groups]
    outs = refs[groups + 1 : 3 + groups if groups == 4 else 2 + groups]
    weight_refs = refs[groups + 1 + len(outs) :]
    me = lax.axis_index("fsdp")
    local = rows_ref.shape[0] // groups
    half, width = outs[0].shape
    for k in range(groups):
        if weight_refs:
            for at, start, there, column in folds(local, width):
                first = pl.multiple_of((me ^ k) * local + start, FOLD)
                cells = pieces[k][there : there + FOLD, column : column + width]
                rows_ref[pl.ds(first, FOLD), at * width : (at + 1) * width] = cells
            channels = weight_refs[0].shape[1]
            rows = weight_refs[0].shape[0] // groups
            at, share = k * rows, rows // 2
            below = pieces[k].shape[0] - share
            weight_refs[0][at : at + share, :] = pieces[k][below:, :channels]
            weight_refs[0][at + share : at + rows, :] = pieces[k][below:, channels:]
        else:
            rows_ref[block(me ^ k, local, local), :] = pieces[k][...]
    for head in range(width // HDIM):
        at = head * HDIM
        queries = rows_ref[:, at : at + HDIM]
        keys = rows_ref[:, width + at : width + at + HDIM]
        values = rows_ref[:, 2 * width + at : 2 * width + at + HDIM]
        scores = product(queries, keys, 1, 1) * ROOT
        exponent = jnp.exp(scores - jnp.max(scores, axis=1, keepdims=True))
        probs = exponent * (1.0 / jnp.sum(exponent, axis=1, keepdims=True))
        mixed = product(probs.astype(BF16), values, 1, 0).astype(BF16)
        for i, out in enumerate(outs):
            out[:, at : at + HDIM] = mixed[i * half : (i + 1) * half, :]


def join_weight(groups, count, mine, other, out):
    me = lax.axis_index("frame")
    rows = mine.shape[0] // (count // 2 * groups)
    width = rows * count
    for i, n in enumerate(order_of(count)[: count // 2]):
        for k in range(groups):
            at = (i * groups + k) * rows
            for core, source in enumerate((mine, other)):
                start = pl.multiple_of(k * width + (me ^ n ^ core) * rows, rows)
                out[pl.ds(start, rows), :] = source[at : at + rows, :]


def shifted(padded, start, tile):
    for residue in range(8):
        taps = range(residue, KERNEL, 8)
        reach = 8 * (len(taps) - 1)
        rows = padded[start + 1 + residue : start + 1 + residue + tile + reach, :]
        yield taps, rows


def convolve(groups, *refs):
    count = 6 if groups == 4 else groups
    pieces = refs[:count]
    weight, taps_ref, attention, projected_ref, slope_ref = refs[count : count + 5]
    ahead = refs[count + 5 : -3]
    padded, taps, result = refs[-3:]
    me = lax.axis_index("fsdp")
    frames = attention.shape[0]
    channels = weight.shape[1]
    local = frames // groups
    padded[0:16, :] = jnp.zeros((16, LANES), F32)
    padded[frames + 16 : frames + 32, :] = jnp.zeros((16, LANES), F32)
    if groups == 4:
        half, depth = pieces[0].shape
        for k, i, source, at in places(pieces[:3], pieces[3:], half):
            start = i * half
            attention[start : start + half, k * depth : (k + 1) * depth] = source[at : at + half, :]
    else:
        depth = pieces[0].shape[1]
        for k in range(groups):
            attention[:, k * depth : (k + 1) * depth] = pieces[k][...]
    projected_ref[...] = product(attention[...], weight[...], 1, 0).astype(BF16)

    def lane_block(c, carry):
        columns = block(c, LANES, LANES)
        padded[16 : frames + 16, :] = projected_ref[:, columns].astype(F32)
        taps[0:KERNEL, :] = taps_ref[:, block(me * (channels // LANES) + c, LANES, LANES)].astype(F32)
        for start in range(0, frames, TILE):
            conv = jnp.zeros((TILE, LANES), F32)
            for indices, rows in shifted(padded, start, TILE):
                for at, j in enumerate(indices):
                    conv += taps[j : j + 1, :] * rows[8 * at : 8 * at + TILE, :]
            gate = 1.0 / (1.0 + jnp.exp(-conv))
            own = padded[start + 16 : start + 16 + TILE, :]
            result[start : start + TILE, :] = own + conv * gate
            slope_ref[start : start + TILE, columns] = gate * (1.0 + conv * (1.0 - gate))
        for k in range(groups):
            cells = result[block(me ^ k, local, local), :].astype(BF16)
            if groups == 4:
                split_up(ahead, k, local, columns, cells)
            else:
                ahead[k][:, columns] = cells
        return carry

    lax.fori_loop(0, channels // LANES, lane_block, 0)


def convolve_back(groups, *refs):
    upstream = refs[:groups]
    projected_ref, slope_ref, weight, taps_ref, grad_ref, tap_ref = refs[groups : groups + 6]
    outs = refs[-groups - 4 : -4]
    padded, taps, above, sums = refs[-4:]
    me = lax.axis_index("fsdp")
    frames, channels = projected_ref.shape
    local = frames // groups
    depth = weight.shape[0] // groups
    padded[0:16, :] = jnp.zeros((16, LANES), F32)
    padded[frames + 16 : frames + 32, :] = jnp.zeros((16, LANES), F32)

    def lane_block(c, carry):
        columns = block(c, LANES, LANES)
        for k in range(groups):
            above[block(me ^ k, local, local), :] = upstream[k][:, columns].astype(F32)
        taps[0:KERNEL, :] = taps_ref[:, block(me * (channels // LANES) + c, LANES, LANES)].astype(F32)
        padded[16 : frames + 16, :] = (above[...] * slope_ref[:, columns]).astype(BF16).astype(F32)
        sums[...] = jnp.zeros(sums.shape, F32)
        for start in range(0, frames, BACK_TILE):
            total = above[start : start + BACK_TILE, :]
            own = projected_ref[start : start + BACK_TILE, columns].astype(F32)
            for indices, rows in shifted(padded, start, BACK_TILE):
                for at, j in enumerate(indices):
                    part = rows[8 * at : 8 * at + BACK_TILE, :]
                    tap = KERNEL - 1 - j
                    total += taps[tap : tap + 1, :] * part
                    terms = own * part
                    sums[8 * tap : 8 * tap + 8, :] += tree_sum(
                        [terms[8 * i : 8 * i + 8, :] for i in range(BACK_TILE // 8)]
                    )
            grad_ref[start : start + BACK_TILE, columns] = total.astype(BF16)
        tap_ref[:, columns] = jnp.sum(sums[...].reshape(TAPS, 8, LANES), axis=1)
        return carry

    lax.fori_loop(0, channels // LANES, lane_block, 0)
    grads = grad_ref[...]
    for k in range(groups):
        terms = product(grads, weight[k * depth : (k + 1) * depth, :], 1, 1).astype(BF16)
        if groups == 4:
            half = frames // 2
            top, end = outs[k % 2], outs[2 + k // 2]
            top[k // 2 * half : (k // 2 + 1) * half, :] = terms[:half, :]
            end[k % 2 * half : (k % 2 + 1) * half, :] = terms[half:, :]
        else:
            outs[k][...] = terms


def weight_terms(groups, order, rows, *refs):
    attention, grads, tap_ref = refs[:3]
    outs = refs[3:5]
    terms = refs[5]
    me = lax.axis_index("frame")
    depth = attention.shape[1] // groups
    half = len(order) // 2
    for k in range(groups):
        cells = product(attention[:, k * depth : (k + 1) * depth], grads[...], 0, 0)
        terms[...] = cells.astype(BF16)
        for i, n in enumerate(order):
            there = pl.ds(pl.multiple_of((me ^ n) * rows, rows), rows)
            at = TAPS + ((i % half) * groups + k) * rows
            outs[i // half][at : at + rows, :] = terms[there, :]
    for out in outs:
        out[0:TAPS, :] = tap_ref[...].astype(BF16)


def plain_terms(attention, grads, out):
    out[...] = product(attention[...], grads[...], 0, 0).astype(BF16)


def add_halves(mine, other, *outs):
    height = mine.shape[0]
    total = mine[...].astype(F32) + other[0:height, :].astype(F32)
    share = (height - TAPS) // len(outs)
    for k, out in enumerate(outs):
        at = TAPS + k * share
        out[0:TAPS, :] = total[0:TAPS, :].astype(BF16)
        out[TAPS : TAPS + share, :] = total[at : at + share, :].astype(BF16)
        if out.shape[0] > TAPS + share:
            out[TAPS + share :, :] = jnp.zeros((out.shape[0] - TAPS - share, out.shape[1]), BF16)


def fold(mine, other, stays, goes):
    total = (mine[...].astype(F32) + other[...].astype(F32)).astype(BF16)
    half = stays.shape[0]
    stays[...] = total[:half, :]
    goes[...] = total[half:, :]


def weigh(rows_ref, out, rounded):
    width = rows_ref.shape[1] // 3
    for head in range(width // HDIM):
        at = head * HDIM
        queries = rows_ref[:, at : at + HDIM]
        keys = rows_ref[:, width + at : width + at + HDIM]
        scores = product(queries, keys, 1, 1) * ROOT
        exponent = jnp.exp(scores - jnp.max(scores, axis=1, keepdims=True))
        weights = exponent * (1.0 / jnp.sum(exponent, axis=1, keepdims=True))
        out[head] = weights
        rounded[head] = weights.astype(BF16)


def attend_back(groups, *refs):
    rows_ref, weights_ref, probs_ref = refs[:3]
    upstream = refs[3 : groups + 3]
    outs = refs[groups + 3 : -2]
    grads, result = refs[-2:]
    me = lax.axis_index("fsdp")
    width = upstream[0].shape[1]
    local = outs[0].shape[0]
    if groups == 4:
        half = upstream[0].shape[0]
        for i in range(2):
            total = upstream[2 * i][...].astype(F32) + upstream[2 * i + 1][...].astype(F32)
            grads[i * half : (i + 1) * half, :] = total.astype(BF16)
    else:
        grads[...] = tree_sum([ref[...].astype(F32) for ref in upstream]).astype(BF16)
    for head in range(width // HDIM):
        at = head * HDIM
        queries = rows_ref[:, at : at + HDIM]
        keys = rows_ref[:, width + at : width + at + HDIM]
        values = rows_ref[:, 2 * width + at : 2 * width + at + HDIM]
        above = grads[:, at : at + HDIM]
        weights = weights_ref[head]
        slopes = product(above, values, 1, 1)
        row_dot = jnp.sum(weights * slopes, axis=1, keepdims=True)
        grad_scores = (weights * (slopes - row_dot)).astype(BF16)
        result[:, at : at + HDIM] = (product(grad_scores, keys, 1, 0) * ROOT).astype(BF16)
        result[:, width + at : width + at + HDIM] = (
            product(grad_scores, queries, 0, 0) * ROOT
        ).astype(BF16)
        result[:, 2 * width + at : 2 * width + at + HDIM] = product(
            probs_ref[head], above, 0, 0
        ).astype(BF16)
    for k in range(groups):
        piece = result[block(me ^ k, local, local), :]
        if len(outs) != groups:
            split_up(outs, k, local, slice(None), piece)
        else:
            outs[k][...] = piece


def scale_sums(groups, scale, *refs):
    sums = refs[:-2]
    weight_ref, tap_ref = refs[-2:]
    me = lax.axis_index("fsdp")
    channels = sums[0].shape[1]
    for k in range(groups):
        columns = block(me ^ k, channels, LANES)
        if len(sums) == groups:
            tap_ref[:, columns] = sums[k][0:KERNEL, :].astype(F32) * scale
            weight_ref[:, columns] = sums[k][TAPS:, :].astype(F32) * scale
    if len(sums) != groups:
        ends = ((sums[0], sums[1], sums[2]), (sums[0], sums[3], sums[4]))
        for k, i, source, at in places(*ends, TAPS):
            at += TAPS if k == 0 and i else 0
            columns = block(me ^ k, channels, LANES)
            if i:
                weight_ref[:, columns] = source[at : at + TAPS, :].astype(F32) * scale
            else:
                tap_ref[:, columns] = source[at : at + KERNEL, :].astype(F32) * scale


def join_ahead(groups, *refs):
    ahead = refs[:-3]
    out, written, sent = refs[-3:]
    me = lax.axis_index("fsdp")
    local, channels = ahead[0].shape
    copies = []
    for i, (k, start, size, source, first) in enumerate(found(groups, local, ahead)):
        there = out.at[0, start : start + size, block(me ^ k, channels, LANES)]
        copies.append(pltpu.make_async_copy(source.at[first : first + size], there, sent.at[i]))
        copies[-1].start()
    for copy in copies:
        copy.wait()
    written[...] = jnp.zeros(written.shape, F32)


def found(groups, local, arrays):
    if len(arrays) == groups:
        return [(k, 0, local, arrays[k], 0) for k in range(groups)]
    share = local // 2
    ends = ((arrays[0], arrays[1], arrays[2]), (arrays[0], arrays[3], arrays[4]))
    parts = [(k, i * share, share, x, at) for k, i, x, at in places(*ends, share) if k]
    return parts + [(0, 0, local, arrays[0], 0)]


def join_all(groups, several, *refs):
    pieces = refs[:several]
    weight_ref, tap_ref = refs[several : several + 2]
    outs = refs[several + 2 : -1]
    sent = refs[-1]
    me = lax.axis_index("fsdp")
    copies = []

    def store(source, target):
        copy = pltpu.make_async_copy(source, target, sent.at[len(copies)])
        copy.start()
        copies.append(copy)

    local, width = pieces[0].shape
    width //= 3
    for k, start, size, source, first in found(groups, local, pieces):
        columns = block(me ^ k, width, LANES)
        for at in range(3):
            part = source.at[first : first + size, at * width : (at + 1) * width]
            store(part, outs[at].at[0, start : start + size, columns])
    store(weight_ref, outs[3])
    store(tap_ref, outs[4])
    for copy in copies:
        copy.wait()


def stack(*arrays, after=()):
    shape = (sum(x.shape[0] for x in arrays),) + arrays[0].shape[1:]
    return call(stack_all, [(shape, arrays[0].dtype)], *arrays, after=after)[0]


def exchange_split(sent, after=()):
    if len(sent) != 5:
        return exchange(sent)
    own, beside, across, later_across, later_beside = sent
    shape = [(beside.shape, beside.dtype)]
    beside, across = swap(beside, "fsdp", 1), swap(across, "fsdp", 2)
    (later_across,) = call(stack_parts, shape, later_across, beside, after=after)
    (later_beside,) = call(stack_parts, shape, later_beside, across, after=after)
    return [own, beside, swap(later_across, "fsdp", 2), across, swap(later_beside, "fsdp", 1)]


def gather_weight(mine, groups, count, after):
    rows, channels = mine.shape[0] // groups, mine.shape[1]
    pieces = [mine]
    for mask in reversed(masks_of(count)[1:]):
        pieces += [swap(piece, "frame", mask) for piece in pieces]
    gathered = stack(*pieces, after=after)
    other = swap(gathered, "frame", 1)
    if rows % 16 == 0:
        return call(
            functools.partial(join_weight, groups, count),
            [((groups * count * rows, channels), BF16)],
            gathered,
            other,
        )[0]
    me = lax.axis_index("frame")
    order = order_of(count)
    place = jnp.array([order.index(n) for n in range(count)])
    both = jnp.concatenate([gathered, other], axis=0).reshape(count, groups, rows, channels)
    ordered = jnp.take(both, place[me ^ jnp.arange(count)], axis=0)
    return ordered.transpose(1, 0, 2, 3).reshape(groups * count * rows, channels)


def weight_halves(attention, grads, tap_terms, groups, count, rows, after):
    channels = grads.shape[1]
    depth = attention.shape[1] // groups
    share = count // 2 * groups * rows
    bits = count.bit_length() - 1
    order = [sum((i >> b & 1) << (bits - 1 - b) for b in range(bits)) for i in range(count)]
    if rows % 16 == 0:
        halves = call(
            functools.partial(weight_terms, groups, order, rows),
            [((TAPS + share, channels), BF16)] * 2,
            attention,
            grads,
            tap_terms,
            scratch=[pltpu.VMEM((depth, channels), BF16)],
            after=after,
        )
    else:
        (terms,) = call(plain_terms, [((groups * depth, channels), BF16)], attention, grads)
        me = lax.axis_index("frame")
        terms = terms.reshape(groups, count, rows, channels)
        terms = jnp.take(terms, me ^ jnp.array(order), axis=1)
        terms = terms.transpose(1, 0, 2, 3).reshape(2, share, channels)
        halves = [jnp.concatenate([tap_terms.astype(BF16), x], axis=0) for x in terms]
    return halves


def add_up(halves, mask, spare):
    mine, other = halves
    height = TAPS + (mine.shape[0] - TAPS) // 2
    shapes = [((height, mine.shape[1]), BF16), ((height + spare, mine.shape[1]), BF16)]
    return call(add_halves, shapes, mine, swap(other, "frame", mask))


def shards(queries, key_rows, value_rows, out_weight, conv_weight, grad_out):
    local, inner = queries.shape[1:]
    rows, model = out_weight.shape
    groups = lax.axis_size("fsdp")
    count = lax.axis_size("frame")
    frames = local * groups
    width = inner // groups
    channels = model // groups
    scale = 1.0 / math.sqrt(frames * count)
    conv_flops = CONV_COST * KERNEL * frames * channels

    folded = groups == 4
    def split(size):
        shape, small = ((local, size), BF16), ((local // 2, size), BF16)
        return [shape, shape, shape, small, small] if folded else [shape] * groups

    merged = folded and rows % 32 == 0 and channels == 2 * width and local % (4 * FOLD) == 0
    shape = (3 * local // 4 + rows // 2, 4 * width) if merged else (local, 3 * width)
    whole = (groups * rows, channels)
    sent = call(
        functools.partial(pack_rows, groups),
        [(shape, BF16)] * groups
        + ([] if merged else [((rows, channels), BF16)] * groups),
        queries[0],
        key_rows[0],
        value_rows[0],
        out_weight,
        near=False,
        limit=PACK_LIMIT,
        pinned=True,
        scratch=[pltpu.VMEM((local, inner), BF16)] * 3
        + [pltpu.VMEM((rows, model), BF16), pltpu.SemaphoreType.DMA((4,))],
    )
    half = ((frames // 2, width), BF16)
    held, *own = call(
        functools.partial(attend, groups),
        [((frames, 3 * width), BF16)]
        + ([half, half] if folded else [((frames, width), BF16)])
        + ([(whole, BF16)] if merged else []),
        *exchange(sent[:groups]),
        flops=ATTEND_COST * frames * frames * width,
    )
    gathered = own.pop() if merged else stack(*exchange(sent[groups:]))
    if folded:
        top, end = own
        beside, across = swap(top, "fsdp", 1), swap(end, "fsdp", 2)
        step = [beside, across]
        attention = [top, beside, swap(stack(top, beside), "fsdp", 2)]
        attention += [end, across, swap(stack(end, across), "fsdp", 1)]
        last = [attention[2], attention[5]]
    else:
        attention = exchange(own * groups)
        step = last = attention[1:2]
    sent = call(
        functools.partial(pack_columns, groups),
        [((local, channels), BF16)] * groups,
        grad_out[0],
        after=step,
    )
    upstream = exchange(sent)
    weight = gather_weight(gathered, groups, count, last + upstream[1:3])

    outs = call(
        functools.partial(convolve, groups),
        [((frames, inner), BF16), ((frames, channels), BF16), ((frames, channels), F32)]
        + split(channels),
        *attention,
        weight,
        conv_weight,
        scratch=[
            pltpu.VMEM((frames + 32, LANES), F32),
            pltpu.VMEM((TAPS, LANES), F32),
            pltpu.VMEM((frames, LANES), F32),
        ],
        flops=conv_flops,
    )
    whole, projected, slope = outs[:3]
    square = (width // HDIM, frames, frames)
    weights, probs = call(weigh, [(square, F32), (square, BF16)], held)
    ahead = exchange_split(outs[3:], after=[weights])

    outs = call(
        functools.partial(convolve_back, groups),
        [((frames, channels), BF16), ((TAPS, channels), F32)] + [((frames, width), BF16)] * groups,
        *upstream,
        projected,
        slope,
        weight,
        conv_weight,
        scratch=[
            pltpu.VMEM((frames + 32, LANES), F32),
            pltpu.VMEM((TAPS, LANES), F32),
            pltpu.VMEM((frames, LANES), F32),
            pltpu.VMEM((8 * TAPS, LANES), F32),
        ],
        flops=conv_flops * 3 // 2,
    )
    grads, tap_terms = outs[:2]
    if folded:
        stay_top, go_top, stay_end, go_end = outs[2:]
        shapes = [((frames // 2, width), BF16)] * 2
        stay_top, go_top = call(fold, shapes, stay_top, swap(go_top, "fsdp", 1))
        stay_end, go_end = call(fold, shapes, stay_end, swap(go_end, "fsdp", 2))
        above = [stay_top, swap(go_top, "fsdp", 2), stay_end, swap(go_end, "fsdp", 1)]
    else:
        above = exchange(outs[2:])
    halves = weight_halves(whole, grads, tap_terms, groups, count, rows, ahead[1:4:2])
    masks = masks_of(count)
    for mask in masks[:-1]:
        halves = add_up(halves, mask, PAD if mask == masks[-2] and rows % 16 == 0 else 0)
    sent = call(
        functools.partial(attend_back, groups),
        split(3 * width) if SPLIT_BACK else [((local, 3 * width), BF16)] * groups,
        held,
        weights,
        probs,
        *above,
        scratch=[pltpu.VMEM((frames, width), BF16), pltpu.VMEM((frames, 3 * width), BF16)],
        flops=BACK_COST * frames * frames * width,
        after=[halves[1], *(ahead[2:5:2] if folded else ())],
    )
    pieces = exchange_split(sent)
    block_out, written = call(
        functools.partial(join_ahead, groups),
        [((1, local, model), BF16), ((8, LANES), F32)],
        *ahead,
        stored=1,
        scratch=[pltpu.SemaphoreType.DMA((2 * groups,))],
    )
    shapes = [((TAPS + rows, channels), BF16)] * groups
    other = swap(halves[1], "frame", masks[-1])
    sums = list(call(add_halves, shapes, halves[0], other, after=[written]))
    first = swap(sums[0], "frame", 1)
    sums[-1] = stack(sums[-1], after=[first, pieces[2]])
    sums = exchange(sums)
    shapes = [((rows, model), F32), ((KERNEL, model), F32)]
    sums = call(functools.partial(scale_sums, groups, scale), shapes, *sums)
    joined = call(
        functools.partial(join_all, groups, len(pieces)),
        [((1, local, inner), BF16)] * 3 + [((rows, model), F32), ((KERNEL, model), F32)],
        *pieces,
        *sums,
        stored=5,
        scratch=[pltpu.SemaphoreType.DMA((8 * groups + 2,))],
    )
    return (block_out, *joined)


def solution(mesh):
    return jax.shard_map(
        shards,
        mesh=mesh,
        in_specs=(
            P("frame", "fsdp", None),
            P("frame", "fsdp", None),
            P("frame", "fsdp", None),
            P(("fsdp", "frame"), None),
            P(),
            P("frame", "fsdp", None),
        ),
        out_specs=(
            P("frame", "fsdp", None),
            P("frame", "fsdp", None),
            P("frame", "fsdp", None),
            P("frame", "fsdp", None),
            P(("fsdp", "frame"), None),
            P(),
        ),
        check_vma=False,
    )
```
